128 devices in a mesh: dp: 4 (over y), seq: 32 (over x, z, core).
Axes of the slice: x: 4, y: 4, z: 4, core: 2. Of those that a mesh axis runs over, the one named last changes fastest.
Arguments:
- tokens: bfloat16 [4, 16384, 1024], P('dp', 'seq'), may hold values from -18 to 18
- lengths: int32 [4, 128], P('dp'), may hold values from 1 to 128
- w_query: bfloat16 [1024, 512], replicated, may hold values from -0.1875 to 0.1875
- w_key: bfloat16 [1024, 512], replicated, may hold values from -0.1875 to 0.1875
- w_value: bfloat16 [1024, 512], replicated, may hold values from -0.1875 to 0.1875
- w_out: bfloat16 [512, 1024], replicated, may hold values from -2 to 2
- cotangent: bfloat16 [4, 16384, 1024], P('dp', 'seq'), may hold values from -6 to 6
Outputs:
- mixed: bfloat16 [4, 16384, 1024], P('dp', 'seq')
- grad_tokens: bfloat16 [4, 16384, 1024], P('dp', 'seq')
- grad_query: float32 [1024, 512], replicated
- grad_key: float32 [1024, 512], replicated
- grad_value: float32 [1024, 512], replicated
- grad_output: float32 [512, 1024], replicated
The draws below stay inside these ranges and needn't reach their ends.
All inputs are finite; a program needn't handle non-finite values.
Results may differ from the reference program's by a relative error of at most 0.014.
The reference program's roundings to bfloat16 on the way count: a program that leaves them out, or rounds other values in their place, can miss the bound.
Values may be sent and summed in bfloat16 or wider, within the bound.
A program may use at most 192 MiB of HBM per device.

```python
import math
import jax
import jax.numpy as jnp
from jax import lax

D = 1024
HEADS = 4
TILE = 128
NBARS = 128
LENGTH = 16384
SEQS = 4
HD = 512


def draw_tokens(key, part):
    base_draw = jax.random.normal(jax.random.fold_in(key, 11), (SEQS, LENGTH, D), jnp.float32)
    base_draw = jnp.clip(base_draw, -4.0, 4.0)
    return base_draw.astype(jnp.bfloat16)


def with_ends(array, stream_key, least, largest):
    longest = array.shape.index(max(array.shape))
    spots = []
    for shift in (0, 1):
        where = [jax.random.randint(jax.random.fold_in(stream_key, axis), (), 0, length) for axis, length in enumerate(array.shape)]
        where[longest] = (where[longest] + shift) % array.shape[longest]
        spots.append(tuple(where))
    return array.at[spots[0]].set(least).at[spots[1]].set(largest)


def block_levels(key, dims, split, least, largest):
    def one(dim, parts):
        steps = jax.random.uniform(jax.random.fold_in(jax.random.fold_in(key, 6), dim), (parts,), jnp.float32, least / len(split), largest / len(split))
        return jnp.repeat(jnp.exp(steps), dims[dim] // parts).reshape((-1,) + (1,) * (len(dims) - dim - 1))

    factor_of = one(*split[0])
    for cut in split[1:]:
        factor_of = factor_of * one(*cut)
    return factor_of


def bell_draw(stream_key, extent, scale, bound, split=(), kind=jnp.bfloat16):
    values = jax.random.normal(stream_key, extent, jnp.float32) * scale
    if len(split) > 0:
        values = block_levels(stream_key, extent, split, -0.22, 0.18) * values
    return jnp.clip(values, min=-bound, max=bound).astype(kind)


def setup_inputs(seed: int = 0) -> dict:
    keys = jax.random.split(jax.random.key(seed), 8)
    tokens = draw_tokens(jax.random.fold_in(keys[7], 71), 0)
    lengths = with_ends(jax.random.randint(keys[1], (SEQS, NBARS), 1, TILE + 1), jax.random.fold_in(keys[1], 1), 1, TILE).astype(jnp.int32)
    w_query = bell_draw(keys[2], (D, HD), D ** -0.5, 0.1875)
    w_key = bell_draw(keys[3], (D, HD), D ** -0.5, 0.1875)
    w_value = bell_draw(keys[4], (D, HD), D ** -0.5, 0.1875)
    w_out = bell_draw(keys[5], (HD, D), (max(HD // 64, 1)) ** -0.5, 2.0)
    cotangent = bell_draw(keys[6], (SEQS, LENGTH, D), 1.0, 6.0, ((0, 4), (1, 32)))
    return {"tokens": tokens, "lengths": lengths, "w_query": w_query, "w_key": w_key, "w_value": w_value, "w_out": w_out, "cotangent": cotangent}


bar_offsets = (0, 1, 2, 4, 8, 12, 16, 24, 32)
group_bars = 4
far_score = -1e+30

def product(form, left, right):
    return jnp.einsum(form, left.astype(jnp.float32), right.astype(jnp.float32))

def summarize(bar_rows, length):
    slot_ids = jnp.arange(bar_rows.shape[1], dtype=jnp.int32)
    live_slots = slot_ids[None, :] < length[:, None]
    running = lax.optimization_barrier(jnp.sum(jnp.where(live_slots[:, :, None], bar_rows.astype(jnp.float32), 0.0), axis=1))
    return (running / length[:, None].astype(jnp.float32)).astype(jnp.bfloat16)

def bar_block(queries, ext_key, ext_value, ext_length, base_bar, bar_ids, query_length, summary_key, summary_value, grad_context):
    group_count, tile_len, head_count, head_dim = queries.shape
    sources = len(bar_offsets)
    key_parts = []
    value_parts = []
    length_parts = []
    for offset in bar_offsets:
        first_bar = base_bar - offset
        key_parts.append(lax.dynamic_slice_in_dim(ext_key, first_bar, group_count, 0))
        value_parts.append(lax.dynamic_slice_in_dim(ext_value, first_bar, group_count, 0))
        length_parts.append(lax.dynamic_slice_in_dim(ext_length, first_bar, group_count, 0))
    fine_key = jnp.stack(key_parts, 1).reshape(group_count, sources * tile_len, head_count, head_dim)
    fine_value = jnp.stack(value_parts, 1).reshape(group_count, sources * tile_len, head_count, head_dim)
    fine_length = jnp.stack(length_parts, 1)
    slot_ids = jnp.arange(tile_len, dtype=jnp.int32)
    key_live = slot_ids[None, None, :] < fine_length[:, :, None]
    causal = slot_ids[None, :] <= slot_ids[:, None]
    other_bar = jnp.arange(sources, dtype=jnp.int32) != 0
    fine_live = key_live[:, None, :, :] & (causal[None, :, None, :] | other_bar[None, None, :, None])
    fine_live = fine_live.reshape(group_count, 1, tile_len, sources * tile_len)
    distance = bar_ids[:, None] - jnp.arange(summary_key.shape[0], dtype=jnp.int32)[None, :]
    coarse_live = distance >= 1
    for offset in bar_offsets[1:]:
        coarse_live = coarse_live & (distance != offset)
    coarse_live = coarse_live[:, None, None, :]
    score_scale = 1.0 / math.sqrt(head_dim)
    fine_score = product('gqhe,gkhe->ghqk', queries, fine_key) * score_scale
    coarse_score = product('gqhe,nhe->ghqn', queries, summary_key) * score_scale
    fine_score = jnp.where(fine_live, fine_score, far_score)
    coarse_score = jnp.where(coarse_live, coarse_score, far_score)
    top_score = jnp.maximum(lax.optimization_barrier(jnp.max(fine_score, axis=-1)), lax.optimization_barrier(jnp.max(coarse_score, axis=-1)))[..., None]
    fine_exp = jnp.where(fine_live, jnp.exp(fine_score - top_score), 0.0)
    coarse_exp = jnp.where(coarse_live, jnp.exp(coarse_score - top_score), 0.0)
    denominator = (lax.optimization_barrier(jnp.sum(fine_exp, axis=-1)) + lax.optimization_barrier(jnp.sum(coarse_exp, axis=-1)))[..., None]
    fine_prob = fine_exp / denominator
    coarse_prob = coarse_exp / denominator
    fine_round = fine_prob.astype(jnp.bfloat16)
    coarse_round = coarse_prob.astype(jnp.bfloat16)
    attended_context = product('ghqk,gkhe->gqhe', fine_round, fine_value) + product('ghqn,nhe->gqhe', coarse_round, summary_value)
    query_live = slot_ids[None, :] < query_length[:, None]
    attended_context = jnp.where(query_live[:, :, None, None], attended_context, 0.0)
    fine_dp = product('gqhe,gkhe->ghqk', grad_context, fine_value)
    coarse_dp = product('gqhe,nhe->ghqn', grad_context, summary_value)
    delta = (lax.optimization_barrier(jnp.sum(fine_prob * fine_dp, axis=-1)) + lax.optimization_barrier(jnp.sum(coarse_prob * coarse_dp, axis=-1)))[..., None]
    fine_ds = (fine_prob * (fine_dp - delta) * score_scale).astype(jnp.bfloat16)
    coarse_ds = (coarse_prob * (coarse_dp - delta) * score_scale).astype(jnp.bfloat16)
    query_gradient_rows = product('ghqk,gkhe->gqhe', fine_ds, fine_key) + product('ghqn,nhe->gqhe', coarse_ds, summary_key)
    fine_gk = product('ghqk,gqhe->gkhe', fine_ds, queries).reshape(group_count, sources, tile_len, head_count, head_dim)
    fine_gv = product('ghqk,gqhe->gkhe', fine_round, grad_context).reshape(group_count, sources, tile_len, head_count, head_dim)
    coarse_key_gradient = product('ghqn,gqhe->nhe', coarse_ds, queries)
    coarse_value_gradient = product('ghqn,gqhe->nhe', coarse_round, grad_context)
    return (attended_context, query_gradient_rows, fine_gk, fine_gv, coarse_key_gradient, coarse_value_gradient)

def spread(running, grads, base_bar):
    group_count = grads.shape[0]
    for position, offset in enumerate(bar_offsets):
        first_bar = base_bar - offset
        current = lax.dynamic_slice_in_dim(running, first_bar, group_count, 0)
        running = lax.dynamic_update_slice_in_dim(running, current + grads[:, position], first_bar, 0)
    return running

def reference(tokens, lengths, w_query, w_key, w_value, w_out, cotangent):
    inner_width = w_query.shape[1]
    head_dim = inner_width // HEADS
    pad_bars = bar_offsets[-1]
    bar_grand_total = lengths.shape[1]
    grad_q_sum = jnp.zeros(w_query.shape, jnp.float32)
    grad_k_sum = jnp.zeros(w_query.shape, jnp.float32)
    grad_v_sum = jnp.zeros(w_query.shape, jnp.float32)
    grad_o_sum = jnp.zeros(w_out.shape, jnp.float32)
    mixed_rows = []
    grad_rows = []
    for seq_row in range(tokens.shape[0]):
        inputs = tokens[seq_row]
        grad_out = cotangent[seq_row]
        length = lengths[seq_row]
        queries = jnp.dot(inputs, w_query, preferred_element_type=jnp.float32).astype(jnp.bfloat16)
        keys_all = jnp.dot(inputs, w_key, preferred_element_type=jnp.float32).astype(jnp.bfloat16)
        values_all = jnp.dot(inputs, w_value, preferred_element_type=jnp.float32).astype(jnp.bfloat16)
        key_bars = keys_all.reshape(bar_grand_total, TILE, inner_width)
        value_bars = values_all.reshape(bar_grand_total, TILE, inner_width)
        summary_key = summarize(key_bars, length).reshape(bar_grand_total, HEADS, head_dim)
        summary_value = summarize(value_bars, length).reshape(bar_grand_total, HEADS, head_dim)
        slot_ids = jnp.arange(TILE, dtype=jnp.int32)
        live_slots = slot_ids[None, :] < length[:, None]
        token_live = live_slots.reshape(-1)
        grad_context = product('td,ed->te', grad_out, w_out)
        grad_context = jnp.where(token_live[:, None], grad_context, 0.0).astype(jnp.bfloat16)
        zero_bars = jnp.zeros((pad_bars, TILE, HEADS, head_dim), jnp.bfloat16)
        ext_key = jnp.concatenate([zero_bars, keys_all.reshape(bar_grand_total, TILE, HEADS, head_dim)], 0)
        ext_value = jnp.concatenate([zero_bars, values_all.reshape(bar_grand_total, TILE, HEADS, head_dim)], 0)
        ext_length = jnp.concatenate([jnp.zeros((pad_bars,), jnp.int32), length], 0)
        query_bars = queries.reshape(bar_grand_total, TILE, HEADS, head_dim)
        grad_bars = grad_context.reshape(bar_grand_total, TILE, HEADS, head_dim)

        def step(carried_state, block_index):
            accumulated_key, accumulated_value, accumulated_summary_key, accumulated_summary_value = carried_state
            begin_bar = (block_index * group_bars).astype(jnp.int32)
            query_block = lax.dynamic_slice_in_dim(query_bars, begin_bar, group_bars, 0)
            grad_block = lax.dynamic_slice_in_dim(grad_bars, begin_bar, group_bars, 0)
            length_block = lax.dynamic_slice_in_dim(length, begin_bar, group_bars, 0)
            base_bar = (pad_bars + begin_bar).astype(jnp.int32)
            bar_ids = begin_bar + jnp.arange(group_bars, dtype=jnp.int32)
            result = bar_block(query_block, ext_key, ext_value, ext_length, base_bar, bar_ids, length_block, summary_key, summary_value, grad_block)
            attended_context, query_gradient_rows, fine_gk, fine_gv, coarse_key_gradient, coarse_value_gradient = result
            accumulated_key = spread(accumulated_key, fine_gk, base_bar)
            accumulated_value = spread(accumulated_value, fine_gv, base_bar)
            return ((accumulated_key, accumulated_value, accumulated_summary_key + coarse_key_gradient, accumulated_summary_value + coarse_value_gradient), (attended_context.astype(jnp.bfloat16), query_gradient_rows.astype(jnp.bfloat16)))
        ext_zero = jnp.zeros((pad_bars + bar_grand_total, TILE, HEADS, head_dim), jnp.float32)
        sum_zero = jnp.zeros((bar_grand_total, HEADS, head_dim), jnp.float32)
        carried_state, stacked = lax.scan(step, (ext_zero, ext_zero, sum_zero, sum_zero), jnp.arange(bar_grand_total // group_bars, dtype=jnp.int32))
        accumulated_key, accumulated_value, accumulated_summary_key, accumulated_summary_value = carried_state
        attended_context = stacked[0].reshape(-1, inner_width)
        query_gradient_rows = stacked[1].reshape(-1, inner_width)
        inverse_denominator = 1.0 / length.astype(jnp.float32)
        shared_key_rows = accumulated_summary_key.reshape(bar_grand_total, inner_width) * inverse_denominator[:, None]
        share_value = accumulated_summary_value.reshape(bar_grand_total, inner_width) * inverse_denominator[:, None]
        own_key = accumulated_key[pad_bars:].reshape(bar_grand_total, TILE, inner_width) + jnp.where(live_slots[:, :, None], shared_key_rows[:, None, :], 0.0)
        own_value = accumulated_value[pad_bars:].reshape(bar_grand_total, TILE, inner_width) + jnp.where(live_slots[:, :, None], share_value[:, None, :], 0.0)
        grad_keys = own_key.reshape(-1, inner_width).astype(jnp.bfloat16)
        grad_values = own_value.reshape(-1, inner_width).astype(jnp.bfloat16)
        mixed_rows.append(jnp.dot(attended_context, w_out, preferred_element_type=jnp.float32).astype(jnp.bfloat16))
        grad_in = product('te,de->td', query_gradient_rows, w_query) + product('te,de->td', grad_keys, w_key) + product('te,de->td', grad_values, w_value)
        grad_rows.append(grad_in.astype(jnp.bfloat16))
        grad_q_sum = grad_q_sum + product('td,te->de', inputs, query_gradient_rows)
        grad_k_sum = grad_k_sum + product('td,te->de', inputs, grad_keys)
        grad_v_sum = grad_v_sum + product('td,te->de', inputs, grad_values)
        grad_o_sum = grad_o_sum + product('te,td->ed', attended_context, grad_out)
    return (jnp.stack(mixed_rows, 0), jnp.stack(grad_rows, 0), grad_q_sum, grad_k_sum, grad_v_sum, grad_o_sum)
```

```python
import functools
import math

import jax
import jax.numpy as jnp
from jax import lax
from jax.experimental import pallas as pl
from jax.experimental.pallas import tpu as pltpu
from jax.sharding import PartitionSpec as P

MESH = pl.DeviceIdType.MESH
BF = jnp.bfloat16
F32 = jnp.float32
HEADS = 4
TILE = 128
OFFSETS = (0, 1, 2, 4, 8, 12, 16, 24, 32)
SCALE = 1.0 / math.sqrt(128.0)
LOG2E = 1.4426950408889634
NEG = -1e30
NT = (((1,), (1,)), ((), ()))
TN = (((0,), (0,)), ((), ()))
OWN = 32 * TILE
MIB = 1024 * 1024


def place():
    s = lax.axis_index("seq")
    return lax.axis_index("dp"), lax.div(s, 8), lax.rem(lax.div(s, 2), 4), lax.rem(s, 2)


def device(y, x, z, c):
    return (y, (x * 4 + z) * 2 + c)


def turn(a, d):
    return lax.rem(a + d, 4)


def remote(src, dst, send, recv, to):
    return pltpu.make_async_remote_copy(
        src_ref=src, dst_ref=dst, send_sem=send, recv_sem=recv, device_id=to, device_id_type=MESH
    )


def greet(partners):
    barrier = pltpu.get_barrier_semaphore()
    for to in partners:
        pl.semaphore_signal(barrier, inc=1, device_id=to, device_id_type=MESH)
    pl.semaphore_wait(barrier, len(partners))


def plane_partners(y, x, z, c):
    found = [device(y, x, z, 1 - c)]
    for d in (1, 2, 3):
        for core in (0, 1):
            found.append(device(y, turn(x, d), z, core))
            found.append(device(y, x, turn(z, d), core))
    return found


def rows_of(start, count):
    return pl.ds(pl.multiple_of(start, TILE), count)


def spread_kernel(
    lens, tok, cot, wq, wk, wv, wo, kv, qg, summ,
    kvs, qgs, sums, s_kv, r_kv, s_qg, r_qg, s_h, r_h, s_x, r_x, s_s, r_s,
):
    y, x, z, c = place()
    greet(plane_partners(y, x, z, c))
    other = device(y, x, z, 1 - c)
    home = lax.div(z, 2)
    slot = lax.rem(z, 2) * 2 + c
    at_home = c == home

    def project(src, w, dst, lane, mask):
        def half(i, carry):
            rows = rows_of(i * 256, 256)
            got = jnp.dot(src[rows, :], w[...], preferred_element_type=F32)
            for h in range(HEADS):
                dst[h, rows, lane : lane + TILE] = got[:, h * TILE : (h + 1) * TILE].astype(BF)
            return carry

        lax.fori_loop(0, 2, half, 0)

    def exchange(staged, landing, base, send, recv):
        spot = rows_of(base + slot * 512, 512)
        copies = []
        for d in (1, 2, 3):
            h = turn(z, d)
            copy = remote(staged.at[h], landing.at[spot], send.at[d], recv.at[slot], device(y, x, h, home))
            copy.start()
            copies.append(copy)
        near = remote(staged.at[z], landing.at[spot], send.at[0], recv.at[slot], other)

        @pl.when(at_home)
        def _():
            landing[spot, :] = staged[z]

        @pl.when(jnp.logical_not(at_home))
        def _():
            near.start()

        return copies, near

    def settle(copies, near):
        for copy in copies:
            copy.wait_send()

        @pl.when(jnp.logical_not(at_home))
        def _():
            near.wait_send()

    def arrived(staged, landing, base, send, recv, i):
        mine = jnp.logical_and(z == 2 * c + i // 2, c == i % 2)

        @pl.when(jnp.logical_not(mine))
        def _():
            remote(
                staged.at[0], landing.at[pl.ds(base + i * 512, 512)], send.at[0], recv.at[i], other
            ).wait_recv()

    project(tok, wk, kvs, 0, False)
    project(tok, wv, kvs, TILE, False)
    kv_sent = exchange(kvs, kv, OWN, s_kv, r_kv)
    project(tok, wq, qgs, 0, False)
    first_own = ((x * 4 + z) * 2 + c) * 4

    def grads(i, carry):
        rows = rows_of(i * TILE, TILE)
        got = lax.dot_general(cot[rows, :], wo[...], NT, preferred_element_type=F32)
        live = lax.broadcasted_iota(jnp.int32, (TILE, 512), 0) < lens[0, first_own + i]
        got = jnp.where(live, got, 0.0).astype(BF)
        for h in range(HEADS):
            qgs[h, rows, TILE : 2 * TILE] = got[:, h * TILE : (h + 1) * TILE]
        return carry

    lax.fori_loop(0, 4, grads, 0)
    qg_sent = exchange(qgs, qg, 0, s_qg, r_qg)

    group = 2 * x + c
    ahead = device(y, turn(x, 1), z, c)
    halos, across = [], []
    for i in range(4):
        arrived(kvs, kv, OWN, s_kv, r_kv, i)
        own = kv.at[pl.ds(OWN + i * 512, 512)]
        halo = remote(own, kv.at[pl.ds(i * 512, 512)], s_h.at[i], r_h.at[i], ahead)
        halo.start()
        halos.append(halo)
        give = remote(own, kv.at[pl.ds(2048 + i * 512, 512)], s_x.at[i], r_x.at[i], other)

        @pl.when(c == 0)
        def _():
            give.start()

    def summary(i, carry):
        rows = rows_of(OWN + i * TILE, TILE)
        length = lens[0, group * 16 + i]
        live = lax.broadcasted_iota(jnp.int32, (TILE, 256), 0) < length
        total = jnp.sum(jnp.where(live, kv[rows, :].astype(F32), 0.0), axis=0, keepdims=True)
        sums[pl.ds(i, 1), :] = total / jnp.full((1, 256), length, jnp.int32).astype(F32)
        return carry

    lax.fori_loop(0, 16, summary, 0)
    summ[group] = sums[...].astype(BF)
    sum_copies = []
    for d, cc in [(d, cc) for d in range(4) for cc in (0, 1) if (d, cc) != (0, 0)]:
        n = d * 2 + cc
        core = lax.rem(c + cc, 2)
        copy = remote(summ.at[group], summ.at[group], s_s.at[n], r_s.at[n], device(y, turn(x, d), z, core))
        copy.start()
        sum_copies.append(copy)

    for i in range(4):
        halos[i].wait_recv()
        pass_on = remote(
            kv.at[pl.ds(i * 512, 512)], kv.at[pl.ds(2048 + i * 512, 512)], s_x.at[i], r_x.at[i], other
        )

        @pl.when(c == 1)
        def _():
            pass_on.start()

        across.append(pass_on)
    for copy in across:
        copy.wait()
    for copy in halos:
        copy.wait_send()
    for i in range(4):
        arrived(qgs, qg, 0, s_qg, r_qg, i)
    for copy in sum_copies:
        copy.wait()
    settle(*kv_sent)
    settle(*qg_sent)


def attend_kernel(lens, kv, qg, summ, cg, gkv, gsum, kvt, gt, pair, sc, dsp):
    y, x, z, c = place()
    group = 2 * x + c
    pair[...] = jnp.zeros_like(pair)
    gsum[...] = jnp.zeros_like(gsum)

    def prepare(b, carry):
        rows = rows_of(b * TILE, TILE)
        kvt[:, rows] = jnp.transpose(kv[rows, :])
        gkv[rows, :] = jnp.zeros((TILE, 256), F32)
        return carry

    lax.fori_loop(0, 48, prepare, 0)
    kvt[:, 48 * TILE : 49 * TILE] = jnp.transpose(summ[...])
    key_slot = lax.broadcasted_iota(jnp.int32, (TILE, TILE), 0)
    query_slot = lax.broadcasted_iota(jnp.int32, (TILE, TILE), 1)
    count = len(OFFSETS)

    def bar(qb, carry):
        rows = rows_of(qb * TILE, TILE)
        pair[0:TILE, 0:TILE] = qg[rows, 0:TILE]
        pair[TILE:, TILE:] = qg[rows, TILE:]
        both = pair[...]
        this = 16 * group + qb
        top = None
        for j in range(count + 1):
            here = slice(j * TILE, (j + 1) * TILE)
            if j < count:
                spot = rows_of((32 + qb - OFFSETS[j]) * TILE, TILE)
                bar_id = this - OFFSETS[j]
                length = jnp.where(bar_id >= 0, lens[0, jnp.maximum(bar_id, 0)], 0)
                source = kv[spot, :]
                gt[:, here] = kvt[:, spot]
                ok = key_slot < length
                if j == 0:
                    ok = jnp.logical_and(ok, key_slot <= query_slot)
            else:
                source = summ[...]
                gt[:, here] = kvt[:, 48 * TILE : 49 * TILE]
                distance = this - key_slot
                ok = distance >= 1
                for o in OFFSETS[1:]:
                    ok = jnp.logical_and(ok, distance != o)
            got = lax.dot_general(source, both, NT, preferred_element_type=F32)
            score = jnp.where(ok, got[:, :TILE] * (SCALE * LOG2E), NEG)
            sc[here, :TILE] = score
            sc[here, TILE:] = got[:, TILE:]
            high = jnp.max(score, axis=0, keepdims=True)
            top = high if top is None else jnp.maximum(top, high)
        total = jnp.zeros((1, TILE), F32)
        weighted = jnp.zeros((1, TILE), F32)
        for j in range(count + 1):
            here = slice(j * TILE, (j + 1) * TILE)
            e = jnp.exp2(sc[here, :TILE] - top)
            sc[here, :TILE] = e
            total = total + jnp.sum(e, axis=0, keepdims=True)
            weighted = weighted + jnp.sum(e * sc[here, TILE:], axis=0, keepdims=True)
        inverse = 1.0 / total
        delta = weighted * inverse
        for j in range(count + 1):
            here = slice(j * TILE, (j + 1) * TILE)
            p = sc[here, :TILE] * inverse
            dsp[here, :TILE] = (p * (sc[here, TILE:] - delta)).astype(BF)
            dsp[here, TILE:] = p.astype(BF)
            got = jnp.dot(dsp[here, :], both, preferred_element_type=F32)
            if j < count:
                spot = rows_of((32 + qb - OFFSETS[j]) * TILE, TILE)
                gkv[spot, :] += got
            else:
                gsum[...] += got
        out = jnp.dot(gt[...], dsp[...], preferred_element_type=F32)
        cg[rows, 0:TILE] = jnp.transpose(out[:TILE, :TILE] * SCALE).astype(BF)
        context = jnp.transpose(out[TILE:, TILE:])
        cg[rows, TILE:] = jnp.where(key_slot < lens[0, this], context, 0.0).astype(BF)
        return carry

    lax.fori_loop(0, 16, bar, 0)


def back_kernel(
    lens, gkv, gsum, cg, tok, cot, wq, wk, wv, wo, mixed, gin, wg,
    sx, rx, sh, rh, gss, gsr, own, ret_kv, ret_cg, flat,
    s_kv, r_kv, s_cg, r_cg, s_h, r_h, s_x, r_x, s_s, r_s,
):
    y, x, z, c = place()
    greet(plane_partners(y, x, z, c))
    other = device(y, x, z, 1 - c)
    home = lax.div(z, 2)
    at_home = c == home
    group = 2 * x + c

    def owner(i):
        to_z = 2 * c + i // 2
        mine = jnp.logical_and(z == to_z, c == i % 2)
        return device(y, x, to_z, i % 2), mine

    def give_back(src, landing, send, recv, i):
        to, mine = owner(i)
        rows = pl.ds(i * 512, 512)

        @pl.when(mine)
        def _():
            landing[z] = src[rows, :]

        @pl.when(jnp.logical_not(mine))
        def _():
            remote(src.at[rows], landing.at[z], send.at[i], recv.at[z], to).start()

    def settle(src, landing, send, recv):
        for i in range(4):
            to, mine = owner(i)

            @pl.when(jnp.logical_not(mine))
            def _():
                remote(src.at[pl.ds(i * 512, 512)], landing.at[z], send.at[i], recv.at[z], to).wait_send()

    def returned(src, landing, send, recv):
        for h in range(HEADS):
            mine = jnp.logical_and(z == h, at_home)

            @pl.when(jnp.logical_not(mine))
            def _():
                remote(src.at[pl.ds(0, 512)], landing.at[h], send.at[0], recv.at[h], other).wait_recv()

    crossing = []
    for i in range(4):
        rows = pl.ds(i * 512, 512)
        sx[rows, :] = gkv[pl.ds(2048 + i * 512, 512), :].astype(BF)
        copy = remote(sx.at[rows], rx.at[rows], s_x.at[i], r_x.at[i], other)
        copy.start()
        crossing.append(copy)
    for i in range(4):
        give_back(cg, ret_cg, s_cg, r_cg, i)
    gss[...] = gsum[...].astype(BF).reshape(8, 16, 256)
    gsr[group] = gss[group]
    sum_copies = []
    for d, cc in [(d, cc) for d in range(4) for cc in (0, 1) if (d, cc) != (0, 0)]:
        n = d * 2 + cc
        to_x, core = turn(x, d), lax.rem(c + cc, 2)
        copy = remote(
            gss.at[to_x * 2 + core], gsr.at[group], s_s.at[n], r_s.at[n], device(y, to_x, z, core)
        )
        copy.start()
        sum_copies.append(copy)
    behind = device(y, turn(x, 3), z, c)
    halos = []
    for i in range(4):
        rows = pl.ds(i * 512, 512)
        crossing[i].wait_recv()

        @pl.when(c == 0)
        def _():
            sh[rows, :] = gkv[rows, :].astype(BF)

        @pl.when(c == 1)
        def _():
            sh[rows, :] = (gkv[rows, :] + rx[rows, :].astype(F32)).astype(BF)

        copy = remote(sh.at[rows], rh.at[rows], s_h.at[i], r_h.at[i], behind)
        copy.start()
        halos.append(copy)

    def flatten(src, lane, n):
        for h in range(HEADS):
            flat[n, :, h * TILE : (h + 1) * TILE] = src[h, :, lane : lane + TILE]

    def weight_grad(n, m):
        def part(i, carry):
            cols = rows_of(i * 256, 256)
            got = lax.dot_general(tok[:, cols], flat[n], TN, preferred_element_type=F32).astype(BF)
            wg[m, 0, cols, :] = got[:, :256]
            wg[m, 1, cols, :] = got[:, 256:]
            return carry

        lax.fori_loop(0, 4, part, 0)

    returned(cg, ret_cg, s_cg, r_cg)
    flatten(ret_cg, 0, 0)
    flatten(ret_cg, TILE, 1)

    def mix(i, carry):
        rows = rows_of(i * 256, 256)
        mixed[rows, :] = jnp.dot(flat[1, rows, :], wo[...], preferred_element_type=F32).astype(BF)
        return carry

    lax.fori_loop(0, 2, mix, 0)
    weight_grad(0, 0)

    def out_grad(i, carry):
        cols = rows_of(i * 256, 256)
        got = lax.dot_general(flat[1], cot[:, cols], TN, preferred_element_type=F32).astype(BF)
        wg[3, lax.div(i, 2), rows_of(lax.rem(i, 2) * 512, 512), :] = got
        return carry

    lax.fori_loop(0, 4, out_grad, 0)

    for copy in sum_copies:
        copy.wait()
    coarse = gsr[0].astype(F32)
    for n in range(1, 8):
        coarse = coarse + gsr[n].astype(F32)
    lane = lax.broadcasted_iota(jnp.int32, (1, 256), 1)
    factor = jnp.where(lane < TILE, SCALE, 1.0)
    for i in range(4):
        halos[i].wait_recv()
        for b in range(4 * i, 4 * i + 4):
            rows = pl.ds(b * TILE, TILE)
            length = lens[0, group * 16 + b]
            live = lax.broadcasted_iota(jnp.int32, (TILE, 256), 0) < length
            share = coarse[b : b + 1, :] * (1.0 / jnp.full((1, 256), length, jnp.int32).astype(F32))
            extra = jnp.where(c == 0, rx[rows, :].astype(F32), 0.0)
            total = gkv[pl.ds(OWN + b * TILE, TILE), :] + rh[rows, :].astype(F32) + extra
            own[rows, :] = ((total + jnp.where(live, share, 0.0)) * factor).astype(BF)
        give_back(own, ret_kv, s_kv, r_kv, i)
    returned(own, ret_kv, s_kv, r_kv)
    flatten(ret_kv, 0, 1)
    flatten(ret_kv, TILE, 2)
    weight_grad(1, 1)
    weight_grad(2, 2)

    def back(i, carry):
        rows = rows_of(i * 256, 256)
        total = lax.dot_general(flat[0, rows, :], wq[...], NT, preferred_element_type=F32)
        total = total + lax.dot_general(flat[1, rows, :], wk[...], NT, preferred_element_type=F32)
        total = total + lax.dot_general(flat[2, rows, :], wv[...], NT, preferred_element_type=F32)
        gin[rows, :] = total.astype(BF)
        return carry

    lax.fori_loop(0, 2, back, 0)
    settle(cg, ret_cg, s_cg, r_cg)
    settle(own, ret_kv, s_kv, r_kv)
    for copy in crossing + halos:
        copy.wait_send()


ORDERS = ("yxz", "xzy", "zyx", "yzx")


def reduce_kernel(wg, out, got0, w0, got1, w1, got2, w2, got3, s0, r0, s1, r1, s2, r2):
    y, x, z, c = place()
    where = {"y": y, "x": x, "z": z}

    def along(axis, d):
        at = dict(where)
        at[axis] = turn(where[axis], d)
        return device(at["y"], at["x"], at["z"], c)

    other = device(y, x, z, 1 - c)
    greet([other] + [along(axis, d) for axis in "yxz" for d in (1, 2, 3)])

    started = []
    first = []
    for m in range(4):
        copy = remote(wg.at[m, 1 - c], got0.at[m], s0.at[0, m], r0.at[0, m], other)
        copy.start()
        first.append(copy)
    sources = [None] * 4
    levels = ((w0, got1, 256), (w1, got2, 64), (w2, got3, 16))
    pending = [None] * 4

    def send_level(m, level):
        src, got, size = levels[level]
        copies = []
        axis = ORDERS[m][level]
        for d in (1, 2, 3):
            piece = pl.ds(pl.multiple_of(turn(where[axis], d) * size, 16), size)
            copy = remote(
                src.at[m, piece], got.at[m, d - 1], s1.at[level, m, d - 1], r1.at[level, m, d - 1], along(axis, d)
            )
            copy.start()
            copies.append(copy)
        return copies

    def place_rows(m, level):
        a, b, d = (where[axis] for axis in ORDERS[m])
        start = a * 256
        if level >= 1:
            start = start + b * 64
        if level >= 2:
            start = start + d * 16
        return pl.ds(pl.multiple_of(start, 16), levels[level][2])

    for m in range(4):
        first[m].wait_recv()

        def add(i, carry, m=m):
            rows = rows_of(i * 256, 256)
            w0[m, rows, :] = (wg[m, c, rows, :].astype(F32) + got0[m, rows, :].astype(F32)).astype(BF)
            return carry

        lax.fori_loop(0, 4, add, 0)
        pending[m] = send_level(m, 0)
        started += pending[m]
    for level in range(3):
        src, got, size = levels[level]
        for m in range(4):
            for copy in pending[m]:
                copy.wait_recv()
            mine = pl.ds(pl.multiple_of(where[ORDERS[m][level]] * size, 16), size)
            total = src[m, mine, :].astype(F32)
            for n in range(3):
                total = total + got[m, n].astype(F32)
            if level < 2:
                levels[level + 1][0][m] = total.astype(BF)
                pending[m] = send_level(m, level + 1)
                started += pending[m]
            else:
                out[m, c, place_rows(m, 2), :] = total.astype(BF)

    def give(m, level):
        block = out.at[m, c, place_rows(m, level)]
        copies = []
        for d in (1, 2, 3):
            copy = remote(
                block, block, s2.at[level, m, d - 1], r2.at[level, m, d - 1], along(ORDERS[m][level], d)
            )
            copy.start()
            copies.append(copy)
        return copies

    for m in range(4):
        pending[m] = give(m, 2)
        started += pending[m]
    last = []
    for level in (1, 0, None):
        for m in range(4):
            for copy in pending[m]:
                copy.wait_recv()
            if level is None:
                copy = remote(out.at[m, c], out.at[m, c], s0.at[1, m], r0.at[1, m], other)
                copy.start()
                last.append(copy)
            else:
                pending[m] = give(m, level)
                started += pending[m]
    for copy in last:
        copy.wait()
    for copy in first + started:
        copy.wait_send()


VM = pl.BlockSpec(memory_space=pltpu.VMEM)
SM = pl.BlockSpec(memory_space=pltpu.SMEM)
DMA = pltpu.SemaphoreType.DMA


def params(identity, mib):
    if identity is None:
        return pltpu.CompilerParams(vmem_limit_bytes=mib * MIB)
    return pltpu.CompilerParams(
        collective_id=identity, has_side_effects=True, vmem_limit_bytes=mib * MIB
    )


def shape(*dims, kind=BF):
    return jax.ShapeDtypeStruct(dims, kind)


def local(tokens, lengths, w_query, w_key, w_value, w_out, cotangent):
    tok, cot = tokens[0], cotangent[0]
    kv, qg, summ = pl.pallas_call(
        spread_kernel,
        out_shape=(shape(6144, 256), shape(2048, 256), shape(8, 16, 256)),
        in_specs=[SM] + [VM] * 6,
        out_specs=(VM, VM, VM),
        scratch_shapes=[
            pltpu.VMEM((4, 512, 256), BF),
            pltpu.VMEM((4, 512, 256), BF),
            pltpu.VMEM((16, 256), F32),
        ]
        + [DMA((4,))] * 8
        + [DMA((8,))] * 2,
        compiler_params=params(0, 40),
        name="spread",
    )(lengths, tok, cot, w_query, w_key, w_value, w_out)
    cg, gkv, gsum = pl.pallas_call(
        attend_kernel,
        out_shape=(shape(2048, 256), shape(6144, 256, kind=F32), shape(128, 256, kind=F32)),
        in_specs=[SM, VM, VM, VM],
        out_specs=(VM, VM, VM),
        scratch_shapes=[
            pltpu.VMEM((256, 49 * TILE), BF),
            pltpu.VMEM((256, 10 * TILE), BF),
            pltpu.VMEM((256, 256), BF),
            pltpu.VMEM((10 * TILE, 256), F32),
            pltpu.VMEM((10 * TILE, 256), BF),
        ],
        compiler_params=params(None, 40),
        name="attend",
    )(lengths, kv, qg, summ.reshape(128, 256))
    mixed, gin, wg = pl.pallas_call(
        back_kernel,
        out_shape=(shape(512, 1024), shape(512, 1024), shape(4, 2, 1024, 256)),
        in_specs=[SM] + [VM] * 9,
        out_specs=(VM, VM, VM),
        scratch_shapes=[pltpu.VMEM((2048, 256), BF)] * 4
        + [pltpu.VMEM((8, 16, 256), BF)] * 2
        + [
            pltpu.VMEM((2048, 256), BF),
            pltpu.VMEM((4, 512, 256), BF),
            pltpu.VMEM((4, 512, 256), BF),
            pltpu.VMEM((3, 512, 512), BF),
        ]
        + [DMA((4,))] * 8
        + [DMA((8,))] * 2,
        compiler_params=params(1, 48),
        name="back",
    )(lengths, gkv, gsum, cg, tok, cot, w_query, w_key, w_value, w_out)
    total = pl.pallas_call(
        reduce_kernel,
        out_shape=shape(4, 2, 1024, 256),
        in_specs=[VM],
        out_specs=VM,
        scratch_shapes=[
            pltpu.VMEM((4, 1024, 256), BF),
            pltpu.VMEM((4, 1024, 256), BF),
            pltpu.VMEM((4, 3, 256, 256), BF),
            pltpu.VMEM((4, 256, 256), BF),
            pltpu.VMEM((4, 3, 64, 256), BF),
            pltpu.VMEM((4, 64, 256), BF),
            pltpu.VMEM((4, 3, 16, 256), BF),
            DMA((2, 4)),
            DMA((2, 4)),
            DMA((3, 4, 3)),
            DMA((3, 4, 3)),
            DMA((3, 4, 3)),
            DMA((3, 4, 3)),
        ],
        compiler_params=params(2, 40),
        name="total",
    )(wg)
    weights = [jnp.concatenate([total[m, 0], total[m, 1]], axis=1).astype(F32) for m in range(3)]
    last = total[3].reshape(4, 512, 256).transpose(1, 0, 2).reshape(512, 1024).astype(F32)
    return (mixed[None], gin[None], *weights, last)


def solution(mesh):
    placed = (P("dp", "seq", None), P("dp", None), P(), P(), P(), P(), P("dp", "seq", None))
    return jax.shard_map(
        local,
        mesh=mesh,
        in_specs=placed,
        out_specs=(P("dp", "seq", None), P("dp", "seq", None), P(), P(), P(), P()),
        check_vma=False,
    )
```

```python
import functools
import math

import jax
import jax.numpy as jnp
from jax import lax
from jax.experimental import pallas as pl
from jax.experimental.pallas import tpu as pltpu
from jax.sharding import PartitionSpec as P

MESH = pl.DeviceIdType.MESH
BF = jnp.bfloat16
F32 = jnp.float32
HEADS = 4
TILE = 128
OFFSETS = (0, 1, 2, 4, 8, 12, 16, 24, 32)
SCALE = 1.0 / math.sqrt(128.0)
LOG2E = 1.4426950408889634
NEG = -1e30
NT = (((1,), (1,)), ((), ()))
TN = (((0,), (0,)), ((), ()))
OWN = 32 * TILE
MIB = 1024 * 1024


def place():
    s = lax.axis_index("seq")
    return lax.axis_index("dp"), lax.div(s, 8), lax.rem(lax.div(s, 2), 4), lax.rem(s, 2)


def device(y, x, z, c):
    return (y, (x * 4 + z) * 2 + c)


def turn(a, d):
    return lax.rem(a + d, 4)


def remote(src, dst, send, recv, to):
    return pltpu.make_async_remote_copy(
        src_ref=src, dst_ref=dst, send_sem=send, recv_sem=recv, device_id=to, device_id_type=MESH
    )


def greet(partners):
    barrier = pltpu.get_barrier_semaphore()
    for to in partners:
        pl.semaphore_signal(barrier, inc=1, device_id=to, device_id_type=MESH)
    pl.semaphore_wait(barrier, len(partners))


def all_partners(y, x, z, c):
    found = [device(y, x, z, 1 - c)]
    for d in (1, 2, 3):
        found.append(device(turn(y, d), x, z, c))
        for core in (0, 1):
            found.append(device(y, turn(x, d), z, core))
            found.append(device(y, x, turn(z, d), core))
    return found


def rows_of(start, count):
    return pl.ds(pl.multiple_of(start, TILE), count)


def whole_kernel(
    lens, tok_in, wk_in, wv_in, wq_in, cot_in, wo_in, mixed, gin, out,
    tok, cot, wq, wk, wv, wo,
    kv, qg, summ, kvs, qgs, sums,
    kvt, gt, pair, pairt, sc, dsp, gkv, gsum, cg,
    sx, rx, sh, rh, gss, gsr, own, ret_kv, ret_cg, flat,
    wg, got0, w0, got1, w1, got2, w2, got3,
    s_in, s_kv, r_kv, s_qg, r_qg, s_h, r_h, s_x, r_x, s_s, r_s,
    s_bkv, r_bkv, s_cg, r_cg, s_bh, r_bh, s_bx, r_bx, s_gs, r_gs,
    s0, r0, s1, r1, s2, r2,
):
    y, x, z, c = place()
    loads = []
    for n, (a, b) in enumerate(
        ((tok_in, tok), (wk_in, wk), (wv_in, wv), (wq_in, wq), (cot_in, cot), (wo_in, wo))
    ):
        copy = pltpu.make_async_copy(a, b, s_in.at[n])
        copy.start()
        loads.append(copy)
    greet(all_partners(y, x, z, c))
    other = device(y, x, z, 1 - c)
    home = lax.div(z, 2)
    at_home = c == home
    slot = lax.rem(z, 2) * 2 + c
    group = 2 * x + c

    def project(src, w, dst, lane):
        def half(i, carry):
            rows = rows_of(i * 256, 256)
            got = jnp.dot(src[rows, :], w[...], preferred_element_type=F32)
            for h in range(HEADS):
                dst[h, rows, lane : lane + TILE] = got[:, h * TILE : (h + 1) * TILE].astype(BF)
            return carry

        lax.fori_loop(0, 2, half, 0)

    def exchange(staged, landing, base, send, recv):
        spot = rows_of(base + slot * 512, 512)
        copies = []
        near = remote(staged.at[z], landing.at[spot], send.at[0], recv.at[slot], other)

        @pl.when(at_home)
        def _():
            landing[spot, :] = staged[z]

        @pl.when(jnp.logical_not(at_home))
        def _():
            near.start()

        for d in (1, 3, 2):
            h = turn(z, d)
            copy = remote(staged.at[h], landing.at[spot], send.at[d], recv.at[slot], device(y, x, h, home))
            copy.start()
            copies.append(copy)
        return copies, near

    def settle_out(copies, near):
        for copy in copies:
            copy.wait_send()

        @pl.when(jnp.logical_not(at_home))
        def _():
            near.wait_send()

    def arrived(staged, landing, base, send, recv, i):
        mine = jnp.logical_and(z == 2 * c + lax.div(i, 2), c == lax.rem(i, 2))

        @pl.when(jnp.logical_not(mine))
        def _():
            remote(
                staged.at[0], landing.at[rows_of(base + i * 512, 512)], send.at[0], recv.at[i], other
            ).wait_recv()

    for n in range(3):
        loads[n].wait()
    project(tok, wk, kvs, 0)
    project(tok, wv, kvs, TILE)
    kv_sent = exchange(kvs, kv, OWN, s_kv, r_kv)
    for n in range(3, 6):
        loads[n].wait()
    project(tok, wq, qgs, 0)
    first_own = ((x * 4 + z) * 2 + c) * 4

    def grads(i, carry):
        rows = rows_of(i * TILE, TILE)
        got = lax.dot_general(cot[rows, :], wo[...], NT, preferred_element_type=F32)
        live = lax.broadcasted_iota(jnp.int32, (TILE, 512), 0) < lens[0, first_own + i]
        got = jnp.where(live, got, 0.0).astype(BF)
        for h in range(HEADS):
            qgs[h, rows, TILE : 2 * TILE] = got[:, h * TILE : (h + 1) * TILE]
        return carry

    lax.fori_loop(0, 4, grads, 0)
    qg_sent = exchange(qgs, qg, 0, s_qg, r_qg)

    ahead = device(y, turn(x, 1), z, c)
    behind = device(y, turn(x, 3), z, c)

    def halo_copy(i):
        return remote(
            kv.at[rows_of(OWN + i * 512, 512)], kv.at[rows_of(i * 512, 512)], s_h.at[i], r_h.at[i], ahead
        )

    def across_copy(start, i):
        return remote(
            kv.at[rows_of(start + i * 512, 512)],
            kv.at[rows_of(2048 + i * 512, 512)],
            s_x.at[i],
            r_x.at[i],
            other,
        )

    order = [lax.rem(lax.rem(z, 2) * 2 + k, 4) for k in range(4)]
    for i in order:
        arrived(kvs, kv, OWN, s_kv, r_kv, i)
        halo_copy(i).start()

        @pl.when(c == 0)
        def _():
            across_copy(OWN, i).start()

    def summary(i, carry):
        rows = rows_of(OWN + i * TILE, TILE)
        length = lens[0, group * 16 + i]
        live = lax.broadcasted_iota(jnp.int32, (TILE, 256), 0) < length
        total = jnp.sum(jnp.where(live, kv[rows, :].astype(F32), 0.0), axis=0, keepdims=True)
        sums[pl.ds(i, 1), :] = total / jnp.full((1, 256), length, jnp.int32).astype(F32)
        return carry

    lax.fori_loop(0, 16, summary, 0)
    summ[group] = sums[...].astype(BF)
    sum_copies = []
    pairs_of = [(d, cc) for d in range(4) for cc in (0, 1) if (d, cc) != (0, 0)]
    for d, cc in pairs_of:
        n = d * 2 + cc
        core = lax.rem(c + cc, 2)
        copy = remote(summ.at[group], summ.at[group], s_s.at[n], r_s.at[n], device(y, turn(x, d), z, core))
        copy.start()
        sum_copies.append(copy)

    def prepare(b, carry):
        rows = rows_of(b * TILE, TILE)
        kvt[:, rows] = jnp.transpose(kv[rows, :])
        return carry

    def clear(b, carry):
        gkv[rows_of(b * TILE, TILE), :] = jnp.zeros((TILE, 256), F32)
        return carry

    lax.fori_loop(0, 48, clear, 0)
    gsum[...] = jnp.zeros_like(gsum)
    for u in range(UNROLL):
        pair[u] = jnp.zeros((256, 256), BF)
        pairt[u] = jnp.zeros((256, 256), BF)
    lax.fori_loop(32, 48, prepare, 0)
    for k in range(4):
        i = lax.rem(lax.rem(z, 2) * 2 + k, 4)
        halo_copy(i).wait_recv()

        @pl.when(c == 1)
        def _():
            across_copy(0, i).start()

    lax.fori_loop(0, 16, prepare, 0)
    for i in range(4):
        across_copy(0, i).wait()
        halo_copy(i).wait_send()
        arrived(qgs, qg, 0, s_qg, r_qg, i)
    lax.fori_loop(16, 32, prepare, 0)
    for copy in sum_copies:
        copy.wait()
    kvt[:, 48 * TILE : 49 * TILE] = jnp.transpose(summ[...].reshape(TILE, 256))
    settle_out(*kv_sent)
    settle_out(*qg_sent)

    key_slot = lax.broadcasted_iota(jnp.int32, (TILE, TILE), 0)
    query_slot = lax.broadcasted_iota(jnp.int32, (TILE, TILE), 1)
    count = len(OFFSETS)

    def bar(it, carry):
        ids = [it * UNROLL + u for u in range(UNROLL)]
        tops, scales, deltas = [], [], []
        for u, qb in enumerate(ids):
            rows = rows_of(qb * TILE, TILE)
            pair[u, 0:TILE, 0:TILE] = qg[rows, 0:TILE]
            pair[u, TILE:, TILE:] = qg[rows, TILE:]
            pairt[u, 0:TILE, 0:TILE] = jnp.transpose(qg[rows, 0:TILE])
            pairt[u, TILE:, TILE:] = jnp.transpose(qg[rows, TILE:])
            both = pairt[u]
            this = 16 * group + qb
            top = None
            for j in range(count + 1):
                here = slice(j * TILE, (j + 1) * TILE)
                if j < count:
                    spot = rows_of((32 + qb - OFFSETS[j]) * TILE, TILE)
                    bar_id = this - OFFSETS[j]
                    length = jnp.where(bar_id >= 0, lens[0, jnp.maximum(bar_id, 0)], 0)
                    source = kv[spot, :]
                    gt[u, :, here] = kvt[:, spot]
                    ok = key_slot < length
                    if j == 0:
                        ok = jnp.logical_and(ok, key_slot <= query_slot)
                else:
                    source = summ[...].reshape(TILE, 256)
                    gt[u, :, here] = kvt[:, 48 * TILE : 49 * TILE]
                    distance = this - key_slot
                    ok = distance >= 1
                    for o in OFFSETS[1:]:
                        ok = jnp.logical_and(ok, distance != o)
                got = jnp.dot(source, both, preferred_element_type=F32)
                score = jnp.where(ok, got[:, :TILE] * (SCALE * LOG2E), NEG)
                sc[u, here, :TILE] = score
                sc[u, here, TILE:] = got[:, TILE:]
                high = jnp.max(score, axis=0, keepdims=True)
                top = high if top is None else jnp.maximum(top, high)
            tops.append(top)
        for u in range(UNROLL):
            total = jnp.zeros((1, TILE), F32)
            weighted = jnp.zeros((1, TILE), F32)
            for j in range(count + 1):
                here = slice(j * TILE, (j + 1) * TILE)
                e = jnp.exp2(sc[u, here, :TILE] - tops[u])
                sc[u, here, :TILE] = e
                total = total + jnp.sum(e, axis=0, keepdims=True)
                weighted = weighted + jnp.sum(e * sc[u, here, TILE:], axis=0, keepdims=True)
            scales.append(1.0 / total)
            deltas.append(weighted * scales[u])
        for u, qb in enumerate(ids):
            rows = rows_of(qb * TILE, TILE)
            both = pair[u]
            for j in range(count + 1):
                here = slice(j * TILE, (j + 1) * TILE)
                p = sc[u, here, :TILE] * scales[u]
                ds = (p * (sc[u, here, TILE:] - deltas[u])).astype(BF)
                block = jnp.concatenate([ds, p.astype(BF)], axis=1)
                dsp[u, here, :] = block
                got = jnp.dot(block, both, preferred_element_type=F32)
                if j < count:
                    spot = rows_of((32 + qb - OFFSETS[j]) * TILE, TILE)
                    gkv[spot, :] += got
                else:
                    gsum[...] += got
            both_out = jnp.dot(gt[u], dsp[u], preferred_element_type=F32)
            cg[rows, 0:TILE] = jnp.transpose(both_out[:TILE, :TILE] * SCALE).astype(BF)
            context = jnp.transpose(both_out[TILE:, TILE:])
            cg[rows, TILE:] = jnp.where(key_slot < lens[0, 16 * group + qb], context, 0.0).astype(BF)
        return carry

    def owner(i):
        to_z = 2 * c + lax.div(i, 2)
        core = lax.rem(i, 2)
        mine = jnp.logical_and(z == to_z, c == core)
        return device(y, x, to_z, core), mine

    def give_back(src, landing, send, recv, i):
        to, mine = owner(i)
        rows = rows_of(i * 512, 512)

        @pl.when(mine)
        def _():
            landing[z] = src[rows, :]

        @pl.when(jnp.logical_not(mine))
        def _():
            remote(src.at[rows], landing.at[z], send.at[i], recv.at[z], to).start()

    def settle(src, landing, send, recv):
        for i in range(4):
            to, mine = owner(i)

            @pl.when(jnp.logical_not(mine))
            def _():
                remote(src.at[pl.ds(i * 512, 512)], landing.at[z], send.at[i], recv.at[z], to).wait_send()

    def returned(src, landing, send, recv):
        for h in range(HEADS):
            mine = jnp.logical_and(z == h, at_home)

            @pl.when(jnp.logical_not(mine))
            def _():
                remote(src.at[pl.ds(0, 512)], landing.at[h], send.at[0], recv.at[h], other).wait_recv()

    def crossing(i):
        rows = rows_of(i * 512, 512)
        return remote(sx.at[rows], rx.at[rows], s_bx.at[i], r_bx.at[i], other)

    def cross(i):
        sx[rows_of(i * 512, 512), :] = gkv[rows_of(2048 + i * 512, 512), :].astype(BF)
        crossing(i).start()

    def halo_back(i):
        rows = rows_of(i * 512, 512)
        return remote(sh.at[rows], rh.at[rows], s_bh.at[i], r_bh.at[i], behind)

    def chunk(i, carry):
        lax.fori_loop(i * (4 // UNROLL), (i + 1) * (4 // UNROLL), bar, 0)

        @pl.when(c == 0)
        def _():
            rows = rows_of(i * 512, 512)
            sh[rows, :] = gkv[rows, :].astype(BF)
            halo_back(i).start()

        @pl.when(i >= 2)
        def _():
            cross(i - 2)
            cross(i)

        give_back(cg, ret_cg, s_cg, r_cg, i)
        return carry

    lax.fori_loop(0, 4, chunk, 0)
    gss[...] = gsum[...].astype(BF).reshape(8, 16, 256)
    gsr[group] = gss[group]
    back_copies = []
    for d, cc in pairs_of:
        n = d * 2 + cc
        to_x, core = turn(x, d), lax.rem(c + cc, 2)
        copy = remote(
            gss.at[to_x * 2 + core], gsr.at[group], s_gs.at[n], r_gs.at[n], device(y, to_x, z, core)
        )
        copy.start()
        back_copies.append(copy)
    turns = (0, 2, 1, 3)
    for i in turns:
        crossing(i).wait_recv()

        @pl.when(c == 1)
        def _():
            rows = pl.ds(i * 512, 512)
            sh[rows, :] = (gkv[rows, :] + rx[rows, :].astype(F32)).astype(BF)
            halo_back(i).start()

    def flatten(src, lane, n):
        for h in range(HEADS):
            flat[n, :, h * TILE : (h + 1) * TILE] = src[h, :, lane : lane + TILE]

    where = {"y": y, "x": x, "z": z}
    levels = ((w0, got1, 256), (w1, got2, 64), (w2, got3, 16))
    pending = [None] * 4
    started = []
    last = []

    def along(axis, d):
        at = dict(where)
        at[axis] = turn(where[axis], d)
        return device(at["y"], at["x"], at["z"], c)

    def core_half(m):
        return remote(wg.at[m, 1 - c], got0.at[m], s0.at[0, m], r0.at[0, m], other)

    def send_level(m, level):
        src, got, size = levels[level]
        copies = []
        axis = ORDERS[m][level]
        for d in (1, 2, 3):
            piece = pl.ds(pl.multiple_of(turn(where[axis], d) * size, 16), size)
            copy = remote(
                src.at[m, piece], got.at[m, d - 1], s1.at[level, m, d - 1], r1.at[level, m, d - 1], along(axis, d)
            )
            copy.start()
            copies.append(copy)
        pending[m] = copies
        started.extend(copies)

    def place_rows(m, level):
        a, b, d = (where[axis] for axis in ORDERS[m])
        start = a * 256
        if level >= 1:
            start = start + b * 64
        if level >= 2:
            start = start + d * 16
        return pl.ds(pl.multiple_of(start, 16), levels[level][2])

    half = pl.ds(pl.multiple_of(c * 256, 256), 256)

    def give(m, level):
        block = out.at[m, place_rows(m, level), half]
        copies = []
        for d in (1, 2, 3):
            copy = remote(
                block, block, s2.at[level, m, d - 1], r2.at[level, m, d - 1], along(ORDERS[m][level], d)
            )
            copy.start()
            copies.append(copy)
        pending[m] = copies
        started.extend(copies)

    def settled(m):
        for copy in pending[m]:
            copy.wait_recv()

    def begin(m):
        core_half(m).wait_recv()

        def add(i, carry):
            rows = rows_of(i * 256, 256)
            w0[m, rows, :] = (wg[m, c, rows, :].astype(F32) + got0[m, rows, :].astype(F32)).astype(BF)
            return carry

        lax.fori_loop(0, 4, add, 0)
        send_level(m, 0)

    def advance(m, level):
        src, got, size = levels[level]
        settled(m)
        mine = pl.ds(pl.multiple_of(where[ORDERS[m][level]] * size, 16), size)
        total = src[m, mine, :].astype(F32)
        for n in range(3):
            total = total + got[m, n].astype(F32)
        if level < 2:
            levels[level + 1][0][m] = total.astype(BF)
            send_level(m, level + 1)
        else:
            out[m, place_rows(m, 2), half] = total.astype(BF)
            give(m, 2)

    def finish(m):
        settled(m)
        copy = remote(out.at[m, :, half], out.at[m, :, half], s0.at[1, m], r0.at[1, m], other)
        copy.start()
        last.append(copy)

    def weight_grad(n, m):
        def part(i, carry):
            cols = rows_of(i * 256, 256)
            got = lax.dot_general(tok[:, cols], flat[n], TN, preferred_element_type=F32).astype(BF)
            wg[m, 0, cols, :] = got[:, :256]
            wg[m, 1, cols, :] = got[:, 256:]
            return carry

        lax.fori_loop(0, 4, part, 0)
        core_half(m).start()

    returned(cg, ret_cg, s_cg, r_cg)
    flatten(ret_cg, 0, 0)
    weight_grad(0, 0)
    flatten(ret_cg, TILE, 3)

    def out_grad(i, carry):
        cols = rows_of(i * 256, 256)
        got = lax.dot_general(flat[3], cot[:, cols], TN, preferred_element_type=F32).astype(BF)
        wg[3, lax.rem(i, 2), rows_of(lax.div(i, 2) * 512, 512), :] = got
        return carry

    lax.fori_loop(0, 4, out_grad, 0)
    core_half(3).start()
    begin(0)
    begin(3)

    for copy in back_copies:
        copy.wait()
    coarse = gsr[0].astype(F32)
    for n in range(1, 8):
        coarse = coarse + gsr[n].astype(F32)
    lane = lax.broadcasted_iota(jnp.int32, (1, 256), 1)
    factor = jnp.where(lane < TILE, SCALE, 1.0)
    for i in turns:
        halo_back(i).wait_recv()
        for b in range(4 * i, 4 * i + 4):
            rows = pl.ds(b * TILE, TILE)
            length = lens[0, group * 16 + b]
            live = lax.broadcasted_iota(jnp.int32, (TILE, 256), 0) < length
            share = coarse[b : b + 1, :] * (1.0 / jnp.full((1, 256), length, jnp.int32).astype(F32))
            extra = jnp.where(c == 0, rx[rows, :].astype(F32), 0.0)
            total = gkv[pl.ds(OWN + b * TILE, TILE), :] + rh[rows, :].astype(F32) + extra
            own[rows, :] = ((total + jnp.where(live, share, 0.0)) * factor).astype(BF)
        give_back(own, ret_kv, s_bkv, r_bkv, i)

    def mix(i, carry):
        rows = rows_of(i * 256, 256)
        mixed[rows, :] = jnp.dot(flat[3, rows, :], wo[...], preferred_element_type=F32).astype(BF)
        return carry

    lax.fori_loop(0, 2, mix, 0)
    advance(0, 0)
    advance(3, 0)
    returned(own, ret_kv, s_bkv, r_bkv)
    flatten(ret_kv, 0, 1)
    weight_grad(1, 1)
    flatten(ret_kv, TILE, 2)
    weight_grad(2, 2)
    begin(1)
    begin(2)
    advance(0, 1)
    advance(3, 1)
    advance(0, 2)
    advance(3, 2)

    def back(i, carry):
        rows = rows_of(i * 256, 256)
        total = lax.dot_general(flat[0, rows, :], wq[...], NT, preferred_element_type=F32)
        total = total + lax.dot_general(flat[1, rows, :], wk[...], NT, preferred_element_type=F32)
        total = total + lax.dot_general(flat[2, rows, :], wv[...], NT, preferred_element_type=F32)
        gin[rows, :] = total.astype(BF)
        return carry

    lax.fori_loop(0, 2, back, 0)
    for m in (0, 3):
        settled(m)
        give(m, 1)
    for m in (1, 2):
        advance(m, 0)
    for m in (0, 3):
        settled(m)
        give(m, 0)
    for level in (1, 2):
        for m in (1, 2):
            advance(m, level)
    for level in (1, 0):
        for m in (1, 2):
            settled(m)
            give(m, level)
    for m in (0, 3, 1, 2):
        finish(m)
    for copy in last:
        copy.wait()
    for m in range(4):
        core_half(m).wait_send()
        crossing(m).wait_send()
        halo_back(m).wait_send()
    for copy in started:
        copy.wait_send()
    settle(cg, ret_cg, s_cg, r_cg)
    settle(own, ret_kv, s_bkv, r_bkv)


ORDERS = ("yxz", "xzy", "zyx", "yzx")
UNROLL = 2

HB = pl.BlockSpec(memory_space=pl.ANY)
VM = pl.BlockSpec(memory_space=pltpu.VMEM)
SM = pl.BlockSpec(memory_space=pltpu.SMEM)
DMA = pltpu.SemaphoreType.DMA


def shape(*dims, kind=BF):
    return jax.ShapeDtypeStruct(dims, kind)


def local(tokens, lengths, w_query, w_key, w_value, w_out, cotangent):
    vm = pltpu.VMEM
    slabs = lambda n: [vm((2048, 256), BF)] * n
    heads = lambda n: [vm((4, 512, 256), BF)] * n
    mixed, gin, total = pl.pallas_call(
        whole_kernel,
        out_shape=(shape(512, 1024), shape(512, 1024), shape(4, 1024, 512)),
        in_specs=[SM] + [HB] * 6,
        out_specs=(VM, VM, VM),
        scratch_shapes=[vm((512, 1024), BF)] * 2
        + [vm((1024, 512), BF)] * 3
        + [vm((512, 1024), BF), vm((6144, 256), BF)]
        + slabs(1)
        + [vm((8, 16, 256), BF)]
        + heads(2)
        + [vm((16, 256), F32)]
        + [
            vm((256, 49 * TILE), BF),
            vm((UNROLL, 256, 10 * TILE), BF),
            vm((UNROLL, 256, 256), BF),
            vm((UNROLL, 256, 256), BF),
            vm((UNROLL, 10 * TILE, 256), F32),
            vm((UNROLL, 10 * TILE, 256), BF),
            vm((6144, 256), F32),
            vm((128, 256), F32),
        ]
        + slabs(5)
        + [vm((8, 16, 256), BF)] * 2
        + slabs(1)
        + heads(2)
        + [
            vm((4, 512, 512), BF),
            vm((4, 2, 1024, 256), BF),
            vm((4, 1024, 256), BF),
            vm((4, 1024, 256), BF),
            vm((4, 3, 256, 256), BF),
            vm((4, 256, 256), BF),
            vm((4, 3, 64, 256), BF),
            vm((4, 64, 256), BF),
            vm((4, 3, 16, 256), BF),
        ]
        + [DMA((6,))]
        + [DMA((4,))] * 8
        + [DMA((8,))] * 2
        + [DMA((4,))] * 8
        + [DMA((8,))] * 2
        + [DMA((2, 4))] * 2
        + [DMA((3, 4, 3))] * 4,
        compiler_params=pltpu.CompilerParams(
            collective_id=0, has_side_effects=True, vmem_limit_bytes=62 * MIB
        ),
        name="whole",
    )(lengths, tokens[0], w_key, w_value, w_query, cotangent[0], w_out)
    weights = [total[m].astype(F32) for m in range(3)]
    last = jnp.concatenate([total[3, :512], total[3, 512:]], axis=1).astype(F32)
    return (mixed[None], gin[None], *weights, last)


def solution(mesh):
    placed = (P("dp", "seq", None), P("dp", None), P(), P(), P(), P(), P("dp", "seq", None))
    return jax.shard_map(
        local,
        mesh=mesh,
        in_specs=placed,
        out_specs=(P("dp", "seq", None), P("dp", "seq", None), P(), P(), P(), P()),
        check_vma=False,
    )
```

```python
import functools
import math

import jax
import jax.numpy as jnp
from jax import lax
from jax.experimental import pallas as pl
from jax.experimental.pallas import tpu as pltpu
from jax.sharding import PartitionSpec as P

MESH = pl.DeviceIdType.MESH
BF = jnp.bfloat16
F32 = jnp.float32
HEADS = 4
TILE = 128
OFFSETS = (0, 1, 2, 4, 8, 12, 16, 24, 32)
SCALE = 1.0 / math.sqrt(128.0)
LOG2E = 1.4426950408889634
NEG = -1e30
NT = (((1,), (1,)), ((), ()))
TN = (((0,), (0,)), ((), ()))
OWN = 32 * TILE
MIB = 1024 * 1024


def place():
    s = lax.axis_index("seq")
    return lax.axis_index("dp"), lax.div(s, 8), lax.rem(lax.div(s, 2), 4), lax.rem(s, 2)


def device(y, x, z, c):
    return (y, (x * 4 + z) * 2 + c)


def turn(a, d):
    return lax.rem(a + d, 4)


def remote(src, dst, send, recv, to):
    return pltpu.make_async_remote_copy(
        src_ref=src, dst_ref=dst, send_sem=send, recv_sem=recv, device_id=to, device_id_type=MESH
    )


def greet(partners):
    barrier = pltpu.get_barrier_semaphore()
    for to in partners:
        pl.semaphore_signal(barrier, inc=1, device_id=to, device_id_type=MESH)
    pl.semaphore_wait(barrier, len(partners))


def all_partners(y, x, z, c):
    found = [device(y, x, z, 1 - c)]
    for d in (1, 2, 3):
        found.append(device(turn(y, d), x, z, c))
        for core in (0, 1):
            found.append(device(y, turn(x, d), z, core))
            found.append(device(y, x, turn(z, d), core))
    return found


def rows_of(start, count):
    return pl.ds(pl.multiple_of(start, TILE), count)


def whole_kernel(
    lens, tok_in, wk_in, wv_in, wq_in, cot_in, wo_in, mixed, gin, out,
    tok, cot, wq, wk, wv, wo,
    kv, qg, summ, kvs, qgs, sums,
    kvt, gt, pair, pairt, sc, dsp, gkv, gsum, cg,
    sx, rx, sh, rh, gss, gsr, own, ret_kv, ret_cg, flat,
    wg, got0, w0, got1, w1, got2, got3,
    s_in, s_kv, r_kv, s_qg, r_qg, s_h, r_h, s_x, r_x, s_s, r_s,
    s_bkv, r_bkv, s_cg, r_cg, s_bh, r_bh, s_bx, r_bx, s_gs, r_gs,
    s0, r0, s1, r1, s2, r2,
):
    y, x, z, c = place()
    loads = []
    for n, (a, b) in enumerate(
        ((tok_in, tok), (wk_in, wk), (wv_in, wv), (wq_in, wq), (cot_in, cot), (wo_in, wo))
    ):
        copy = pltpu.make_async_copy(a, b, s_in.at[n])
        copy.start()
        loads.append(copy)
    greet(all_partners(y, x, z, c))
    other = device(y, x, z, 1 - c)
    home = lax.div(z, 2)
    at_home = c == home
    slot = lax.rem(z, 2) * 2 + c
    group = 2 * x + c

    def project(src, w, dst, lane):
        def half(i, carry):
            rows = rows_of(i * 256, 256)
            got = jnp.dot(src[rows, :], w[...], preferred_element_type=F32)
            for h in range(HEADS):
                dst[h, rows, lane : lane + TILE] = got[:, h * TILE : (h + 1) * TILE].astype(BF)
            return carry

        lax.fori_loop(0, 2, half, 0)

    def exchange(staged, landing, base, send, recv):
        spot = rows_of(base + slot * 512, 512)
        copies = []
        near = remote(staged.at[z], landing.at[spot], send.at[0], recv.at[slot], other)

        @pl.when(at_home)
        def _():
            landing[spot, :] = staged[z]

        @pl.when(jnp.logical_not(at_home))
        def _():
            near.start()

        for d in (1, 3, 2):
            h = turn(z, d)
            copy = remote(staged.at[h], landing.at[spot], send.at[d], recv.at[slot], device(y, x, h, home))
            copy.start()
            copies.append(copy)
        return copies, near

    def settle_out(copies, near):
        for copy in copies:
            copy.wait_send()

        @pl.when(jnp.logical_not(at_home))
        def _():
            near.wait_send()

    def arrived(staged, landing, base, send, recv, i):
        mine = jnp.logical_and(z == 2 * c + lax.div(i, 2), c == lax.rem(i, 2))

        @pl.when(jnp.logical_not(mine))
        def _():
            remote(
                staged.at[0], landing.at[rows_of(base + i * 512, 512)], send.at[0], recv.at[i], other
            ).wait_recv()

    for n in range(3):
        loads[n].wait()
    project(tok, wk, kvs, 0)
    project(tok, wv, kvs, TILE)
    kv_sent = exchange(kvs, kv, OWN, s_kv, r_kv)
    for n in range(3, 6):
        loads[n].wait()
    project(tok, wq, qgs, 0)
    first_own = ((x * 4 + z) * 2 + c) * 4

    def grads(i, carry):
        rows = rows_of(i * TILE, TILE)
        got = lax.dot_general(cot[rows, :], wo[...], NT, preferred_element_type=F32)
        live = lax.broadcasted_iota(jnp.int32, (TILE, 512), 0) < lens[0, first_own + i]
        got = jnp.where(live, got, 0.0).astype(BF)
        for h in range(HEADS):
            qgs[h, rows, TILE : 2 * TILE] = got[:, h * TILE : (h + 1) * TILE]
        return carry

    lax.fori_loop(0, 4, grads, 0)
    qg_sent = exchange(qgs, qg, 0, s_qg, r_qg)

    ahead = device(y, turn(x, 1), z, c)
    behind = device(y, turn(x, 3), z, c)

    def halo_copy(i):
        return remote(
            kv.at[rows_of(OWN + i * 512, 512)], kv.at[rows_of(i * 512, 512)], s_h.at[i], r_h.at[i], ahead
        )

    def across_copy(start, i):
        return remote(
            kv.at[rows_of(start + i * 512, 512)],
            kv.at[rows_of(2048 + i * 512, 512)],
            s_x.at[i],
            r_x.at[i],
            other,
        )

    order = [lax.rem(lax.rem(z, 2) * 2 + k, 4) for k in range(4)]
    for i in order:
        arrived(kvs, kv, OWN, s_kv, r_kv, i)
        halo_copy(i).start()

        @pl.when(c == 0)
        def _():
            across_copy(OWN, i).start()

    def summary(i, carry):
        rows = rows_of(OWN + i * TILE, TILE)
        length = lens[0, group * 16 + i]
        live = lax.broadcasted_iota(jnp.int32, (TILE, 256), 0) < length
        total = jnp.sum(jnp.where(live, kv[rows, :].astype(F32), 0.0), axis=0, keepdims=True)
        sums[pl.ds(i, 1), :] = total / jnp.full((1, 256), length, jnp.int32).astype(F32)
        return carry

    lax.fori_loop(0, 16, summary, 0)
    summ[group] = sums[...].astype(BF)
    sum_copies = []
    pairs_of = [(d, cc) for d in range(4) for cc in (0, 1) if (d, cc) != (0, 0)]
    for d, cc in pairs_of:
        n = d * 2 + cc
        core = lax.rem(c + cc, 2)
        copy = remote(summ.at[group], summ.at[group], s_s.at[n], r_s.at[n], device(y, turn(x, d), z, core))
        copy.start()
        sum_copies.append(copy)

    def prepare(b, carry):
        rows = rows_of(b * TILE, TILE)
        kvt[:, rows] = jnp.transpose(kv[rows, :])
        return carry

    def clear(b, carry):
        gkv[rows_of(b * TILE, TILE), :] = jnp.zeros((TILE, 256), F32)
        return carry

    lax.fori_loop(0, 48, clear, 0)
    gsum[...] = jnp.zeros_like(gsum)
    for u in range(UNROLL):
        pair[u] = jnp.zeros((256, 256), BF)
        pairt[u] = jnp.zeros((256, 256), BF)
    lax.fori_loop(32, 48, prepare, 0)
    for k in range(4):
        i = lax.rem(lax.rem(z, 2) * 2 + k, 4)
        halo_copy(i).wait_recv()

        @pl.when(c == 1)
        def _():
            across_copy(0, i).start()

    lax.fori_loop(0, 16, prepare, 0)
    for i in range(4):
        across_copy(0, i).wait()
        halo_copy(i).wait_send()
        arrived(qgs, qg, 0, s_qg, r_qg, i)
    lax.fori_loop(16, 32, prepare, 0)
    for copy in sum_copies:
        copy.wait()
    kvt[:, 48 * TILE : 49 * TILE] = jnp.transpose(summ[...].reshape(TILE, 256))
    settle_out(*kv_sent)
    settle_out(*qg_sent)

    key_slot = lax.broadcasted_iota(jnp.int32, (TILE, TILE), 0)
    query_slot = lax.broadcasted_iota(jnp.int32, (TILE, TILE), 1)
    count = len(OFFSETS)

    def bar(it, carry):
        ids = [it * UNROLL + u for u in range(UNROLL)]
        tops, scales, deltas = [], [], []
        for u, qb in enumerate(ids):
            rows = rows_of(qb * TILE, TILE)
            pair[u, 0:TILE, 0:TILE] = qg[rows, 0:TILE]
            pair[u, TILE:, TILE:] = qg[rows, TILE:]
            pairt[u, 0:TILE, 0:TILE] = jnp.transpose(qg[rows, 0:TILE])
            pairt[u, TILE:, TILE:] = jnp.transpose(qg[rows, TILE:])
            both = pairt[u]
            this = 16 * group + qb
            top = None
            for j in range(count + 1):
                here = slice(j * TILE, (j + 1) * TILE)
                if j < count:
                    spot = rows_of((32 + qb - OFFSETS[j]) * TILE, TILE)
                    bar_id = this - OFFSETS[j]
                    length = jnp.where(bar_id >= 0, lens[0, jnp.maximum(bar_id, 0)], 0)
                    source = kv[spot, :]
                    gt[u, :, here] = kvt[:, spot]
                    ok = key_slot < length
                    if j == 0:
                        ok = jnp.logical_and(ok, key_slot <= query_slot)
                else:
                    source = summ[...].reshape(TILE, 256)
                    gt[u, :, here] = kvt[:, 48 * TILE : 49 * TILE]
                    distance = this - key_slot
                    ok = distance >= 1
                    for o in OFFSETS[1:]:
                        ok = jnp.logical_and(ok, distance != o)
                got = jnp.dot(source, both, preferred_element_type=F32)
                score = jnp.where(ok, got[:, :TILE] * (SCALE * LOG2E), NEG)
                sc[u, here, :TILE] = score
                sc[u, here, TILE:] = got[:, TILE:]
                high = jnp.max(score, axis=0, keepdims=True)
                top = high if top is None else jnp.maximum(top, high)
            tops.append(top)
        for u in range(UNROLL):
            total = jnp.zeros((1, TILE), F32)
            weighted = jnp.zeros((1, TILE), F32)
            for j in range(count + 1):
                here = slice(j * TILE, (j + 1) * TILE)
                e = jnp.exp2(sc[u, here, :TILE] - tops[u])
                sc[u, here, :TILE] = e
                total = total + jnp.sum(e, axis=0, keepdims=True)
                weighted = weighted + jnp.sum(e * sc[u, here, TILE:], axis=0, keepdims=True)
            scales.append(1.0 / total)
            deltas.append(weighted * scales[u])
        for u, qb in enumerate(ids):
            rows = rows_of(qb * TILE, TILE)
            both = pair[u]
            for j in range(count + 1):
                here = slice(j * TILE, (j + 1) * TILE)
                p = sc[u, here, :TILE] * scales[u]
                ds = (p * (sc[u, here, TILE:] - deltas[u])).astype(BF)
                block = jnp.concatenate([ds, p.astype(BF)], axis=1)
                dsp[u, here, :] = block
                got = jnp.dot(block, both, preferred_element_type=F32)
                if j < count:
                    spot = rows_of((32 + qb - OFFSETS[j]) * TILE, TILE)
                    gkv[spot, :] += got
                else:
                    gsum[...] += got
            both_out = jnp.dot(gt[u], dsp[u], preferred_element_type=F32)
            cg[rows, 0:TILE] = jnp.transpose(both_out[:TILE, :TILE] * SCALE).astype(BF)
            context = jnp.transpose(both_out[TILE:, TILE:])
            cg[rows, TILE:] = jnp.where(key_slot < lens[0, 16 * group + qb], context, 0.0).astype(BF)
        return carry

    def owner(i):
        to_z = 2 * c + lax.div(i, 2)
        core = lax.rem(i, 2)
        mine = jnp.logical_and(z == to_z, c == core)
        return device(y, x, to_z, core), mine

    def give_back(src, landing, send, recv, i):
        to, mine = owner(i)
        rows = rows_of(i * 512, 512)

        @pl.when(mine)
        def _():
            landing[z] = src[rows, :]

        @pl.when(jnp.logical_not(mine))
        def _():
            remote(src.at[rows], landing.at[z], send.at[i], recv.at[z], to).start()

    def settle(src, landing, send, recv):
        for i in range(4):
            to, mine = owner(i)

            @pl.when(jnp.logical_not(mine))
            def _():
                remote(src.at[pl.ds(i * 512, 512)], landing.at[z], send.at[i], recv.at[z], to).wait_send()

    def returned(src, landing, send, recv):
        for h in range(HEADS):
            mine = jnp.logical_and(z == h, at_home)

            @pl.when(jnp.logical_not(mine))
            def _():
                remote(src.at[pl.ds(0, 512)], landing.at[h], send.at[0], recv.at[h], other).wait_recv()

    def crossing(i):
        rows = rows_of(i * 512, 512)
        return remote(sx.at[rows], rx.at[rows], s_bx.at[i], r_bx.at[i], other)

    def cross(i):
        sx[rows_of(i * 512, 512), :] = gkv[rows_of(2048 + i * 512, 512), :].astype(BF)
        crossing(i).start()

    def halo_back(i):
        rows = rows_of(i * 512, 512)
        return remote(sh.at[rows], rh.at[rows], s_bh.at[i], r_bh.at[i], behind)

    def chunk(i, carry):
        lax.fori_loop(i * (4 // UNROLL), (i + 1) * (4 // UNROLL), bar, 0)

        @pl.when(c == 0)
        def _():
            rows = rows_of(i * 512, 512)
            sh[rows, :] = gkv[rows, :].astype(BF)
            halo_back(i).start()

        @pl.when(i >= 2)
        def _():
            cross(i - 2)
            cross(i)

        give_back(cg, ret_cg, s_cg, r_cg, i)
        return carry

    lax.fori_loop(0, 4, chunk, 0)
    gss[...] = gsum[...].astype(BF).reshape(8, 16, 256)
    gsr[group] = gss[group]
    back_copies = []
    for d, cc in pairs_of:
        n = d * 2 + cc
        to_x, core = turn(x, d), lax.rem(c + cc, 2)
        copy = remote(
            gss.at[to_x * 2 + core], gsr.at[group], s_gs.at[n], r_gs.at[n], device(y, to_x, z, core)
        )
        copy.start()
        back_copies.append(copy)
    turns = (0, 2, 1, 3)
    for i in turns:
        crossing(i).wait_recv()

        @pl.when(c == 1)
        def _():
            rows = pl.ds(i * 512, 512)
            sh[rows, :] = (gkv[rows, :] + rx[rows, :].astype(F32)).astype(BF)
            halo_back(i).start()

    def flatten(src, lane, n):
        for h in range(HEADS):
            flat[n, :, h * TILE : (h + 1) * TILE] = src[h, :, lane : lane + TILE]

    where = {"y": y, "x": x, "z": z}
    levels = ((w0, got1, 256), (w1, got2, 64))
    pending = [None] * 4
    started = []
    last = []

    def along(axis, d):
        at = dict(where)
        at[axis] = turn(where[axis], d)
        return device(at["y"], at["x"], at["z"], c)

    def core_half(m):
        return remote(wg.at[m, 1 - c], got0.at[m], s0.at[0, m], r0.at[0, m], other)

    def send_level(m, level):
        src, got, size = levels[level]
        copies = []
        axis = ORDERS[m][level]
        for d in (1, 2, 3):
            piece = pl.ds(pl.multiple_of(turn(where[axis], d) * size, 16), size)
            copy = remote(
                src.at[m, piece], got.at[m, d - 1], s1.at[level, m, d - 1], r1.at[level, m, d - 1], along(axis, d)
            )
            copy.start()
            copies.append(copy)
        pending[m] = copies
        started.extend(copies)

    def place_rows(m, level):
        start = where[ORDERS[m][0]] * 256
        if level == 1:
            start = start + where[ORDERS[m][1]] * 64
        return pl.ds(pl.multiple_of(start, 16), levels[level][2])

    half = pl.ds(pl.multiple_of(c * 256, 256), 256)

    def give(m, level):
        block = out.at[m, place_rows(m, level), half]
        copies = []
        for d in (1, 2, 3):
            copy = remote(
                block, block, s2.at[level, m, d - 1], r2.at[level, m, d - 1], along(ORDERS[m][level], d)
            )
            copy.start()
            copies.append(copy)
        pending[m] = copies
        started.extend(copies)

    def settled(m):
        for copy in pending[m]:
            copy.wait_recv()

    def begin(m):
        core_half(m).wait_recv()

        def add(i, carry):
            rows = rows_of(i * 256, 256)
            w0[m, rows, :] = (wg[m, c, rows, :].astype(F32) + got0[m, rows, :].astype(F32)).astype(BF)
            return carry

        lax.fori_loop(0, 4, add, 0)
        send_level(m, 0)

    def advance(m, level):
        settled(m)
        if level == 2:
            total = got3[m, 0].astype(F32)
            for n in range(1, 4):
                total = total + got3[m, n].astype(F32)
            out[m, place_rows(m, 1), half] = total.astype(BF)
            give(m, 1)
            return
        src, got, size = levels[level]
        mine = pl.ds(pl.multiple_of(where[ORDERS[m][level]] * size, 16), size)
        total = src[m, mine, :].astype(F32)
        for n in range(3):
            total = total + got[m, n].astype(F32)
        if level == 0:
            w1[m] = total.astype(BF)
            send_level(m, 1)
        else:
            axis = ORDERS[m][2]
            got3[m, where[axis]] = total.astype(BF)
            block = got3.at[m, where[axis]]
            copies = []
            for d in (1, 2, 3):
                copy = remote(block, block, s1.at[2, m, d - 1], r1.at[2, m, d - 1], along(axis, d))
                copy.start()
                copies.append(copy)
            pending[m] = copies
            started.extend(copies)

    def finish(m):
        settled(m)
        copy = remote(out.at[m, :, half], out.at[m, :, half], s0.at[1, m], r0.at[1, m], other)
        copy.start()
        last.append(copy)

    def weight_grad(n, m):
        def part(i, carry):
            cols = rows_of(i * 256, 256)
            got = lax.dot_general(tok[:, cols], flat[n], TN, preferred_element_type=F32).astype(BF)
            wg[m, 0, cols, :] = got[:, :256]
            wg[m, 1, cols, :] = got[:, 256:]
            return carry

        lax.fori_loop(0, 4, part, 0)
        core_half(m).start()

    returned(cg, ret_cg, s_cg, r_cg)
    flatten(ret_cg, 0, 0)
    weight_grad(0, 0)
    flatten(ret_cg, TILE, 3)

    def out_grad(i, carry):
        cols = rows_of(i * 256, 256)
        got = lax.dot_general(flat[3], cot[:, cols], TN, preferred_element_type=F32).astype(BF)
        wg[3, lax.rem(i, 2), rows_of(lax.div(i, 2) * 512, 512), :] = got
        return carry

    lax.fori_loop(0, 4, out_grad, 0)
    core_half(3).start()
    begin(0)
    begin(3)

    for copy in back_copies:
        copy.wait()
    coarse = gsr[0].astype(F32)
    for n in range(1, 8):
        coarse = coarse + gsr[n].astype(F32)
    lane = lax.broadcasted_iota(jnp.int32, (1, 256), 1)
    factor = jnp.where(lane < TILE, SCALE, 1.0)
    for i in turns:
        halo_back(i).wait_recv()
        for b in range(4 * i, 4 * i + 4):
            rows = pl.ds(b * TILE, TILE)
            length = lens[0, group * 16 + b]
            live = lax.broadcasted_iota(jnp.int32, (TILE, 256), 0) < length
            share = coarse[b : b + 1, :] * (1.0 / jnp.full((1, 256), length, jnp.int32).astype(F32))
            extra = jnp.where(c == 0, rx[rows, :].astype(F32), 0.0)
            total = gkv[pl.ds(OWN + b * TILE, TILE), :] + rh[rows, :].astype(F32) + extra
            own[rows, :] = ((total + jnp.where(live, share, 0.0)) * factor).astype(BF)
        give_back(own, ret_kv, s_bkv, r_bkv, i)

    def mix(i, carry):
        rows = rows_of(i * 256, 256)
        mixed[rows, :] = jnp.dot(flat[3, rows, :], wo[...], preferred_element_type=F32).astype(BF)
        return carry

    lax.fori_loop(0, 2, mix, 0)
    for level in range(3):
        advance(0, level)
        advance(3, level)
    returned(own, ret_kv, s_bkv, r_bkv)
    flatten(ret_kv, 0, 1)
    weight_grad(1, 1)
    flatten(ret_kv, TILE, 2)
    weight_grad(2, 2)
    begin(1)
    begin(2)
    for m in (0, 3):
        settled(m)
        give(m, 0)

    def back(i, carry):
        rows = rows_of(i * 256, 256)
        total = lax.dot_general(flat[0, rows, :], wq[...], NT, preferred_element_type=F32)
        total = total + lax.dot_general(flat[1, rows, :], wk[...], NT, preferred_element_type=F32)
        total = total + lax.dot_general(flat[2, rows, :], wv[...], NT, preferred_element_type=F32)
        gin[rows, :] = total.astype(BF)
        return carry

    lax.fori_loop(0, 2, back, 0)
    for level in range(3):
        advance(1, level)
        advance(2, level)
    for m in (1, 2):
        settled(m)
        give(m, 0)
    for m in (0, 3, 1, 2):
        finish(m)
    for copy in last:
        copy.wait()
    for m in range(4):
        core_half(m).wait_send()
        crossing(m).wait_send()
        halo_back(m).wait_send()
    for copy in started:
        copy.wait_send()
    settle(cg, ret_cg, s_cg, r_cg)
    settle(own, ret_kv, s_bkv, r_bkv)


def hand_over(mixed, gin, a, b, c, low, high, mixed_out, gin_out, a_out, b_out, c_out, d_out):
    mixed_out[...] = mixed[...]
    gin_out[...] = gin[...]
    for src, dst in ((a, a_out), (b, b_out), (c, c_out)):
        dst[...] = src[0].astype(F32)
    d_out[:, :512] = low[0].astype(F32)
    d_out[:, 512:] = high[0].astype(F32)


ORDERS = ("yxz", "xzy", "zyx", "yzx")
UNROLL = 2

HB = pl.BlockSpec(memory_space=pl.ANY)
VM = pl.BlockSpec(memory_space=pltpu.VMEM)
SM = pl.BlockSpec(memory_space=pltpu.SMEM)
DMA = pltpu.SemaphoreType.DMA


def shape(*dims, kind=BF):
    return jax.ShapeDtypeStruct(dims, kind)


def local(tokens, lengths, w_query, w_key, w_value, w_out, cotangent):
    vm = pltpu.VMEM
    slabs = lambda n: [vm((2048, 256), BF)] * n
    heads = lambda n: [vm((4, 512, 256), BF)] * n
    mixed, gin, total = pl.pallas_call(
        whole_kernel,
        out_shape=(shape(512, 1024), shape(512, 1024), shape(4, 1024, 512)),
        in_specs=[SM] + [HB] * 6,
        out_specs=(VM, VM, VM),
        scratch_shapes=[vm((512, 1024), BF)] * 2
        + [vm((1024, 512), BF)] * 3
        + [vm((512, 1024), BF), vm((6144, 256), BF)]
        + slabs(1)
        + [vm((8, 16, 256), BF)]
        + heads(2)
        + [vm((16, 256), F32)]
        + [
            vm((256, 49 * TILE), BF),
            vm((UNROLL, 256, 10 * TILE), BF),
            vm((UNROLL, 256, 256), BF),
            vm((UNROLL, 256, 256), BF),
            vm((UNROLL, 10 * TILE, 256), F32),
            vm((UNROLL, 10 * TILE, 256), BF),
            vm((6144, 256), F32),
            vm((128, 256), F32),
        ]
        + slabs(5)
        + [vm((8, 16, 256), BF)] * 2
        + slabs(1)
        + heads(2)
        + [
            vm((4, 512, 512), BF),
            vm((4, 2, 1024, 256), BF),
            vm((4, 1024, 256), BF),
            vm((4, 1024, 256), BF),
            vm((4, 3, 256, 256), BF),
            vm((4, 256, 256), BF),
            vm((4, 3, 64, 256), BF),
            vm((4, 4, 64, 256), BF),
        ]
        + [DMA((6,))]
        + [DMA((4,))] * 8
        + [DMA((8,))] * 2
        + [DMA((4,))] * 8
        + [DMA((8,))] * 2
        + [DMA((2, 4))] * 2
        + [DMA((3, 4, 3))] * 2
        + [DMA((2, 4, 3))] * 2,
        compiler_params=pltpu.CompilerParams(
            collective_id=0, has_side_effects=True, vmem_limit_bytes=62 * MIB
        ),
        name="whole",
    )(lengths, tokens[0], w_key, w_value, w_query, cotangent[0], w_out)
    block = pl.BlockSpec
    mixed, gin, *weights = pl.pallas_call(
        hand_over,
        grid=(8,),
        out_shape=(shape(512, 1024), shape(512, 1024))
        + (shape(1024, 512, kind=F32),) * 3
        + (shape(512, 1024, kind=F32),),
        in_specs=[block((64, 1024), lambda i: (i, 0))] * 2
        + [block((1, 128, 512), lambda i, m=m: (m, i, 0)) for m in range(3)]
        + [block((1, 64, 512), lambda i, n=n: (3, n + i, 0)) for n in (0, 8)],
        out_specs=[block((64, 1024), lambda i: (i, 0))] * 2
        + [block((128, 512), lambda i: (i, 0))] * 3
        + [block((64, 1024), lambda i: (i, 0))],
        compiler_params=pltpu.CompilerParams(vmem_limit_bytes=40 * MIB),
        name="hand_over",
    )(mixed, gin, total, total, total, total, total)
    return (mixed[None], gin[None], *weights)


def solution(mesh):
    placed = (P("dp", "seq", None), P("dp", None), P(), P(), P(), P(), P("dp", "seq", None))
    return jax.shard_map(
        local,
        mesh=mesh,
        in_specs=placed,
        out_specs=(P("dp", "seq", None), P("dp", "seq", None), P(), P(), P(), P()),
        check_vma=False,
    )
```

```python
import functools
import math

import jax
import jax.numpy as jnp
from jax import lax
from jax.experimental import pallas as pl
from jax.experimental.pallas import tpu as pltpu
from jax.sharding import PartitionSpec as P

MESH = pl.DeviceIdType.MESH
BF = jnp.bfloat16
F32 = jnp.float32
HEADS = 4
TILE = 128
OFFSETS = (0, 1, 2, 4, 8, 12, 16, 24, 32)
SCALE = 1.0 / math.sqrt(128.0)
LOG2E = 1.4426950408889634
NEG = -1e30
NT = (((1,), (1,)), ((), ()))
TN = (((0,), (0,)), ((), ()))
OWN = 32 * TILE
MIB = 1024 * 1024


def place():
    s = lax.axis_index("seq")
    return lax.axis_index("dp"), lax.div(s, 8), lax.rem(lax.div(s, 2), 4), lax.rem(s, 2)


def device(y, x, z, c):
    return (y, (x * 4 + z) * 2 + c)


def turn(a, d):
    return lax.rem(a + d, 4)


def remote(src, dst, send, recv, to):
    return pltpu.make_async_remote_copy(
        src_ref=src, dst_ref=dst, send_sem=send, recv_sem=recv, device_id=to, device_id_type=MESH
    )


def all_partners(y, x, z, c):
    found = [device(y, x, z, 1 - c)]
    for d in (1, 2, 3):
        found.append(device(turn(y, d), x, z, c))
        for core in (0, 1):
            found.append(device(y, turn(x, d), z, core))
            found.append(device(y, x, turn(z, d), core))
    return found


def rows_of(start, count):
    return pl.ds(pl.multiple_of(start, TILE), count)


def whole_kernel(
    lens, tok_in, wk_in, wv_in, wq_in, cot_in, wo_in, mixed, gin, out,
    tok, cot, wq, wk, wv, wo,
    kv, qg, summ, kvs, qgs, sums,
    kvt, gt, pair, pairt, sc, dsp, gkv, gsum, cg,
    sx, rx, sh, rh, gss, gsr, own, ret_kv, ret_cg, flat,
    wg, got0, w0, got1, w1, got2, got3,
    s_in, s_kv, r_kv, s_qg, r_qg, s_h, r_h, s_x, r_x, s_s, r_s,
    s_bkv, r_bkv, s_cg, r_cg, s_bh, r_bh, s_bx, r_bx, s_gs, r_gs,
    s0, r0, s1, r1, s2, r2,
):
    y, x, z, c = place()
    loads = []
    for n, (a, b) in enumerate(
        ((tok_in, tok), (wk_in, wk), (wv_in, wv), (wq_in, wq), (cot_in, cot), (wo_in, wo))
    ):
        copy = pltpu.make_async_copy(a, b, s_in.at[n])
        copy.start()
        loads.append(copy)
    partners = all_partners(y, x, z, c)
    barrier = pltpu.get_barrier_semaphore()
    for to in partners:
        pl.semaphore_signal(barrier, inc=1, device_id=to, device_id_type=MESH)
    other = device(y, x, z, 1 - c)
    home = lax.div(z, 2)
    at_home = c == home
    slot = lax.rem(z, 2) * 2 + c
    group = 2 * x + c

    def project(src, w, dst, lane):
        def half(i, carry):
            rows = rows_of(i * 256, 256)
            got = jnp.dot(src[rows, :], w[...], preferred_element_type=F32)
            for h in range(HEADS):
                dst[h, rows, lane : lane + TILE] = got[:, h * TILE : (h + 1) * TILE].astype(BF)
            return carry

        lax.fori_loop(0, 2, half, 0)

    def exchange(staged, landing, base, send, recv):
        spot = rows_of(base + slot * 512, 512)
        copies = []
        near = remote(staged.at[z], landing.at[spot], send.at[0], recv.at[slot], other)

        @pl.when(at_home)
        def _():
            landing[spot, :] = staged[z]

        @pl.when(jnp.logical_not(at_home))
        def _():
            near.start()

        for d in (1, 3, 2):
            h = turn(z, d)
            copy = remote(staged.at[h], landing.at[spot], send.at[d], recv.at[slot], device(y, x, h, home))
            copy.start()
            copies.append(copy)
        return copies, near

    def settle_out(copies, near):
        for copy in copies:
            copy.wait_send()

        @pl.when(jnp.logical_not(at_home))
        def _():
            near.wait_send()

    def arrived(staged, landing, base, send, recv, i):
        mine = jnp.logical_and(z == 2 * c + lax.div(i, 2), c == lax.rem(i, 2))

        @pl.when(jnp.logical_not(mine))
        def _():
            remote(
                staged.at[0], landing.at[rows_of(base + i * 512, 512)], send.at[0], recv.at[i], other
            ).wait_recv()

    for n in range(3):
        loads[n].wait()
    project(tok, wk, kvs, 0)
    project(tok, wv, kvs, TILE)
    pl.semaphore_wait(barrier, len(partners))
    kv_sent = exchange(kvs, kv, OWN, s_kv, r_kv)
    for n in range(3, 6):
        loads[n].wait()
    project(tok, wq, qgs, 0)
    first_own = ((x * 4 + z) * 2 + c) * 4

    def grads(i, carry):
        rows = rows_of(i * TILE, TILE)
        got = lax.dot_general(cot[rows, :], wo[...], NT, preferred_element_type=F32)
        live = lax.broadcasted_iota(jnp.int32, (TILE, 512), 0) < lens[0, first_own + i]
        got = jnp.where(live, got, 0.0).astype(BF)
        for h in range(HEADS):
            qgs[h, rows, TILE : 2 * TILE] = got[:, h * TILE : (h + 1) * TILE]
        return carry

    lax.fori_loop(0, 4, grads, 0)
    ahead = device(y, turn(x, 1), z, c)
    behind = device(y, turn(x, 3), z, c)

    def halo_copy(i):
        return remote(
            kv.at[rows_of(OWN + i * 512, 512)], kv.at[rows_of(i * 512, 512)], s_h.at[i], r_h.at[i], ahead
        )

    def across_copy(start, i):
        return remote(
            kv.at[rows_of(start + i * 512, 512)],
            kv.at[rows_of(2048 + i * 512, 512)],
            s_x.at[i],
            r_x.at[i],
            other,
        )

    order = [lax.rem(lax.rem(z, 2) * 2 + k, 4) for k in range(4)]
    for i in order:
        arrived(kvs, kv, OWN, s_kv, r_kv, i)
        halo_copy(i).start()

        @pl.when(c == 0)
        def _():
            across_copy(OWN, i).start()

    qg_sent = exchange(qgs, qg, 0, s_qg, r_qg)

    def summary(i, carry):
        rows = rows_of(OWN + i * TILE, TILE)
        length = lens[0, group * 16 + i]
        live = lax.broadcasted_iota(jnp.int32, (TILE, 256), 0) < length
        total = jnp.sum(jnp.where(live, kv[rows, :].astype(F32), 0.0), axis=0, keepdims=True)
        sums[pl.ds(i, 1), :] = total / jnp.full((1, 256), length, jnp.int32).astype(F32)
        return carry

    lax.fori_loop(0, 16, summary, 0)
    summ[group] = sums[...].astype(BF)
    sum_copies = []
    pairs_of = [(d, cc) for d in range(4) for cc in (0, 1) if (d, cc) != (0, 0)]
    for d, cc in pairs_of:
        n = d * 2 + cc
        core = lax.rem(c + cc, 2)
        copy = remote(summ.at[group], summ.at[group], s_s.at[n], r_s.at[n], device(y, turn(x, d), z, core))
        copy.start()
        sum_copies.append(copy)

    def prepare(b, carry):
        rows = rows_of(b * TILE, TILE)
        kvt[:, rows] = jnp.transpose(kv[rows, :])
        return carry

    def clear(b, carry):
        gkv[rows_of(b * TILE, TILE), :] = jnp.zeros((TILE, 256), F32)
        return carry

    lax.fori_loop(0, 48, clear, 0)
    gsum[...] = jnp.zeros_like(gsum)
    for u in range(UNROLL):
        pair[u] = jnp.zeros((256, 256), BF)
        pairt[u] = jnp.zeros((256, 256), BF)
    lax.fori_loop(32, 48, prepare, 0)
    for k in range(4):
        i = lax.rem(lax.rem(z, 2) * 2 + k, 4)
        halo_copy(i).wait_recv()

        @pl.when(c == 1)
        def _():
            across_copy(0, i).start()

    lax.fori_loop(0, 16, prepare, 0)
    for i in range(4):
        across_copy(0, i).wait()
        halo_copy(i).wait_send()
        arrived(qgs, qg, 0, s_qg, r_qg, i)
    lax.fori_loop(16, 32, prepare, 0)
    for copy in sum_copies:
        copy.wait()
    kvt[:, 48 * TILE : 49 * TILE] = jnp.transpose(summ[...].reshape(TILE, 256))
    settle_out(*kv_sent)
    settle_out(*qg_sent)

    key_slot = lax.broadcasted_iota(jnp.int32, (TILE, TILE), 0)
    query_slot = lax.broadcasted_iota(jnp.int32, (TILE, TILE), 1)
    count = len(OFFSETS)

    def bar(it, carry):
        ids = [it * UNROLL + u for u in range(UNROLL)]
        tops, scales, deltas = [], [], []
        for u, qb in enumerate(ids):
            rows = rows_of(qb * TILE, TILE)
            pair[u, 0:TILE, 0:TILE] = qg[rows, 0:TILE]
            pair[u, TILE:, TILE:] = qg[rows, TILE:]
            pairt[u, 0:TILE, 0:TILE] = jnp.transpose(qg[rows, 0:TILE])
            pairt[u, TILE:, TILE:] = jnp.transpose(qg[rows, TILE:])
            both = pairt[u]
            this = 16 * group + qb
            top = None
            for j in range(count + 1):
                here = slice(j * TILE, (j + 1) * TILE)
                if j < count:
                    spot = rows_of((32 + qb - OFFSETS[j]) * TILE, TILE)
                    bar_id = this - OFFSETS[j]
                    length = jnp.where(bar_id >= 0, lens[0, jnp.maximum(bar_id, 0)], 0)
                    source = kv[spot, :]
                    gt[u, :, here] = kvt[:, spot]
                    ok = key_slot < length
                    if j == 0:
                        ok = jnp.logical_and(ok, key_slot <= query_slot)
                else:
                    source = summ[...].reshape(TILE, 256)
                    gt[u, :, here] = kvt[:, 48 * TILE : 49 * TILE]
                    distance = this - key_slot
                    ok = distance >= 1
                    for o in OFFSETS[1:]:
                        ok = jnp.logical_and(ok, distance != o)
                got = jnp.dot(source, both, preferred_element_type=F32)
                score = jnp.where(ok, got[:, :TILE] * (SCALE * LOG2E), NEG)
                sc[u, here, :TILE] = score
                sc[u, here, TILE:] = got[:, TILE:]
                high = jnp.max(score, axis=0, keepdims=True)
                top = high if top is None else jnp.maximum(top, high)
            tops.append(top)
        for u in range(UNROLL):
            total = jnp.zeros((1, TILE), F32)
            weighted = jnp.zeros((1, TILE), F32)
            for j in range(count + 1):
                here = slice(j * TILE, (j + 1) * TILE)
                e = jnp.exp2(sc[u, here, :TILE] - tops[u])
                sc[u, here, :TILE] = e
                total = total + jnp.sum(e, axis=0, keepdims=True)
                weighted = weighted + jnp.sum(e * sc[u, here, TILE:], axis=0, keepdims=True)
            scales.append(1.0 / total)
            deltas.append(weighted * scales[u])
        for u, qb in enumerate(ids):
            rows = rows_of(qb * TILE, TILE)
            both = pair[u]
            for j in range(count + 1):
                here = slice(j * TILE, (j + 1) * TILE)
                p = sc[u, here, :TILE] * scales[u]
                ds = (p * (sc[u, here, TILE:] - deltas[u])).astype(BF)
                block = jnp.concatenate([ds, p.astype(BF)], axis=1)
                dsp[u, here, :] = block
                got = jnp.dot(block, both, preferred_element_type=F32)
                if j < count:
                    spot = rows_of((32 + qb - OFFSETS[j]) * TILE, TILE)
                    gkv[spot, :] += got
                else:
                    gsum[...] += got
            both_out = jnp.dot(gt[u], dsp[u], preferred_element_type=F32)
            cg[rows, 0:TILE] = jnp.transpose(both_out[:TILE, :TILE] * SCALE).astype(BF)
            context = jnp.transpose(both_out[TILE:, TILE:])
            cg[rows, TILE:] = jnp.where(key_slot < lens[0, 16 * group + qb], context, 0.0).astype(BF)
        return carry

    def owner(i):
        to_z = 2 * c + lax.div(i, 2)
        core = lax.rem(i, 2)
        mine = jnp.logical_and(z == to_z, c == core)
        return device(y, x, to_z, core), mine

    def give_back(src, landing, send, recv, i):
        to, mine = owner(i)
        rows = rows_of(i * 512, 512)

        @pl.when(mine)
        def _():
            landing[z] = src[rows, :]

        @pl.when(jnp.logical_not(mine))
        def _():
            remote(src.at[rows], landing.at[z], send.at[i], recv.at[z], to).start()

    def settle(src, landing, send, recv):
        for i in range(4):
            to, mine = owner(i)

            @pl.when(jnp.logical_not(mine))
            def _():
                remote(src.at[pl.ds(i * 512, 512)], landing.at[z], send.at[i], recv.at[z], to).wait_send()

    def returned(src, landing, send, recv):
        for h in range(HEADS):
            mine = jnp.logical_and(z == h, at_home)

            @pl.when(jnp.logical_not(mine))
            def _():
                remote(src.at[pl.ds(0, 512)], landing.at[h], send.at[0], recv.at[h], other).wait_recv()

    def crossing(i):
        rows = rows_of(i * 512, 512)
        return remote(sx.at[rows], rx.at[rows], s_bx.at[i], r_bx.at[i], other)

    def cross(i):
        sx[rows_of(i * 512, 512), :] = gkv[rows_of(2048 + i * 512, 512), :].astype(BF)
        crossing(i).start()

    def halo_back(i):
        rows = rows_of(i * 512, 512)
        return remote(sh.at[rows], rh.at[rows], s_bh.at[i], r_bh.at[i], behind)

    def chunk(i, carry):
        lax.fori_loop(i * (4 // UNROLL), (i + 1) * (4 // UNROLL), bar, 0)

        @pl.when(c == 0)
        def _():
            rows = rows_of(i * 512, 512)
            sh[rows, :] = gkv[rows, :].astype(BF)
            halo_back(i).start()

        @pl.when(i >= 2)
        def _():
            cross(i - 2)
            cross(i)

        give_back(cg, ret_cg, s_cg, r_cg, i)
        return carry

    lax.fori_loop(0, 4, chunk, 0)
    gss[...] = gsum[...].astype(BF).reshape(8, 16, 256)
    gsr[group] = gss[group]
    back_copies = []
    for d, cc in pairs_of:
        n = d * 2 + cc
        to_x, core = turn(x, d), lax.rem(c + cc, 2)
        copy = remote(
            gss.at[to_x * 2 + core], gsr.at[group], s_gs.at[n], r_gs.at[n], device(y, to_x, z, core)
        )
        copy.start()
        back_copies.append(copy)
    turns = (0, 2, 1, 3)
    for i in turns:
        crossing(i).wait_recv()

        @pl.when(c == 1)
        def _():
            rows = pl.ds(i * 512, 512)
            sh[rows, :] = (gkv[rows, :] + rx[rows, :].astype(F32)).astype(BF)
            halo_back(i).start()

    def flatten(src, lane, n):
        for h in range(HEADS):
            flat[n, :, h * TILE : (h + 1) * TILE] = src[h, :, lane : lane + TILE]

    where = {"y": y, "x": x, "z": z}
    levels = ((w0, got1, 256), (w1, got2, 64))
    pending = [None] * 4
    started = []
    last = []

    def along(axis, d):
        at = dict(where)
        at[axis] = turn(where[axis], d)
        return device(at["y"], at["x"], at["z"], c)

    def core_half(m):
        return remote(wg.at[m, 1 - c], got0.at[m], s0.at[0, m], r0.at[0, m], other)

    def send_level(m, level):
        src, got, size = levels[level]
        copies = []
        axis = ORDERS[m][level]
        for d in (1, 2, 3):
            piece = pl.ds(pl.multiple_of(turn(where[axis], d) * size, 16), size)
            copy = remote(
                src.at[m, piece], got.at[m, d - 1], s1.at[level, m, d - 1], r1.at[level, m, d - 1], along(axis, d)
            )
            copy.start()
            copies.append(copy)
        pending[m] = copies
        started.extend(copies)

    def place_rows(m, level):
        start = where[ORDERS[m][0]] * 256
        if level == 1:
            start = start + where[ORDERS[m][1]] * 64
        return pl.ds(pl.multiple_of(start, 16), levels[level][2])

    half = pl.ds(pl.multiple_of(c * 256, 256), 256)

    def give(m, level):
        block = out.at[m, place_rows(m, level), half]
        copies = []
        for d in (1, 2, 3):
            copy = remote(
                block, block, s2.at[level, m, d - 1], r2.at[level, m, d - 1], along(ORDERS[m][level], d)
            )
            copy.start()
            copies.append(copy)
        pending[m] = copies
        started.extend(copies)

    def settled(m):
        for copy in pending[m]:
            copy.wait_recv()

    def begin(m):
        core_half(m).wait_recv()

        def add(i, carry):
            rows = rows_of(i * 256, 256)
            w0[m, rows, :] = (wg[m, c, rows, :].astype(F32) + got0[m, rows, :].astype(F32)).astype(BF)
            return carry

        lax.fori_loop(0, 4, add, 0)
        send_level(m, 0)

    def advance(m, level):
        settled(m)
        if level == 2:
            total = got3[m, 0].astype(F32)
            for n in range(1, 4):
                total = total + got3[m, n].astype(F32)
            out[m, place_rows(m, 1), half] = total.astype(BF)
            give(m, 1)
            return
        src, got, size = levels[level]
        mine = pl.ds(pl.multiple_of(where[ORDERS[m][level]] * size, 16), size)
        total = src[m, mine, :].astype(F32)
        for n in range(3):
            total = total + got[m, n].astype(F32)
        if level == 0:
            w1[m] = total.astype(BF)
            send_level(m, 1)
        else:
            axis = ORDERS[m][2]
            got3[m, where[axis]] = total.astype(BF)
            block = got3.at[m, where[axis]]
            copies = []
            for d in (1, 2, 3):
                copy = remote(block, block, s1.at[2, m, d - 1], r1.at[2, m, d - 1], along(axis, d))
                copy.start()
                copies.append(copy)
            pending[m] = copies
            started.extend(copies)

    def finish(m):
        settled(m)
        copy = remote(out.at[m, :, half], out.at[m, :, half], s0.at[1, m], r0.at[1, m], other)
        copy.start()
        last.append(copy)

    def weight_grad(n, m):
        def part(i, carry):
            cols = rows_of(i * 256, 256)
            got = lax.dot_general(tok[:, cols], flat[n], TN, preferred_element_type=F32).astype(BF)
            wg[m, 0, cols, :] = got[:, :256]
            wg[m, 1, cols, :] = got[:, 256:]
            return carry

        lax.fori_loop(0, 4, part, 0)
        core_half(m).start()

    returned(cg, ret_cg, s_cg, r_cg)
    flatten(ret_cg, 0, 0)
    weight_grad(0, 0)
    flatten(ret_cg, TILE, 3)

    def out_grad(i, carry):
        cols = rows_of(i * 256, 256)
        got = lax.dot_general(flat[3], cot[:, cols], TN, preferred_element_type=F32).astype(BF)
        wg[3, lax.rem(i, 2), rows_of(lax.div(i, 2) * 512, 512), :] = got
        return carry

    lax.fori_loop(0, 4, out_grad, 0)
    core_half(3).start()
    begin(0)
    begin(3)

    for copy in back_copies:
        copy.wait()
    coarse = gsr[0].astype(F32)
    for n in range(1, 8):
        coarse = coarse + gsr[n].astype(F32)
    lane = lax.broadcasted_iota(jnp.int32, (1, 256), 1)
    factor = jnp.where(lane < TILE, SCALE, 1.0)
    for i in turns:
        halo_back(i).wait_recv()
        for b in range(4 * i, 4 * i + 4):
            rows = pl.ds(b * TILE, TILE)
            length = lens[0, group * 16 + b]
            live = lax.broadcasted_iota(jnp.int32, (TILE, 256), 0) < length
            share = coarse[b : b + 1, :] * (1.0 / jnp.full((1, 256), length, jnp.int32).astype(F32))
            extra = jnp.where(c == 0, rx[rows, :].astype(F32), 0.0)
            total = gkv[pl.ds(OWN + b * TILE, TILE), :] + rh[rows, :].astype(F32) + extra
            own[rows, :] = ((total + jnp.where(live, share, 0.0)) * factor).astype(BF)
        give_back(own, ret_kv, s_bkv, r_bkv, i)

    def mix(i, carry):
        rows = rows_of(i * 256, 256)
        mixed[rows, :] = jnp.dot(flat[3, rows, :], wo[...], preferred_element_type=F32).astype(BF)
        return carry

    lax.fori_loop(0, 2, mix, 0)
    for level in range(2):
        advance(0, level)
        advance(3, level)
    returned(own, ret_kv, s_bkv, r_bkv)
    flatten(ret_kv, 0, 1)
    weight_grad(1, 1)
    flatten(ret_kv, TILE, 2)
    weight_grad(2, 2)
    begin(1)
    begin(2)
    advance(0, 2)
    advance(3, 2)

    def back(i, carry):
        rows = rows_of(i * 256, 256)
        total = lax.dot_general(flat[0, rows, :], wq[...], NT, preferred_element_type=F32)
        total = total + lax.dot_general(flat[1, rows, :], wk[...], NT, preferred_element_type=F32)
        total = total + lax.dot_general(flat[2, rows, :], wv[...], NT, preferred_element_type=F32)
        gin[rows, :] = total.astype(BF)
        return carry

    lax.fori_loop(0, 2, back, 0)
    for m in (0, 3):
        settled(m)
        give(m, 0)
    for level in range(3):
        advance(1, level)
        advance(2, level)
    for m in (1, 2):
        settled(m)
        give(m, 0)
    for m in (0, 3, 1, 2):
        finish(m)
    for copy in last:
        copy.wait()
    for m in range(4):
        core_half(m).wait_send()
        crossing(m).wait_send()
        halo_back(m).wait_send()
    for copy in started:
        copy.wait_send()
    settle(cg, ret_cg, s_cg, r_cg)
    settle(own, ret_kv, s_bkv, r_bkv)


def hand_over(mixed, gin, a, b, c, low, high, mixed_out, gin_out, a_out, b_out, c_out, d_out):
    mixed_out[...] = mixed[...]
    gin_out[...] = gin[...]
    for src, dst in ((a, a_out), (b, b_out), (c, c_out)):
        dst[...] = src[0].astype(F32)
    d_out[:, :512] = low[0].astype(F32)
    d_out[:, 512:] = high[0].astype(F32)


ORDERS = ("yxz", "xzy", "zyx", "yzx")
UNROLL = 4

HB = pl.BlockSpec(memory_space=pl.ANY)
VM = pl.BlockSpec(memory_space=pltpu.VMEM)
SM = pl.BlockSpec(memory_space=pltpu.SMEM)
DMA = pltpu.SemaphoreType.DMA


def shape(*dims, kind=BF):
    return jax.ShapeDtypeStruct(dims, kind)


def local(tokens, lengths, w_query, w_key, w_value, w_out, cotangent):
    vm = pltpu.VMEM
    slabs = lambda n: [vm((2048, 256), BF)] * n
    heads = lambda n: [vm((4, 512, 256), BF)] * n
    mixed, gin, total = pl.pallas_call(
        whole_kernel,
        out_shape=(shape(512, 1024), shape(512, 1024), shape(4, 1024, 512)),
        in_specs=[SM] + [HB] * 6,
        out_specs=(VM, VM, VM),
        scratch_shapes=[vm((512, 1024), BF)] * 2
        + [vm((1024, 512), BF)] * 3
        + [vm((512, 1024), BF), vm((6144, 256), BF)]
        + slabs(1)
        + [vm((8, 16, 256), BF)]
        + heads(2)
        + [vm((16, 256), F32)]
        + [
            vm((256, 49 * TILE), BF),
            vm((UNROLL, 256, 10 * TILE), BF),
            vm((UNROLL, 256, 256), BF),
            vm((UNROLL, 256, 256), BF),
            vm((UNROLL, 10 * TILE, 256), F32),
            vm((UNROLL, 10 * TILE, 256), BF),
            vm((6144, 256), F32),
            vm((128, 256), F32),
        ]
        + slabs(5)
        + [vm((8, 16, 256), BF)] * 2
        + slabs(1)
        + heads(2)
        + [
            vm((4, 512, 512), BF),
            vm((4, 2, 1024, 256), BF),
            vm((4, 1024, 256), BF),
            vm((4, 1024, 256), BF),
            vm((4, 3, 256, 256), BF),
            vm((4, 256, 256), BF),
            vm((4, 3, 64, 256), BF),
            vm((4, 4, 64, 256), BF),
        ]
        + [DMA((6,))]
        + [DMA((4,))] * 8
        + [DMA((8,))] * 2
        + [DMA((4,))] * 8
        + [DMA((8,))] * 2
        + [DMA((2, 4))] * 2
        + [DMA((3, 4, 3))] * 2
        + [DMA((2, 4, 3))] * 2,
        compiler_params=pltpu.CompilerParams(
            collective_id=0, has_side_effects=True, vmem_limit_bytes=62 * MIB
        ),
        name="whole",
    )(lengths, tokens[0], w_key, w_value, w_query, cotangent[0], w_out)
    block = pl.BlockSpec
    mixed, gin, *weights = pl.pallas_call(
        hand_over,
        grid=(8,),
        out_shape=(shape(512, 1024), shape(512, 1024))
        + (shape(1024, 512, kind=F32),) * 3
        + (shape(512, 1024, kind=F32),),
        in_specs=[block((64, 1024), lambda i: (i, 0))] * 2
        + [block((1, 128, 512), lambda i, m=m: (m, i, 0)) for m in range(3)]
        + [block((1, 64, 512), lambda i, n=n: (3, n + i, 0)) for n in (0, 8)],
        out_specs=[block((64, 1024), lambda i: (i, 0))] * 2
        + [block((128, 512), lambda i: (i, 0))] * 3
        + [block((64, 1024), lambda i: (i, 0))],
        compiler_params=pltpu.CompilerParams(vmem_limit_bytes=62 * MIB),
        name="hand_over",
    )(mixed, gin, total, total, total, total, total)
    return (mixed[None], gin[None], *weights)


def solution(mesh):
    placed = (P("dp", "seq", None), P("dp", None), P(), P(), P(), P(), P("dp", "seq", None))
    return jax.shard_map(
        local,
        mesh=mesh,
        in_specs=placed,
        out_specs=(P("dp", "seq", None), P("dp", "seq", None), P(), P(), P(), P()),
        check_vma=False,
    )
```

```python
import functools
import math

import jax
import jax.numpy as jnp
from jax import lax
from jax.experimental import pallas as pl
from jax.experimental.pallas import tpu as pltpu
from jax.sharding import PartitionSpec as P

MESH = pl.DeviceIdType.MESH
BF = jnp.bfloat16
F32 = jnp.float32
HEADS = 4
TILE = 128
OFFSETS = (0, 1, 2, 4, 8, 12, 16, 24, 32)
SCALE = 1.0 / math.sqrt(128.0)
LOG2E = 1.4426950408889634
NEG = -1e30
NT = (((1,), (1,)), ((), ()))
TN = (((0,), (0,)), ((), ()))
OWN = 32 * TILE
MIB = 1024 * 1024


def place():
    s = lax.axis_index("seq")
    return lax.axis_index("dp"), lax.div(s, 8), lax.rem(lax.div(s, 2), 4), lax.rem(s, 2)


def device(y, x, z, c):
    return (y, (x * 4 + z) * 2 + c)


def turn(a, d):
    return lax.rem(a + d, 4)


def remote(src, dst, send, recv, to):
    return pltpu.make_async_remote_copy(
        src_ref=src, dst_ref=dst, send_sem=send, recv_sem=recv, device_id=to, device_id_type=MESH
    )


def all_partners(y, x, z, c):
    found = [device(y, x, z, 1 - c)]
    for d in (1, 2, 3):
        found.append(device(turn(y, d), x, z, c))
        for core in (0, 1):
            found.append(device(y, turn(x, d), z, core))
            found.append(device(y, x, turn(z, d), core))
    return found


def rows_of(start, count):
    return pl.ds(pl.multiple_of(start, TILE), count)


def whole_kernel(
    lens, tok_in, wk_in, wv_in, wq_in, cot_in, wo_in, mixed, gin, out,
    tok, tokt, cot, wq, wk, wv, wo,
    kv, qg, summ, kvs, qgs, sums,
    kvt, gt, pair, pairt, sc, dsp, gkv, gsum, cg,
    rx, rh, gss, gsr, ret_kv, ret_cg, flat,
    wg, got0, w0, got1, w1, got2, got3,
    s_in, s_kv, r_kv, s_qg, r_qg, s_h, r_h, s_x, r_x, s_s, r_s,
    s_bkv, r_bkv, s_cg, r_cg, s_bh, r_bh, s_bx, r_bx, s_gs, r_gs,
    s0, r0, s1, r1, s2, r2,
):
    y, x, z, c = place()
    loads = []
    for n, (a, b) in enumerate(
        ((tok_in, tok), (wk_in, wk), (wv_in, wv), (wq_in, wq), (cot_in, cot), (wo_in, wo))
    ):
        copy = pltpu.make_async_copy(a, b, s_in.at[n])
        copy.start()
        loads.append(copy)
    partners = all_partners(y, x, z, c)
    barrier = pltpu.get_barrier_semaphore()
    for to in partners:
        pl.semaphore_signal(barrier, inc=1, device_id=to, device_id_type=MESH)
    other = device(y, x, z, 1 - c)
    home = lax.div(z, 2)
    at_home = c == home
    slot = lax.rem(z, 2) * 2 + c
    group = 2 * x + c

    def project(src, w, dst, lane):
        def half(i, carry):
            rows = rows_of(i * 256, 256)
            got = jnp.dot(src[rows, :], w[...], preferred_element_type=F32)
            for h in range(HEADS):
                dst[h, rows, lane : lane + TILE] = got[:, h * TILE : (h + 1) * TILE].astype(BF)
            return carry

        lax.fori_loop(0, 2, half, 0)

    def exchange(staged, landing, base, send, recv):
        spot = rows_of(base + slot * 512, 512)
        copies = []
        near = remote(staged.at[z], landing.at[spot], send.at[0], recv.at[slot], other)

        @pl.when(at_home)
        def _():
            landing[spot, :] = staged[z]

        @pl.when(jnp.logical_not(at_home))
        def _():
            near.start()

        for d in (1, 3, 2):
            h = turn(z, d)
            copy = remote(staged.at[h], landing.at[spot], send.at[d], recv.at[slot], device(y, x, h, home))
            if d != 2:
                copy.start()
            copies.append(copy)
        return copies, near

    def settle_out(copies, near):
        for copy in copies:
            copy.wait_send()

        @pl.when(jnp.logical_not(at_home))
        def _():
            near.wait_send()

    def arrived(staged, landing, base, send, recv, i):
        mine = jnp.logical_and(z == 2 * c + lax.div(i, 2), c == lax.rem(i, 2))

        @pl.when(jnp.logical_not(mine))
        def _():
            remote(
                staged.at[0], landing.at[rows_of(base + i * 512, 512)], send.at[0], recv.at[i], other
            ).wait_recv()

    for n in range(3):
        loads[n].wait()
    project(tok, wk, kvs, 0)
    project(tok, wv, kvs, TILE)
    pl.semaphore_wait(barrier, len(partners))
    kv_sent = exchange(kvs, kv, OWN, s_kv, r_kv)
    for n in range(3, 6):
        loads[n].wait()
    project(tok, wq, qgs, 0)
    first_own = ((x * 4 + z) * 2 + c) * 4

    def grads(i, carry):
        rows = rows_of(i * TILE, TILE)
        got = lax.dot_general(cot[rows, :], wo[...], NT, preferred_element_type=F32)
        live = lax.broadcasted_iota(jnp.int32, (TILE, 512), 0) < lens[0, first_own + i]
        got = jnp.where(live, got, 0.0).astype(BF)
        for h in range(HEADS):
            qgs[h, rows, TILE : 2 * TILE] = got[:, h * TILE : (h + 1) * TILE]
        return carry

    lax.fori_loop(0, 4, grads, 0)
    kv_sent[0][2].start()

    ahead = device(y, turn(x, 1), z, c)
    behind = device(y, turn(x, 3), z, c)

    def halo_copy(i):
        return remote(
            kv.at[rows_of(OWN + i * 512, 512)], kv.at[rows_of(i * 512, 512)], s_h.at[i], r_h.at[i], ahead
        )

    def across_copy(start, i):
        return remote(
            kv.at[rows_of(start + i * 512, 512)],
            kv.at[rows_of(2048 + i * 512, 512)],
            s_x.at[i],
            r_x.at[i],
            other,
        )

    nearest = lax.rem(z + jnp.where(at_home, 0, 1), 2) * 2
    order = [lax.rem(nearest + k, 4) for k in range(4)]
    for i in order:
        arrived(kvs, kv, OWN, s_kv, r_kv, i)
        halo_copy(i).start()

        @pl.when(c == 0)
        def _():
            across_copy(OWN, i).start()

    qg_sent = exchange(qgs, qg, 0, s_qg, r_qg)
    qg_sent[0][2].start()

    def summary(i, carry):
        rows = rows_of(OWN + i * TILE, TILE)
        length = lens[0, group * 16 + i]
        live = lax.broadcasted_iota(jnp.int32, (TILE, 256), 0) < length
        total = jnp.sum(jnp.where(live, kv[rows, :].astype(F32), 0.0), axis=0, keepdims=True)
        sums[pl.ds(i, 1), :] = total / jnp.full((1, 256), length, jnp.int32).astype(F32)
        return carry

    lax.fori_loop(0, 16, summary, 0)
    summ[group] = sums[...].astype(BF)
    sum_copies = []
    pairs_of = [(d, cc) for d in range(4) for cc in (0, 1) if (d, cc) != (0, 0)]
    for d, cc in pairs_of:
        n = d * 2 + cc
        core = lax.rem(c + cc, 2)
        copy = remote(summ.at[group], summ.at[group], s_s.at[n], r_s.at[n], device(y, turn(x, d), z, core))
        copy.start()
        sum_copies.append(copy)

    def prepare(b, carry):
        rows = rows_of(b * TILE, TILE)
        kvt[:, rows] = jnp.transpose(kv[rows, :])
        return carry

    def clear(b, carry):
        gkv[rows_of(b * TILE, TILE), :] = jnp.zeros((TILE, 256), F32)
        return carry

    lax.fori_loop(0, 48, clear, 0)
    gsum[...] = jnp.zeros_like(gsum)
    for u in range(UNROLL):
        pair[u] = jnp.zeros((256, 256), BF)
        pairt[u] = jnp.zeros((256, 256), BF)
    lax.fori_loop(32, 48, prepare, 0)

    def turned(i, carry):
        cols = rows_of(i * TILE, TILE)
        tokt[cols, :] = jnp.transpose(tok[:, cols])
        return carry

    lax.fori_loop(0, 8, turned, 0)
    for i in order:
        halo_copy(i).wait_recv()

        @pl.when(c == 1)
        def _():
            across_copy(0, i).start()

    lax.fori_loop(0, 16, prepare, 0)
    for i in range(4):
        across_copy(0, i).wait()
        halo_copy(i).wait_send()
        arrived(qgs, qg, 0, s_qg, r_qg, i)
    lax.fori_loop(16, 32, prepare, 0)
    for copy in sum_copies:
        copy.wait()
    kvt[:, 48 * TILE : 49 * TILE] = jnp.transpose(summ[...].reshape(TILE, 256))
    settle_out(*kv_sent)
    settle_out(*qg_sent)

    key_slot = lax.broadcasted_iota(jnp.int32, (TILE, TILE), 0)
    query_slot = lax.broadcasted_iota(jnp.int32, (TILE, TILE), 1)
    count = len(OFFSETS)

    def bar(it, carry):
        ids = [it * UNROLL + u for u in range(UNROLL)]
        tops, scales, deltas = [], [], []
        for u, qb in enumerate(ids):
            rows = rows_of(qb * TILE, TILE)
            pair[u, 0:TILE, 0:TILE] = qg[rows, 0:TILE]
            pair[u, TILE:, TILE:] = qg[rows, TILE:]
            pairt[u, 0:TILE, 0:TILE] = jnp.transpose(qg[rows, 0:TILE])
            pairt[u, TILE:, TILE:] = jnp.transpose(qg[rows, TILE:])
            both = pairt[u]
            this = 16 * group + qb
            top = None
            for j in range(count + 1):
                here = slice(j * TILE, (j + 1) * TILE)
                if j < count:
                    spot = rows_of((32 + qb - OFFSETS[j]) * TILE, TILE)
                    bar_id = this - OFFSETS[j]
                    length = jnp.where(bar_id >= 0, lens[0, jnp.maximum(bar_id, 0)], 0)
                    source = kv[spot, :]
                    gt[u, :, here] = kvt[:, spot]
                    ok = key_slot < length
                    if j == 0:
                        ok = jnp.logical_and(ok, key_slot <= query_slot)
                else:
                    source = summ[...].reshape(TILE, 256)
                    gt[u, :, here] = kvt[:, 48 * TILE : 49 * TILE]
                    distance = this - key_slot
                    ok = distance >= 1
                    for o in OFFSETS[1:]:
                        ok = jnp.logical_and(ok, distance != o)
                got = jnp.dot(source, both, preferred_element_type=F32)
                score = jnp.where(ok, got[:, :TILE] * (SCALE * LOG2E), NEG)
                sc[u, here, :TILE] = score
                sc[u, here, TILE:] = got[:, TILE:]
                high = jnp.max(score, axis=0, keepdims=True)
                top = high if top is None else jnp.maximum(top, high)
            tops.append(top)
        for u in range(UNROLL):
            total = jnp.zeros((1, TILE), F32)
            weighted = jnp.zeros((1, TILE), F32)
            for j in range(count + 1):
                here = slice(j * TILE, (j + 1) * TILE)
                e = jnp.exp2(sc[u, here, :TILE] - tops[u])
                sc[u, here, :TILE] = e
                total = total + jnp.sum(e, axis=0, keepdims=True)
                weighted = weighted + jnp.sum(e * sc[u, here, TILE:], axis=0, keepdims=True)
            scales.append(1.0 / total)
            deltas.append(weighted * scales[u])
        for u, qb in enumerate(ids):
            rows = rows_of(qb * TILE, TILE)
            both = pair[u]
            for j in range(count + 1):
                here = slice(j * TILE, (j + 1) * TILE)
                p = sc[u, here, :TILE] * scales[u]
                ds = (p * (sc[u, here, TILE:] - deltas[u])).astype(BF)
                block = jnp.concatenate([ds, p.astype(BF)], axis=1)
                dsp[u, here, :] = block
                got = jnp.dot(block, both, preferred_element_type=F32)
                if j < count:
                    spot = rows_of((32 + qb - OFFSETS[j]) * TILE, TILE)
                    gkv[spot, :] += got
                else:
                    gsum[...] += got
            both_out = jnp.dot(gt[u], dsp[u], preferred_element_type=F32)
            cg[rows, 0:TILE] = jnp.transpose(both_out[:TILE, :TILE] * SCALE).astype(BF)
            context = jnp.transpose(both_out[TILE:, TILE:])
            cg[rows, TILE:] = jnp.where(key_slot < lens[0, 16 * group + qb], context, 0.0).astype(BF)
        return carry

    def owner(i):
        to_z = 2 * c + lax.div(i, 2)
        core = lax.rem(i, 2)
        mine = jnp.logical_and(z == to_z, c == core)
        return device(y, x, to_z, core), mine

    def give_back(src, landing, send, recv, i):
        to, mine = owner(i)
        rows = rows_of(i * 512, 512)

        @pl.when(mine)
        def _():
            landing[z] = src[rows, :]

        @pl.when(jnp.logical_not(mine))
        def _():
            remote(src.at[rows], landing.at[z], send.at[i], recv.at[z], to).start()

    def settle(src, landing, send, recv):
        for i in range(4):
            to, mine = owner(i)

            @pl.when(jnp.logical_not(mine))
            def _():
                remote(src.at[pl.ds(i * 512, 512)], landing.at[z], send.at[i], recv.at[z], to).wait_send()

    def returned(src, landing, send, recv):
        for h in range(HEADS):
            mine = jnp.logical_and(z == h, at_home)

            @pl.when(jnp.logical_not(mine))
            def _():
                remote(src.at[pl.ds(0, 512)], landing.at[h], send.at[0], recv.at[h], other).wait_recv()

    def crossing(i):
        rows = rows_of(i * 512, 512)
        return remote(kvs.at[i], rx.at[rows], s_bx.at[i], r_bx.at[i], other)

    def cross(i):
        kvs[i] = gkv[rows_of(2048 + i * 512, 512), :].astype(BF)
        crossing(i).start()

    def halo_back(i):
        rows = rows_of(i * 512, 512)
        return remote(qgs.at[i], rh.at[rows], s_bh.at[i], r_bh.at[i], behind)

    def chunk(i, carry):
        lax.fori_loop(i * (4 // UNROLL), (i + 1) * (4 // UNROLL), bar, 0)

        @pl.when(c == 0)
        def _():
            rows = rows_of(i * 512, 512)
            qgs[i] = gkv[rows, :].astype(BF)
            halo_back(i).start()

        @pl.when(i >= 2)
        def _():
            cross(i - 2)
            cross(i)

        give_back(cg, ret_cg, s_cg, r_cg, i)
        return carry

    lax.fori_loop(0, 4, chunk, 0)
    gss[...] = gsum[...].astype(BF).reshape(8, 16, 256)
    gsr[group] = gss[group]
    back_copies = []
    for d, cc in pairs_of:
        n = d * 2 + cc
        to_x, core = turn(x, d), lax.rem(c + cc, 2)
        copy = remote(
            gss.at[to_x * 2 + core], gsr.at[group], s_gs.at[n], r_gs.at[n], device(y, to_x, z, core)
        )
        copy.start()
        back_copies.append(copy)
    turns = (0, 2, 1, 3)
    for i in turns:
        crossing(i).wait_recv()

        @pl.when(c == 1)
        def _():
            rows = pl.ds(i * 512, 512)
            qgs[i] = (gkv[rows, :] + rx[rows, :].astype(F32)).astype(BF)
            halo_back(i).start()

    def flatten(src, lane, n):
        for h in range(HEADS):
            flat[n, :, h * TILE : (h + 1) * TILE] = src[h, :, lane : lane + TILE]

    where = {"y": y, "x": x, "z": z}
    levels = ((w0, got1, 256), (w1, got2, 64))
    pending = [None] * 4
    started = []
    last = []

    def along(axis, d):
        at = dict(where)
        at[axis] = turn(where[axis], d)
        return device(at["y"], at["x"], at["z"], c)

    def core_half(m):
        return remote(wg.at[m, 1 - c], got0.at[m], s0.at[0, m], r0.at[0, m], other)

    def send_level(m, level):
        src, got, size = levels[level]
        copies = []
        axis = ORDERS[m][level]
        for d in (1, 2, 3):
            piece = pl.ds(pl.multiple_of(turn(where[axis], d) * size, 16), size)
            copy = remote(
                src.at[m, piece], got.at[m, d - 1], s1.at[level, m, d - 1], r1.at[level, m, d - 1], along(axis, d)
            )
            copy.start()
            copies.append(copy)
        pending[m] = copies
        started.extend(copies)

    def place_rows(m, level):
        start = where[ORDERS[m][0]] * 256
        if level == 1:
            start = start + where[ORDERS[m][1]] * 64
        return pl.ds(pl.multiple_of(start, 16), levels[level][2])

    half = pl.ds(pl.multiple_of(c * 256, 256), 256)

    def give(m, level):
        block = out.at[m, place_rows(m, level), half]
        copies = []
        for d in (1, 2, 3):
            copy = remote(
                block, block, s2.at[level, m, d - 1], r2.at[level, m, d - 1], along(ORDERS[m][level], d)
            )
            copy.start()
            copies.append(copy)
        pending[m] = copies
        started.extend(copies)

    def settled(m):
        for copy in pending[m]:
            copy.wait_recv()

    def begin(m):
        core_half(m).wait_recv()

        def add(i, carry):
            rows = rows_of(i * 256, 256)
            w0[m, rows, :] = (wg[m, c, rows, :].astype(F32) + got0[m, rows, :].astype(F32)).astype(BF)
            return carry

        lax.fori_loop(0, 4, add, 0)
        send_level(m, 0)

    def advance(m, level):
        settled(m)
        if level == 2:
            total = got3[m, 0].astype(F32)
            for n in range(1, 4):
                total = total + got3[m, n].astype(F32)
            out[m, place_rows(m, 1), half] = total.astype(BF)
            give(m, 1)
            return
        src, got, size = levels[level]
        mine = pl.ds(pl.multiple_of(where[ORDERS[m][level]] * size, 16), size)
        total = src[m, mine, :].astype(F32)
        for n in range(3):
            total = total + got[m, n].astype(F32)
        if level == 0:
            w1[m] = total.astype(BF)
            send_level(m, 1)
        else:
            axis = ORDERS[m][2]
            got3[m, where[axis]] = total.astype(BF)
            block = got3.at[m, where[axis]]
            copies = []
            for d in (1, 2, 3):
                copy = remote(block, block, s1.at[2, m, d - 1], r1.at[2, m, d - 1], along(axis, d))
                copy.start()
                copies.append(copy)
            pending[m] = copies
            started.extend(copies)

    def finish(m):
        settled(m)
        copy = remote(out.at[m, :, half], out.at[m, :, half], s0.at[1, m], r0.at[1, m], other)
        copy.start()
        last.append(copy)

    def weight_grad(n, m):
        def part(i, carry):
            cols = rows_of(i * 256, 256)
            got = jnp.dot(tokt[cols, :], flat[n], preferred_element_type=F32).astype(BF)
            wg[m, 0, cols, :] = got[:, :256]
            wg[m, 1, cols, :] = got[:, 256:]
            return carry

        lax.fori_loop(0, 4, part, 0)
        core_half(m).start()

    returned(cg, ret_cg, s_cg, r_cg)
    flatten(ret_cg, 0, 0)
    weight_grad(0, 0)
    flatten(ret_cg, TILE, 3)

    def out_grad(i, carry):
        cols = rows_of(i * 256, 256)
        got = lax.dot_general(flat[3], cot[:, cols], TN, preferred_element_type=F32).astype(BF)
        wg[3, lax.rem(i, 2), rows_of(lax.div(i, 2) * 512, 512), :] = got
        return carry

    lax.fori_loop(0, 4, out_grad, 0)
    core_half(3).start()
    begin(0)
    begin(3)

    for copy in back_copies:
        copy.wait()
    coarse = gsr[0].astype(F32)
    for n in range(1, 8):
        coarse = coarse + gsr[n].astype(F32)
    lane = lax.broadcasted_iota(jnp.int32, (1, 256), 1)
    factor = jnp.where(lane < TILE, SCALE, 1.0)
    for i in turns:
        halo_back(i).wait_recv()
        for b in range(4 * i, 4 * i + 4):
            rows = pl.ds(b * TILE, TILE)
            length = lens[0, group * 16 + b]
            live = lax.broadcasted_iota(jnp.int32, (TILE, 256), 0) < length
            share = coarse[b : b + 1, :] * (1.0 / jnp.full((1, 256), length, jnp.int32).astype(F32))
            extra = jnp.where(c == 0, rx[rows, :].astype(F32), 0.0)
            total = gkv[pl.ds(OWN + b * TILE, TILE), :] + rh[rows, :].astype(F32) + extra
            qg[rows, :] = ((total + jnp.where(live, share, 0.0)) * factor).astype(BF)
        give_back(qg, ret_kv, s_bkv, r_bkv, i)

    def mix(i, carry):
        rows = rows_of(i * 256, 256)
        mixed[rows, :] = jnp.dot(flat[3, rows, :], wo[...], preferred_element_type=F32).astype(BF)
        return carry

    lax.fori_loop(0, 2, mix, 0)
    advance(0, 0)
    advance(3, 0)
    returned(qg, ret_kv, s_bkv, r_bkv)
    flatten(ret_kv, 0, 1)
    weight_grad(1, 1)
    flatten(ret_kv, TILE, 2)
    weight_grad(2, 2)
    begin(1)
    begin(2)
    advance(0, 1)
    advance(3, 1)

    def back(i, carry):
        rows = rows_of(i * 256, 256)
        total = lax.dot_general(flat[0, rows, :], wq[...], NT, preferred_element_type=F32)
        total = total + lax.dot_general(flat[1, rows, :], wk[...], NT, preferred_element_type=F32)
        total = total + lax.dot_general(flat[2, rows, :], wv[...], NT, preferred_element_type=F32)
        gin[rows, :] = total.astype(BF)
        return carry

    lax.fori_loop(0, 2, back, 0)
    advance(0, 2)
    advance(3, 2)
    advance(1, 0)
    advance(2, 0)
    for m in (0, 3):
        settled(m)
        give(m, 0)
    for level in (1, 2):
        advance(1, level)
        advance(2, level)
    for m in (1, 2):
        settled(m)
        give(m, 0)
    for m in (0, 3, 1, 2):
        finish(m)
    for copy in last:
        copy.wait()
    for m in range(4):
        core_half(m).wait_send()
        crossing(m).wait_send()
        halo_back(m).wait_send()
    for copy in started:
        copy.wait_send()
    settle(cg, ret_cg, s_cg, r_cg)
    settle(qg, ret_kv, s_bkv, r_bkv)


def hand_over(mixed, gin, total, *refs):
    mixed_out, gin_out, outs = refs[0], refs[1], refs[2:6]
    narrow, wide, s_in, s_out, s_pass = refs[6:]
    passed = [
        pltpu.make_async_copy(mixed, mixed_out, s_pass.at[0]),
        pltpu.make_async_copy(gin, gin_out, s_pass.at[1]),
    ]
    loads, stores = [], []
    for n in range(8):
        piece = pl.ds((n % 2) * 512, 512)
        loads.append(pltpu.make_async_copy(total.at[n // 2, piece], narrow.at[n], s_in.at[n]))
    for copy in loads + passed:
        copy.start()
    for n in range(8):
        loads[n].wait()
        wide[n] = narrow[n].astype(F32)
        piece = pl.ds((n % 2) * 512, 512)
        to = outs[3].at[:, piece] if n >= 6 else outs[n // 2].at[piece]
        copy = pltpu.make_async_copy(wide.at[n], to, s_out.at[n])
        copy.start()
        stores.append(copy)
    for copy in stores + passed:
        copy.wait()


ORDERS = ("yxz", "xzy", "zyx", "yzx")
UNROLL = 4

HB = pl.BlockSpec(memory_space=pl.ANY)
VM = pl.BlockSpec(memory_space=pltpu.VMEM)
SM = pl.BlockSpec(memory_space=pltpu.SMEM)
DMA = pltpu.SemaphoreType.DMA


def shape(*dims, kind=BF):
    return jax.ShapeDtypeStruct(dims, kind)


def local(tokens, lengths, w_query, w_key, w_value, w_out, cotangent):
    vm = pltpu.VMEM
    slabs = lambda n: [vm((2048, 256), BF)] * n
    heads = lambda n: [vm((4, 512, 256), BF)] * n
    mixed, gin, total = pl.pallas_call(
        whole_kernel,
        out_shape=(shape(512, 1024), shape(512, 1024), shape(4, 1024, 512)),
        in_specs=[SM] + [HB] * 6,
        out_specs=(VM, VM, VM),
        scratch_shapes=[vm((512, 1024), BF), vm((1024, 512), BF), vm((512, 1024), BF)]
        + [vm((1024, 512), BF)] * 3
        + [vm((512, 1024), BF), vm((6144, 256), BF)]
        + slabs(1)
        + [vm((8, 16, 256), BF)]
        + heads(2)
        + [vm((16, 256), F32)]
        + [
            vm((256, 49 * TILE), BF),
            vm((UNROLL, 256, 10 * TILE), BF),
            vm((UNROLL, 256, 256), BF),
            vm((UNROLL, 256, 256), BF),
            vm((UNROLL, 10 * TILE, 256), F32),
            vm((UNROLL, 10 * TILE, 256), BF),
            vm((6144, 256), F32),
            vm((128, 256), F32),
        ]
        + slabs(3)
        + [vm((8, 16, 256), BF)] * 2
        + heads(2)
        + [
            vm((4, 512, 512), BF),
            vm((4, 2, 1024, 256), BF),
            vm((4, 1024, 256), BF),
            vm((4, 1024, 256), BF),
            vm((4, 3, 256, 256), BF),
            vm((4, 256, 256), BF),
            vm((4, 3, 64, 256), BF),
            vm((4, 4, 64, 256), BF),
        ]
        + [DMA((6,))]
        + [DMA((4,))] * 8
        + [DMA((8,))] * 2
        + [DMA((4,))] * 8
        + [DMA((8,))] * 2
        + [DMA((2, 4))] * 2
        + [DMA((3, 4, 3))] * 2
        + [DMA((2, 4, 3))] * 2,
        compiler_params=pltpu.CompilerParams(
            collective_id=0, has_side_effects=True, vmem_limit_bytes=62 * MIB
        ),
        name="whole",
    )(lengths, tokens[0], w_key, w_value, w_query, cotangent[0], w_out)
    mixed, gin, *weights = pl.pallas_call(
        hand_over,
        out_shape=(shape(512, 1024), shape(512, 1024))
        + (shape(1024, 512, kind=F32),) * 3
        + (shape(512, 1024, kind=F32),),
        in_specs=[HB] * 3,
        out_specs=(HB,) * 6,
        scratch_shapes=[vm((8, 512, 512), BF), vm((8, 512, 512), F32), DMA((8,)), DMA((8,)), DMA((2,))],
        compiler_params=pltpu.CompilerParams(vmem_limit_bytes=62 * MIB),
        name="hand_over",
    )(mixed, gin, total)
    return (mixed[None], gin[None], *weights)


def solution(mesh):
    placed = (P("dp", "seq", None), P("dp", None), P(), P(), P(), P(), P("dp", "seq", None))
    return jax.shard_map(
        local,
        mesh=mesh,
        in_specs=placed,
        out_specs=(P("dp", "seq", None), P("dp", "seq", None), P(), P(), P(), P()),
        check_vma=False,
    )
```

```python
import functools
import math

import jax
import jax.numpy as jnp
from jax import lax
from jax.experimental import pallas as pl
from jax.experimental.pallas import tpu as pltpu
from jax.sharding import PartitionSpec as P

MESH = pl.DeviceIdType.MESH
BF = jnp.bfloat16
F32 = jnp.float32
HEADS = 4
TILE = 128
OFFSETS = (0, 1, 2, 4, 8, 12, 16, 24, 32)
SCALE = 1.0 / math.sqrt(128.0)
LOG2E = 1.4426950408889634
NEG = -1e30
NT = (((1,), (1,)), ((), ()))
TN = (((0,), (0,)), ((), ()))
OWN = 32 * TILE
MIB = 1024 * 1024


def place():
    s = lax.axis_index("seq")
    return lax.axis_index("dp"), lax.div(s, 8), lax.rem(lax.div(s, 2), 4), lax.rem(s, 2)


def device(y, x, z, c):
    return (y, (x * 4 + z) * 2 + c)


def turn(a, d):
    return lax.rem(a + d, 4)


def remote(src, dst, send, recv, to):
    return pltpu.make_async_remote_copy(
        src_ref=src, dst_ref=dst, send_sem=send, recv_sem=recv, device_id=to, device_id_type=MESH
    )


def all_partners(y, x, z, c):
    found = [device(y, x, z, 1 - c)]
    for d in (1, 2, 3):
        found.append(device(turn(y, d), x, z, c))
        for core in (0, 1):
            found.append(device(y, turn(x, d), z, core))
            found.append(device(y, x, turn(z, d), core))
    return found


def rows_of(start, count):
    return pl.ds(pl.multiple_of(start, TILE), count)


def whole_kernel(
    lens, tok_in, wk_in, wv_in, wq_in, cot_in, wo_in, mixed, gin, out,
    tok, tokt, cot, wq, wk, wv, wo,
    kv, qg, summ, kvs, qgs, sums,
    kvt, gt, pair, pairt, sc, dsp, gkv, gsum, cg,
    rx, rh, gss, gsr, ret_kv, ret_cg, flat,
    wg, got0, w0, got1, w1, got2, got3,
    s_in, s_kv, r_kv, s_qg, r_qg, s_h, r_h, s_x, r_x, s_s, r_s,
    s_bkv, r_bkv, s_cg, r_cg, s_bh, r_bh, s_bx, r_bx, s_gs, r_gs,
    s0, r0, s1, r1, s2, r2,
):
    y, x, z, c = place()
    loads = []
    for n, (a, b) in enumerate(
        ((tok_in, tok), (wk_in, wk), (wv_in, wv), (wq_in, wq), (cot_in, cot), (wo_in, wo))
    ):
        copy = pltpu.make_async_copy(a, b, s_in.at[n])
        copy.start()
        loads.append(copy)
    partners = all_partners(y, x, z, c)
    barrier = pltpu.get_barrier_semaphore()
    for to in partners:
        pl.semaphore_signal(barrier, inc=1, device_id=to, device_id_type=MESH)
    other = device(y, x, z, 1 - c)
    home = lax.div(z, 2)
    at_home = c == home
    slot = lax.rem(z, 2) * 2 + c
    group = 2 * x + c

    def project(src, w, dst, lane):
        def half(i, carry):
            rows = rows_of(i * 256, 256)
            got = jnp.dot(src[rows, :], w[...], preferred_element_type=F32)
            for h in range(HEADS):
                dst[h, rows, lane : lane + TILE] = got[:, h * TILE : (h + 1) * TILE].astype(BF)
            return carry

        lax.fori_loop(0, 2, half, 0)

    def exchange(staged, landing, base, send, recv):
        spot = rows_of(base + slot * 512, 512)
        copies = []
        near = remote(staged.at[z], landing.at[spot], send.at[0], recv.at[slot], other)

        @pl.when(at_home)
        def _():
            landing[spot, :] = staged[z]

        @pl.when(jnp.logical_not(at_home))
        def _():
            near.start()

        for d in (1, 3, 2):
            h = turn(z, d)
            copy = remote(staged.at[h], landing.at[spot], send.at[d], recv.at[slot], device(y, x, h, home))
            if d != 2:
                copy.start()
            copies.append(copy)
        return copies, near

    def settle_out(copies, near):
        for copy in copies:
            copy.wait_send()

        @pl.when(jnp.logical_not(at_home))
        def _():
            near.wait_send()

    def arrived(staged, landing, base, send, recv, i):
        mine = jnp.logical_and(z == 2 * c + lax.div(i, 2), c == lax.rem(i, 2))

        @pl.when(jnp.logical_not(mine))
        def _():
            remote(
                staged.at[0], landing.at[rows_of(base + i * 512, 512)], send.at[0], recv.at[i], other
            ).wait_recv()

    for n in range(3):
        loads[n].wait()
    project(tok, wk, kvs, 0)
    project(tok, wv, kvs, TILE)
    pl.semaphore_wait(barrier, len(partners))
    kv_sent = exchange(kvs, kv, OWN, s_kv, r_kv)
    for n in range(3, 6):
        loads[n].wait()
    project(tok, wq, qgs, 0)
    first_own = ((x * 4 + z) * 2 + c) * 4

    def grads(i, carry):
        rows = rows_of(i * TILE, TILE)
        got = lax.dot_general(cot[rows, :], wo[...], NT, preferred_element_type=F32)
        live = lax.broadcasted_iota(jnp.int32, (TILE, 512), 0) < lens[0, first_own + i]
        got = jnp.where(live, got, 0.0).astype(BF)
        for h in range(HEADS):
            qgs[h, rows, TILE : 2 * TILE] = got[:, h * TILE : (h + 1) * TILE]
        return carry

    lax.fori_loop(0, 4, grads, 0)
    kv_sent[0][2].start()

    ahead = device(y, turn(x, 1), z, c)
    behind = device(y, turn(x, 3), z, c)

    def halo_copy(i):
        return remote(
            kv.at[rows_of(OWN + i * 512, 512)], kv.at[rows_of(i * 512, 512)], s_h.at[i], r_h.at[i], ahead
        )

    def across_copy(start, i):
        return remote(
            kv.at[rows_of(start + i * 512, 512)],
            kv.at[rows_of(2048 + i * 512, 512)],
            s_x.at[i],
            r_x.at[i],
            other,
        )

    nearest = lax.rem(z + jnp.where(at_home, 0, 1), 2) * 2
    order = [lax.rem(nearest + k, 4) for k in range(4)]
    for i in order:
        arrived(kvs, kv, OWN, s_kv, r_kv, i)
        halo_copy(i).start()

        @pl.when(c == 0)
        def _():
            across_copy(OWN, i).start()

    qg_sent = exchange(qgs, qg, 0, s_qg, r_qg)
    qg_sent[0][2].start()

    def summary(i, carry):
        rows = rows_of(OWN + i * TILE, TILE)
        length = lens[0, group * 16 + i]
        live = lax.broadcasted_iota(jnp.int32, (TILE, 256), 0) < length
        total = jnp.sum(jnp.where(live, kv[rows, :].astype(F32), 0.0), axis=0, keepdims=True)
        sums[pl.ds(i, 1), :] = total / jnp.full((1, 256), length, jnp.int32).astype(F32)
        return carry

    lax.fori_loop(0, 16, summary, 0)
    summ[group] = sums[...].astype(BF)
    sum_copies = []
    pairs_of = [(d, cc) for d in range(4) for cc in (0, 1) if (d, cc) != (0, 0)]
    for d, cc in pairs_of:
        n = d * 2 + cc
        core = lax.rem(c + cc, 2)
        copy = remote(summ.at[group], summ.at[group], s_s.at[n], r_s.at[n], device(y, turn(x, d), z, core))
        copy.start()
        sum_copies.append(copy)

    def prepare(b, carry):
        rows = rows_of(b * TILE, TILE)
        kvt[:, rows] = jnp.transpose(kv[rows, :])
        return carry

    def clear(b, carry):
        gkv[rows_of(b * TILE, TILE), :] = jnp.zeros((TILE, 256), F32)
        return carry

    lax.fori_loop(0, 48, clear, 0)
    gsum[...] = jnp.zeros_like(gsum)
    for u in range(UNROLL):
        pair[u] = jnp.zeros((256, 256), BF)
        pairt[u] = jnp.zeros((256, 256), BF)
    lax.fori_loop(32, 48, prepare, 0)

    def turned(i, carry):
        cols = rows_of(i * TILE, TILE)
        tokt[cols, :] = jnp.transpose(tok[:, cols])
        return carry

    lax.fori_loop(0, 8, turned, 0)
    for i in order:
        halo_copy(i).wait_recv()

        @pl.when(c == 1)
        def _():
            across_copy(0, i).start()

    lax.fori_loop(0, 16, prepare, 0)
    for i in range(4):
        across_copy(0, i).wait()
        halo_copy(i).wait_send()
        arrived(qgs, qg, 0, s_qg, r_qg, i)
    lax.fori_loop(16, 32, prepare, 0)
    for copy in sum_copies:
        copy.wait()
    kvt[:, 48 * TILE : 49 * TILE] = jnp.transpose(summ[...].reshape(TILE, 256))
    settle_out(*kv_sent)
    settle_out(*qg_sent)

    key_slot = lax.broadcasted_iota(jnp.int32, (TILE, TILE), 0)
    query_slot = lax.broadcasted_iota(jnp.int32, (TILE, TILE), 1)
    count = len(OFFSETS)

    def bar(it, carry):
        ids = [it * UNROLL + u for u in range(UNROLL)]
        tops, scales, deltas = [], [], []
        for u, qb in enumerate(ids):
            rows = rows_of(qb * TILE, TILE)
            pair[u, 0:TILE, 0:TILE] = qg[rows, 0:TILE]
            pair[u, TILE:, TILE:] = qg[rows, TILE:]
            pairt[u, 0:TILE, 0:TILE] = jnp.transpose(qg[rows, 0:TILE])
            pairt[u, TILE:, TILE:] = jnp.transpose(qg[rows, TILE:])
            both = pairt[u]
            this = 16 * group + qb
            top = None
            for j in range(count + 1):
                here = slice(j * TILE, (j + 1) * TILE)
                if j < count:
                    spot = rows_of((32 + qb - OFFSETS[j]) * TILE, TILE)
                    bar_id = this - OFFSETS[j]
                    length = jnp.where(bar_id >= 0, lens[0, jnp.maximum(bar_id, 0)], 0)
                    source = kv[spot, :]
                    gt[u, :, here] = kvt[:, spot]
                    ok = key_slot < length
                    if j == 0:
                        ok = jnp.logical_and(ok, key_slot <= query_slot)
                else:
                    source = summ[...].reshape(TILE, 256)
                    gt[u, :, here] = kvt[:, 48 * TILE : 49 * TILE]
                    distance = this - key_slot
                    ok = distance >= 1
                    for o in OFFSETS[1:]:
                        ok = jnp.logical_and(ok, distance != o)
                got = jnp.dot(source, both, preferred_element_type=F32)
                score = jnp.where(ok, got[:, :TILE] * (SCALE * LOG2E), NEG)
                sc[u, here, :TILE] = score
                sc[u, here, TILE:] = got[:, TILE:]
                high = jnp.max(score, axis=0, keepdims=True)
                top = high if top is None else jnp.maximum(top, high)
            tops.append(top)
        for u in range(UNROLL):
            total = jnp.zeros((1, TILE), F32)
            weighted = jnp.zeros((1, TILE), F32)
            for j in range(count + 1):
                here = slice(j * TILE, (j + 1) * TILE)
                e = jnp.exp2(sc[u, here, :TILE] - tops[u])
                sc[u, here, :TILE] = e
                total = total + jnp.sum(e, axis=0, keepdims=True)
                weighted = weighted + jnp.sum(e * sc[u, here, TILE:], axis=0, keepdims=True)
            scales.append(1.0 / total)
            deltas.append(weighted * scales[u])
        for u, qb in enumerate(ids):
            rows = rows_of(qb * TILE, TILE)
            both = pair[u]
            for j in range(count + 1):
                here = slice(j * TILE, (j + 1) * TILE)
                p = sc[u, here, :TILE] * scales[u]
                ds = (p * (sc[u, here, TILE:] - deltas[u])).astype(BF)
                block = jnp.concatenate([ds, p.astype(BF)], axis=1)
                dsp[u, here, :] = block
                got = jnp.dot(block, both, preferred_element_type=F32)
                if j < count:
                    spot = rows_of((32 + qb - OFFSETS[j]) * TILE, TILE)
                    gkv[spot, :] += got
                else:
                    gsum[...] += got
            both_out = jnp.dot(gt[u], dsp[u], preferred_element_type=F32)
            cg[rows, 0:TILE] = jnp.transpose(both_out[:TILE, :TILE] * SCALE).astype(BF)
            context = jnp.transpose(both_out[TILE:, TILE:])
            cg[rows, TILE:] = jnp.where(key_slot < lens[0, 16 * group + qb], context, 0.0).astype(BF)
        return carry

    def owner(i):
        to_z = 2 * c + lax.div(i, 2)
        core = lax.rem(i, 2)
        mine = jnp.logical_and(z == to_z, c == core)
        return device(y, x, to_z, core), mine

    def give_back(src, landing, send, recv, i):
        to, mine = owner(i)
        rows = rows_of(i * 512, 512)

        @pl.when(mine)
        def _():
            landing[z] = src[rows, :]

        @pl.when(jnp.logical_not(mine))
        def _():
            remote(src.at[rows], landing.at[z], send.at[i], recv.at[z], to).start()

    def settle(src, landing, send, recv):
        for i in range(4):
            to, mine = owner(i)

            @pl.when(jnp.logical_not(mine))
            def _():
                remote(src.at[pl.ds(i * 512, 512)], landing.at[z], send.at[i], recv.at[z], to).wait_send()

    def returned(src, landing, send, recv):
        for h in range(HEADS):
            mine = jnp.logical_and(z == h, at_home)

            @pl.when(jnp.logical_not(mine))
            def _():
                remote(src.at[pl.ds(0, 512)], landing.at[h], send.at[0], recv.at[h], other).wait_recv()

    def crossing(i):
        rows = rows_of(i * 512, 512)
        return remote(kvs.at[i], rx.at[rows], s_bx.at[i], r_bx.at[i], other)

    def cross(i):
        kvs[i] = gkv[rows_of(2048 + i * 512, 512), :].astype(BF)
        crossing(i).start()

    def halo_back(i):
        rows = rows_of(i * 512, 512)
        return remote(qgs.at[i], rh.at[rows], s_bh.at[i], r_bh.at[i], behind)

    def chunk(i, carry):
        lax.fori_loop(i * (4 // UNROLL), (i + 1) * (4 // UNROLL), bar, 0)

        @pl.when(c == 0)
        def _():
            rows = rows_of(i * 512, 512)
            qgs[i] = gkv[rows, :].astype(BF)
            halo_back(i).start()

        @pl.when(i >= 2)
        def _():
            cross(i - 2)
            cross(i)

        give_back(cg, ret_cg, s_cg, r_cg, i)
        return carry

    lax.fori_loop(0, 4, chunk, 0)
    gss[...] = gsum[...].astype(BF).reshape(8, 16, 256)
    gsr[group] = gss[group]
    back_copies = []
    for d, cc in pairs_of:
        n = d * 2 + cc
        to_x, core = turn(x, d), lax.rem(c + cc, 2)
        copy = remote(
            gss.at[to_x * 2 + core], gsr.at[group], s_gs.at[n], r_gs.at[n], device(y, to_x, z, core)
        )
        copy.start()
        back_copies.append(copy)
    turns = (0, 2, 1, 3)
    for i in turns:
        crossing(i).wait_recv()

        @pl.when(c == 1)
        def _():
            rows = pl.ds(i * 512, 512)
            qgs[i] = (gkv[rows, :] + rx[rows, :].astype(F32)).astype(BF)
            halo_back(i).start()

    def flatten(src, lane, n):
        for h in range(HEADS):
            flat[n, :, h * TILE : (h + 1) * TILE] = src[h, :, lane : lane + TILE]

    where = {"y": y, "x": x, "z": z}
    levels = ((w0, got1, 256), (w1, got2, 64))
    pending = [None] * 4
    started = []
    last = []

    def along(axis, d):
        at = dict(where)
        at[axis] = turn(where[axis], d)
        return device(at["y"], at["x"], at["z"], c)

    def core_half(m):
        return remote(wg.at[m, 1 - c], got0.at[m], s0.at[0, m], r0.at[0, m], other)

    def send_level(m, level):
        src, got, size = levels[level]
        copies = []
        axis = ORDERS[m][level]
        for d in (1, 2, 3):
            piece = pl.ds(pl.multiple_of(turn(where[axis], d) * size, 16), size)
            copy = remote(
                src.at[m, piece], got.at[m, d - 1], s1.at[level, m, d - 1], r1.at[level, m, d - 1], along(axis, d)
            )
            copy.start()
            copies.append(copy)
        pending[m] = copies
        started.extend(copies)

    def place_rows(m, level):
        start = where[ORDERS[m][0]] * 256
        if level == 1:
            start = start + where[ORDERS[m][1]] * 64
        return pl.ds(pl.multiple_of(start, 16), levels[level][2])

    half = pl.ds(pl.multiple_of(c * 256, 256), 256)

    def give(m, level):
        block = out.at[m, place_rows(m, level), half]
        copies = []
        for d in (1, 2, 3):
            copy = remote(
                block, block, s2.at[level, m, d - 1], r2.at[level, m, d - 1], along(ORDERS[m][level], d)
            )
            copy.start()
            copies.append(copy)
        pending[m] = copies
        started.extend(copies)

    def settled(m):
        for copy in pending[m]:
            copy.wait_recv()

    def begin(m):
        core_half(m).wait_recv()

        def add(i, carry):
            rows = rows_of(i * 256, 256)
            w0[m, rows, :] = (wg[m, c, rows, :].astype(F32) + got0[m, rows, :].astype(F32)).astype(BF)
            return carry

        lax.fori_loop(0, 4, add, 0)
        send_level(m, 0)

    def advance(m, level):
        settled(m)
        if level == 2:
            total = got3[m, 0].astype(F32)
            for n in range(1, 4):
                total = total + got3[m, n].astype(F32)
            out[m, place_rows(m, 1), half] = total.astype(BF)
            give(m, 1)
            return
        src, got, size = levels[level]
        mine = pl.ds(pl.multiple_of(where[ORDERS[m][level]] * size, 16), size)
        total = src[m, mine, :].astype(F32)
        for n in range(3):
            total = total + got[m, n].astype(F32)
        if level == 0:
            w1[m] = total.astype(BF)
            send_level(m, 1)
        else:
            axis = ORDERS[m][2]
            got3[m, where[axis]] = total.astype(BF)
            block = got3.at[m, where[axis]]
            copies = []
            for d in (1, 2, 3):
                copy = remote(block, block, s1.at[2, m, d - 1], r1.at[2, m, d - 1], along(axis, d))
                copy.start()
                copies.append(copy)
            pending[m] = copies
            started.extend(copies)

    def finish(m):
        settled(m)
        copy = remote(out.at[m, :, half], out.at[m, :, half], s0.at[1, m], r0.at[1, m], other)
        copy.start()
        last.append(copy)

    def weight_grad(n, m):
        def part(i, carry):
            cols = rows_of(i * 256, 256)
            got = jnp.dot(tokt[cols, :], flat[n], preferred_element_type=F32).astype(BF)
            wg[m, 0, cols, :] = got[:, :256]
            wg[m, 1, cols, :] = got[:, 256:]
            return carry

        lax.fori_loop(0, 4, part, 0)
        core_half(m).start()

    returned(cg, ret_cg, s_cg, r_cg)
    flatten(ret_cg, 0, 0)
    weight_grad(0, 0)
    flatten(ret_cg, TILE, 3)

    def out_grad(i, carry):
        cols = rows_of(i * 256, 256)
        got = lax.dot_general(flat[3], cot[:, cols], TN, preferred_element_type=F32).astype(BF)
        wg[3, lax.rem(i, 2), rows_of(lax.div(i, 2) * 512, 512), :] = got
        return carry

    lax.fori_loop(0, 4, out_grad, 0)
    core_half(3).start()
    begin(0)
    begin(3)

    for copy in back_copies:
        copy.wait()
    coarse = gsr[0].astype(F32)
    for n in range(1, 8):
        coarse = coarse + gsr[n].astype(F32)
    lane = lax.broadcasted_iota(jnp.int32, (1, 256), 1)
    factor = jnp.where(lane < TILE, SCALE, 1.0)
    for i in turns:
        halo_back(i).wait_recv()
        for b in range(4 * i, 4 * i + 4):
            rows = pl.ds(b * TILE, TILE)
            length = lens[0, group * 16 + b]
            live = lax.broadcasted_iota(jnp.int32, (TILE, 256), 0) < length
            share = coarse[b : b + 1, :] * (1.0 / jnp.full((1, 256), length, jnp.int32).astype(F32))
            extra = jnp.where(c == 0, rx[rows, :].astype(F32), 0.0)
            total = gkv[pl.ds(OWN + b * TILE, TILE), :] + rh[rows, :].astype(F32) + extra
            qg[rows, :] = ((total + jnp.where(live, share, 0.0)) * factor).astype(BF)
        give_back(qg, ret_kv, s_bkv, r_bkv, i)

    def mix(i, carry):
        rows = rows_of(i * 256, 256)
        mixed[rows, :] = jnp.dot(flat[3, rows, :], wo[...], preferred_element_type=F32).astype(BF)
        return carry

    lax.fori_loop(0, 2, mix, 0)
    advance(0, 0)
    advance(3, 0)
    returned(qg, ret_kv, s_bkv, r_bkv)
    flatten(ret_kv, 0, 1)
    weight_grad(1, 1)
    flatten(ret_kv, TILE, 2)
    weight_grad(2, 2)
    begin(1)
    begin(2)
    advance(0, 1)
    advance(3, 1)

    def back(i, carry):
        rows = rows_of(i * 256, 256)
        total = lax.dot_general(flat[0, rows, :], wq[...], NT, preferred_element_type=F32)
        total = total + lax.dot_general(flat[1, rows, :], wk[...], NT, preferred_element_type=F32)
        total = total + lax.dot_general(flat[2, rows, :], wv[...], NT, preferred_element_type=F32)
        gin[rows, :] = total.astype(BF)
        return carry

    lax.fori_loop(0, 2, back, 0)
    advance(0, 2)
    advance(3, 2)
    settled(0)
    give(0, 0)
    for level in (0, 1):
        advance(1, level)
        advance(2, level)
    settled(3)
    give(3, 0)
    advance(1, 2)
    advance(2, 2)
    finish(0)
    for m in (1, 2):
        settled(m)
        give(m, 0)
    for m in (3, 1, 2):
        finish(m)
    for copy in last:
        copy.wait()
    for m in range(4):
        core_half(m).wait_send()
        crossing(m).wait_send()
        halo_back(m).wait_send()
    for copy in started:
        copy.wait_send()
    settle(cg, ret_cg, s_cg, r_cg)
    settle(qg, ret_kv, s_bkv, r_bkv)


def hand_over(mixed, gin, total, *refs):
    mixed_out, gin_out, outs = refs[0], refs[1], refs[2:6]
    narrow, wide, s_in, s_out, kept, s_kept, s_pass = refs[6:]
    halves = [pl.ds(0, 512), pl.ds(512, 512)]
    held = [
        pltpu.make_async_copy(src, kept.at[n], s_kept.at[n]) for n, src in enumerate((mixed, gin))
    ]
    passed = [
        pltpu.make_async_copy(kept.at[n], dst, s_pass.at[n])
        for n, dst in enumerate((mixed_out, gin_out))
    ]
    loads = [
        pltpu.make_async_copy(total.at[n // 2, halves[n % 2]], narrow.at[n], s_in.at[n]) for n in range(8)
    ]
    for copy in loads + held:
        copy.start()
    stores = []
    for n in range(8):
        loads[n].wait()
        wide[n] = narrow[n].astype(F32)
        to = outs[3].at[:, halves[n % 2]] if n >= 6 else outs[n // 2].at[halves[n % 2]]
        stores.append(pltpu.make_async_copy(wide.at[n], to, s_out.at[n]))
        stores[n].start()
    for n in range(2):
        held[n].wait()
        passed[n].start()
    for copy in stores + passed:
        copy.wait()


ORDERS = ("yxz", "xzy", "zxy", "yzx")
UNROLL = 4

HB = pl.BlockSpec(memory_space=pl.ANY)
VM = pl.BlockSpec(memory_space=pltpu.VMEM)
SM = pl.BlockSpec(memory_space=pltpu.SMEM)
DMA = pltpu.SemaphoreType.DMA


def shape(*dims, kind=BF):
    return jax.ShapeDtypeStruct(dims, kind)


def local(tokens, lengths, w_query, w_key, w_value, w_out, cotangent):
    vm = pltpu.VMEM
    slabs = lambda n: [vm((2048, 256), BF)] * n
    heads = lambda n: [vm((4, 512, 256), BF)] * n
    mixed, gin, total = pl.pallas_call(
        whole_kernel,
        out_shape=(shape(512, 1024), shape(512, 1024), shape(4, 1024, 512)),
        in_specs=[SM] + [HB] * 6,
        out_specs=(VM, VM, VM),
        scratch_shapes=[vm((512, 1024), BF), vm((1024, 512), BF), vm((512, 1024), BF)]
        + [vm((1024, 512), BF)] * 3
        + [vm((512, 1024), BF), vm((6144, 256), BF)]
        + slabs(1)
        + [vm((8, 16, 256), BF)]
        + heads(2)
        + [vm((16, 256), F32)]
        + [
            vm((256, 49 * TILE), BF),
            vm((UNROLL, 256, 10 * TILE), BF),
            vm((UNROLL, 256, 256), BF),
            vm((UNROLL, 256, 256), BF),
            vm((UNROLL, 10 * TILE, 256), F32),
            vm((UNROLL, 10 * TILE, 256), BF),
            vm((6144, 256), F32),
            vm((128, 256), F32),
        ]
        + slabs(3)
        + [vm((8, 16, 256), BF)] * 2
        + heads(2)
        + [
            vm((4, 512, 512), BF),
            vm((4, 2, 1024, 256), BF),
            vm((4, 1024, 256), BF),
            vm((4, 1024, 256), BF),
            vm((4, 3, 256, 256), BF),
            vm((4, 256, 256), BF),
            vm((4, 3, 64, 256), BF),
            vm((4, 4, 64, 256), BF),
        ]
        + [DMA((6,))]
        + [DMA((4,))] * 8
        + [DMA((8,))] * 2
        + [DMA((4,))] * 8
        + [DMA((8,))] * 2
        + [DMA((2, 4))] * 2
        + [DMA((3, 4, 3))] * 2
        + [DMA((2, 4, 3))] * 2,
        compiler_params=pltpu.CompilerParams(
            collective_id=0, has_side_effects=True, vmem_limit_bytes=62 * MIB
        ),
        name="whole",
    )(lengths, tokens[0], w_key, w_value, w_query, cotangent[0], w_out)
    mixed, gin, *weights = pl.pallas_call(
        hand_over,
        out_shape=(shape(512, 1024), shape(512, 1024))
        + (shape(1024, 512, kind=F32),) * 3
        + (shape(512, 1024, kind=F32),),
        in_specs=[HB] * 3,
        out_specs=(HB,) * 6,
        scratch_shapes=[vm((8, 512, 512), BF), vm((8, 512, 512), F32), DMA((8,)), DMA((8,))]
        + [vm((2, 512, 1024), BF), DMA((2,)), DMA((2,))],
        compiler_params=pltpu.CompilerParams(vmem_limit_bytes=62 * MIB),
        name="hand_over",
    )(mixed, gin, total)
    return (mixed[None], gin[None], *weights)


def solution(mesh):
    placed = (P("dp", "seq", None), P("dp", None), P(), P(), P(), P(), P("dp", "seq", None))
    return jax.shard_map(
        local,
        mesh=mesh,
        in_specs=placed,
        out_specs=(P("dp", "seq", None), P("dp", "seq", None), P(), P(), P(), P()),
        check_vma=False,
    )
```

```python
import functools
import math

import jax
import jax.numpy as jnp
from jax import lax
from jax.experimental import pallas as pl
from jax.experimental.pallas import tpu as pltpu
from jax.sharding import PartitionSpec as P

MESH = pl.DeviceIdType.MESH
BF = jnp.bfloat16
F32 = jnp.float32
HEADS = 4
TILE = 128
OFFSETS = (0, 1, 2, 4, 8, 12, 16, 24, 32)
SCALE = 1.0 / math.sqrt(128.0)
LOG2E = 1.4426950408889634
NEG = -1e30
NT = (((1,), (1,)), ((), ()))
TN = (((0,), (0,)), ((), ()))
OWN = 32 * TILE
MIB = 1024 * 1024


def place():
    s = lax.axis_index("seq")
    return lax.axis_index("dp"), lax.div(s, 8), lax.rem(lax.div(s, 2), 4), lax.rem(s, 2)


def device(y, x, z, c):
    return (y, (x * 4 + z) * 2 + c)


def turn(a, d):
    return lax.rem(a + d, 4)


def remote(src, dst, send, recv, to):
    return pltpu.make_async_remote_copy(
        src_ref=src, dst_ref=dst, send_sem=send, recv_sem=recv, device_id=to, device_id_type=MESH
    )


def all_partners(y, x, z, c):
    found = [device(y, x, z, 1 - c)]
    for d in (1, 2, 3):
        found.append(device(turn(y, d), x, z, c))
        for core in (0, 1):
            found.append(device(y, turn(x, d), z, core))
            found.append(device(y, x, turn(z, d), core))
    return found


def rows_of(start, count):
    return pl.ds(pl.multiple_of(start, TILE), count)


def whole_kernel(
    lens, tok_in, wk_in, wv_in, wq_in, cot_in, wo_in, mixed_out, gin_out, total_out,
    mixed, gin, out,
    tok, tokt, cot, wq, wk, wv, wo,
    kv, qg, summ, kvs, qgs, sums,
    kvt, gt, pair, pairt, sc, dsp, gkv, gsum, cg,
    rx, rh, gss, gsr, ret_kv, ret_cg, flat,
    wg, got0, w0, got1, w1, got2, got3,
    s_in, s_kv, r_kv, s_qg, r_qg, s_h, r_h, s_x, r_x, s_s, r_s,
    s_bkv, r_bkv, s_cg, r_cg, s_bh, r_bh, s_bx, r_bx, s_gs, r_gs,
    s0, r0, s1, r1, s2, r2,
):
    y, x, z, c = place()
    loads = []
    for n, (a, b) in enumerate(
        ((tok_in, tok), (wk_in, wk), (wv_in, wv), (wq_in, wq), (cot_in, cot), (wo_in, wo))
    ):
        copy = pltpu.make_async_copy(a, b, s_in.at[n])
        copy.start()
        loads.append(copy)
    partners = all_partners(y, x, z, c)
    barrier = pltpu.get_barrier_semaphore()
    for to in partners:
        pl.semaphore_signal(barrier, inc=1, device_id=to, device_id_type=MESH)
    other = device(y, x, z, 1 - c)
    home = lax.div(z, 2)
    at_home = c == home
    slot = lax.rem(z, 2) * 2 + c
    group = 2 * x + c

    def project(src, w, dst, lane):
        def half(i, carry):
            rows = rows_of(i * 256, 256)
            got = jnp.dot(src[rows, :], w[...], preferred_element_type=F32)
            for h in range(HEADS):
                dst[h, rows, lane : lane + TILE] = got[:, h * TILE : (h + 1) * TILE].astype(BF)
            return carry

        lax.fori_loop(0, 2, half, 0)

    def exchange(staged, landing, base, send, recv):
        spot = rows_of(base + slot * 512, 512)
        copies = []
        near = remote(staged.at[z], landing.at[spot], send.at[0], recv.at[slot], other)

        @pl.when(at_home)
        def _():
            landing[spot, :] = staged[z]

        @pl.when(jnp.logical_not(at_home))
        def _():
            near.start()

        for d in (1, 3, 2):
            h = turn(z, d)
            copy = remote(staged.at[h], landing.at[spot], send.at[d], recv.at[slot], device(y, x, h, home))
            if d != 2:
                copy.start()
            copies.append(copy)
        return copies, near

    def settle_out(copies, near):
        for copy in copies:
            copy.wait_send()

        @pl.when(jnp.logical_not(at_home))
        def _():
            near.wait_send()

    def arrived(staged, landing, base, send, recv, i):
        mine = jnp.logical_and(z == 2 * c + lax.div(i, 2), c == lax.rem(i, 2))

        @pl.when(jnp.logical_not(mine))
        def _():
            remote(
                staged.at[0], landing.at[rows_of(base + i * 512, 512)], send.at[0], recv.at[i], other
            ).wait_recv()

    for n in range(3):
        loads[n].wait()
    project(tok, wk, kvs, 0)
    project(tok, wv, kvs, TILE)
    pl.semaphore_wait(barrier, len(partners))
    kv_sent = exchange(kvs, kv, OWN, s_kv, r_kv)
    for n in range(3, 6):
        loads[n].wait()
    project(tok, wq, qgs, 0)
    first_own = ((x * 4 + z) * 2 + c) * 4

    def grads(i, carry):
        rows = rows_of(i * TILE, TILE)
        got = lax.dot_general(cot[rows, :], wo[...], NT, preferred_element_type=F32)
        live = lax.broadcasted_iota(jnp.int32, (TILE, 512), 0) < lens[0, first_own + i]
        got = jnp.where(live, got, 0.0).astype(BF)
        for h in range(HEADS):
            qgs[h, rows, TILE : 2 * TILE] = got[:, h * TILE : (h + 1) * TILE]
        return carry

    lax.fori_loop(0, 4, grads, 0)
    kv_sent[0][2].start()

    ahead = device(y, turn(x, 1), z, c)
    behind = device(y, turn(x, 3), z, c)

    def halo_copy(i):
        return remote(
            kv.at[rows_of(OWN + i * 512, 512)], kv.at[rows_of(i * 512, 512)], s_h.at[i], r_h.at[i], ahead
        )

    def across_copy(start, i):
        return remote(
            kv.at[rows_of(start + i * 512, 512)],
            kv.at[rows_of(2048 + i * 512, 512)],
            s_x.at[i],
            r_x.at[i],
            other,
        )

    nearest = lax.rem(z + jnp.where(at_home, 0, 1), 2) * 2
    order = [lax.rem(nearest + k, 4) for k in range(4)]
    for i in order:
        arrived(kvs, kv, OWN, s_kv, r_kv, i)
        halo_copy(i).start()

        @pl.when(c == 0)
        def _():
            across_copy(OWN, i).start()

    qg_sent = exchange(qgs, qg, 0, s_qg, r_qg)
    qg_sent[0][2].start()

    def summary(i, carry):
        rows = rows_of(OWN + i * TILE, TILE)
        length = lens[0, group * 16 + i]
        live = lax.broadcasted_iota(jnp.int32, (TILE, 256), 0) < length
        total = jnp.sum(jnp.where(live, kv[rows, :].astype(F32), 0.0), axis=0, keepdims=True)
        sums[pl.ds(i, 1), :] = total / jnp.full((1, 256), length, jnp.int32).astype(F32)
        return carry

    lax.fori_loop(0, 16, summary, 0)
    summ[group] = sums[...].astype(BF)
    sum_copies = []
    pairs_of = [(d, cc) for d in range(4) for cc in (0, 1) if (d, cc) != (0, 0)]
    for d, cc in pairs_of:
        n = d * 2 + cc
        core = lax.rem(c + cc, 2)
        copy = remote(summ.at[group], summ.at[group], s_s.at[n], r_s.at[n], device(y, turn(x, d), z, core))
        copy.start()
        sum_copies.append(copy)

    def prepare(b, carry):
        rows = rows_of(b * TILE, TILE)
        kvt[:, rows] = jnp.transpose(kv[rows, :])
        return carry

    def clear(b, carry):
        gkv[rows_of(b * TILE, TILE), :] = jnp.zeros((TILE, 256), F32)
        return carry

    lax.fori_loop(0, 48, clear, 0)
    gsum[...] = jnp.zeros_like(gsum)
    for u in range(UNROLL):
        pair[u] = jnp.zeros((256, 256), BF)
        pairt[u] = jnp.zeros((256, 256), BF)
    lax.fori_loop(32, 48, prepare, 0)

    def turned(i, carry):
        cols = rows_of(i * TILE, TILE)
        tokt[cols, :] = jnp.transpose(tok[:, cols])
        return carry

    lax.fori_loop(0, 8, turned, 0)
    for i in order:
        halo_copy(i).wait_recv()

        @pl.when(c == 1)
        def _():
            across_copy(0, i).start()

    lax.fori_loop(0, 16, prepare, 0)
    for i in range(4):
        across_copy(0, i).wait()
        halo_copy(i).wait_send()
        arrived(qgs, qg, 0, s_qg, r_qg, i)
    lax.fori_loop(16, 32, prepare, 0)
    for copy in sum_copies:
        copy.wait()
    kvt[:, 48 * TILE : 49 * TILE] = jnp.transpose(summ[...].reshape(TILE, 256))
    settle_out(*kv_sent)
    settle_out(*qg_sent)

    key_slot = lax.broadcasted_iota(jnp.int32, (TILE, TILE), 0)
    query_slot = lax.broadcasted_iota(jnp.int32, (TILE, TILE), 1)
    count = len(OFFSETS)

    def bar(it, carry):
        ids = [it * UNROLL + u for u in range(UNROLL)]
        tops, scales, deltas = [], [], []
        for u, qb in enumerate(ids):
            rows = rows_of(qb * TILE, TILE)
            pair[u, 0:TILE, 0:TILE] = qg[rows, 0:TILE]
            pair[u, TILE:, TILE:] = qg[rows, TILE:]
            pairt[u, 0:TILE, 0:TILE] = jnp.transpose(qg[rows, 0:TILE])
            pairt[u, TILE:, TILE:] = jnp.transpose(qg[rows, TILE:])
            both = pairt[u]
            this = 16 * group + qb
            top = None
            for j in range(count + 1):
                here = slice(j * TILE, (j + 1) * TILE)
                if j < count:
                    spot = rows_of((32 + qb - OFFSETS[j]) * TILE, TILE)
                    bar_id = this - OFFSETS[j]
                    length = jnp.where(bar_id >= 0, lens[0, jnp.maximum(bar_id, 0)], 0)
                    source = kv[spot, :]
                    gt[u, :, here] = kvt[:, spot]
                    ok = key_slot < length
                    if j == 0:
                        ok = jnp.logical_and(ok, key_slot <= query_slot)
                else:
                    source = summ[...].reshape(TILE, 256)
                    gt[u, :, here] = kvt[:, 48 * TILE : 49 * TILE]
                    distance = this - key_slot
                    ok = distance >= 1
                    for o in OFFSETS[1:]:
                        ok = jnp.logical_and(ok, distance != o)
                got = jnp.dot(source, both, preferred_element_type=F32)
                score = jnp.where(ok, got[:, :TILE] * (SCALE * LOG2E), NEG)
                sc[u, here, :TILE] = score
                sc[u, here, TILE:] = got[:, TILE:]
                high = jnp.max(score, axis=0, keepdims=True)
                top = high if top is None else jnp.maximum(top, high)
            tops.append(top)
        for u in range(UNROLL):
            total = jnp.zeros((1, TILE), F32)
            weighted = jnp.zeros((1, TILE), F32)
            for j in range(count + 1):
                here = slice(j * TILE, (j + 1) * TILE)
                e = jnp.exp2(sc[u, here, :TILE] - tops[u])
                sc[u, here, :TILE] = e
                total = total + jnp.sum(e, axis=0, keepdims=True)
                weighted = weighted + jnp.sum(e * sc[u, here, TILE:], axis=0, keepdims=True)
            scales.append(1.0 / total)
            deltas.append(weighted * scales[u])
        for u, qb in enumerate(ids):
            rows = rows_of(qb * TILE, TILE)
            both = pair[u]
            for j in range(count + 1):
                here = slice(j * TILE, (j + 1) * TILE)
                p = sc[u, here, :TILE] * scales[u]
                ds = (p * (sc[u, here, TILE:] - deltas[u])).astype(BF)
                block = jnp.concatenate([ds, p.astype(BF)], axis=1)
                dsp[u, here, :] = block
                got = jnp.dot(block, both, preferred_element_type=F32)
                if j < count:
                    spot = rows_of((32 + qb - OFFSETS[j]) * TILE, TILE)
                    gkv[spot, :] += got
                else:
                    gsum[...] += got
            both_out = jnp.dot(gt[u], dsp[u], preferred_element_type=F32)
            cg[rows, 0:TILE] = jnp.transpose(both_out[:TILE, :TILE] * SCALE).astype(BF)
            context = jnp.transpose(both_out[TILE:, TILE:])
            cg[rows, TILE:] = jnp.where(key_slot < lens[0, 16 * group + qb], context, 0.0).astype(BF)
        return carry

    def owner(i):
        to_z = 2 * c + lax.div(i, 2)
        core = lax.rem(i, 2)
        mine = jnp.logical_and(z == to_z, c == core)
        return device(y, x, to_z, core), mine

    def give_back(src, landing, send, recv, i):
        to, mine = owner(i)
        rows = rows_of(i * 512, 512)

        @pl.when(mine)
        def _():
            landing[z] = src[rows, :]

        @pl.when(jnp.logical_not(mine))
        def _():
            remote(src.at[rows], landing.at[z], send.at[i], recv.at[z], to).start()

    def settle(src, landing, send, recv):
        for i in range(4):
            to, mine = owner(i)

            @pl.when(jnp.logical_not(mine))
            def _():
                remote(src.at[pl.ds(i * 512, 512)], landing.at[z], send.at[i], recv.at[z], to).wait_send()

    def returned(src, landing, send, recv):
        for h in range(HEADS):
            mine = jnp.logical_and(z == h, at_home)

            @pl.when(jnp.logical_not(mine))
            def _():
                remote(src.at[pl.ds(0, 512)], landing.at[h], send.at[0], recv.at[h], other).wait_recv()

    def crossing(i):
        rows = rows_of(i * 512, 512)
        return remote(kvs.at[i], rx.at[rows], s_bx.at[i], r_bx.at[i], other)

    def cross(i):
        kvs[i] = gkv[rows_of(2048 + i * 512, 512), :].astype(BF)
        crossing(i).start()

    def halo_back(i):
        rows = rows_of(i * 512, 512)
        return remote(qgs.at[i], rh.at[rows], s_bh.at[i], r_bh.at[i], behind)

    def core_one(i):
        @pl.when(c == 1)
        def _():
            rows = pl.ds(i * 512, 512)
            qgs[i] = (gkv[rows, :] + rx[rows, :].astype(F32)).astype(BF)
            halo_back(i).start()

    def chunk(step, carry):
        i = jnp.where(step == 1, 2, jnp.where(step == 2, 1, step))
        lax.fori_loop(0, 4 // UNROLL, lambda u, kept: bar(i * (4 // UNROLL) + u, kept), 0)

        @pl.when(c == 0)
        def _():
            rows = rows_of(i * 512, 512)
            qgs[i] = gkv[rows, :].astype(BF)
            halo_back(i).start()

        @pl.when(step == 1)
        def _():
            cross(0)

        @pl.when(step == 2)
        def _():
            cross(2)
            crossing(0).wait_recv()
            core_one(0)

        give_back(cg, ret_cg, s_cg, r_cg, i)
        return carry

    lax.fori_loop(0, 4, chunk, 0)
    cross(1)
    cross(3)
    gss[...] = gsum[...].astype(BF).reshape(8, 16, 256)
    gsr[group] = gss[group]
    back_copies = []
    for d, cc in pairs_of:
        n = d * 2 + cc
        to_x, core = turn(x, d), lax.rem(c + cc, 2)
        copy = remote(
            gss.at[to_x * 2 + core], gsr.at[group], s_gs.at[n], r_gs.at[n], device(y, to_x, z, core)
        )
        copy.start()
        back_copies.append(copy)
    turns = (0, 2, 1, 3)
    for i in turns[1:]:
        crossing(i).wait_recv()
        core_one(i)

    def flatten(src, lane, n):
        for h in range(HEADS):
            flat[n, :, h * TILE : (h + 1) * TILE] = src[h, :, lane : lane + TILE]

    where = {"y": y, "x": x, "z": z}
    levels = ((w0, got1, 256), (w1, got2, 64))
    pending = [None] * 4
    started = []
    last = []

    def along(axis, d):
        at = dict(where)
        at[axis] = turn(where[axis], d)
        return device(at["y"], at["x"], at["z"], c)

    def core_half(m):
        return remote(wg.at[m, 1 - c], got0.at[m], s0.at[0, m], r0.at[0, m], other)

    def send_level(m, level):
        src, got, size = levels[level]
        copies = []
        axis = ORDERS[m][level]
        for d in (1, 2, 3):
            piece = pl.ds(pl.multiple_of(turn(where[axis], d) * size, 16), size)
            copy = remote(
                src.at[m, piece], got.at[m, d - 1], s1.at[level, m, d - 1], r1.at[level, m, d - 1], along(axis, d)
            )
            copy.start()
            copies.append(copy)
        pending[m] = copies
        started.extend(copies)

    def place_rows(m, level):
        start = where[ORDERS[m][0]] * 256
        if level == 1:
            start = start + where[ORDERS[m][1]] * 64
        return pl.ds(pl.multiple_of(start, 16), levels[level][2])

    half = pl.ds(pl.multiple_of(c * 256, 256), 256)

    def give(m, level):
        block = out.at[m, place_rows(m, level), half]
        copies = []
        for d in (1, 2, 3):
            copy = remote(
                block, block, s2.at[level, m, d - 1], r2.at[level, m, d - 1], along(ORDERS[m][level], d)
            )
            copy.start()
            copies.append(copy)
        pending[m] = copies
        started.extend(copies)

    def settled(m):
        for copy in pending[m]:
            copy.wait_recv()

    def begin(m):
        core_half(m).wait_recv()

        def add(i, carry):
            rows = rows_of(i * 256, 256)
            w0[m, rows, :] = (wg[m, c, rows, :].astype(F32) + got0[m, rows, :].astype(F32)).astype(BF)
            return carry

        lax.fori_loop(0, 4, add, 0)
        send_level(m, 0)

    def advance(m, level):
        settled(m)
        if level == 2:
            total = got3[m, 0].astype(F32)
            for n in range(1, 4):
                total = total + got3[m, n].astype(F32)
            out[m, place_rows(m, 1), half] = total.astype(BF)
            give(m, 1)
            return
        src, got, size = levels[level]
        mine = pl.ds(pl.multiple_of(where[ORDERS[m][level]] * size, 16), size)
        total = src[m, mine, :].astype(F32)
        for n in range(3):
            total = total + got[m, n].astype(F32)
        if level == 0:
            w1[m] = total.astype(BF)
            send_level(m, 1)
        else:
            axis = ORDERS[m][2]
            got3[m, where[axis]] = total.astype(BF)
            block = got3.at[m, where[axis]]
            copies = []
            for d in (1, 2, 3):
                copy = remote(block, block, s1.at[2, m, d - 1], r1.at[2, m, d - 1], along(axis, d))
                copy.start()
                copies.append(copy)
            pending[m] = copies
            started.extend(copies)

    def finish(m):
        settled(m)
        copy = remote(out.at[m, :, half], out.at[m, :, half], s0.at[1, m], r0.at[1, m], other)
        copy.start()
        last.append(copy)

    def weight_grad(n, m):
        def part(i, carry):
            cols = rows_of(i * 256, 256)
            got = jnp.dot(tokt[cols, :], flat[n], preferred_element_type=F32).astype(BF)
            wg[m, 0, cols, :] = got[:, :256]
            wg[m, 1, cols, :] = got[:, 256:]
            return carry

        lax.fori_loop(0, 4, part, 0)
        core_half(m).start()

    returned(cg, ret_cg, s_cg, r_cg)
    flatten(ret_cg, 0, 0)
    weight_grad(0, 0)
    flatten(ret_cg, TILE, 3)

    def out_grad(i, carry):
        cols = rows_of(i * 256, 256)
        got = lax.dot_general(flat[3], cot[:, cols], TN, preferred_element_type=F32).astype(BF)
        wg[3, lax.rem(i, 2), rows_of(lax.div(i, 2) * 512, 512), :] = got
        return carry

    lax.fori_loop(0, 4, out_grad, 0)
    core_half(3).start()
    begin(0)
    begin(3)

    for copy in back_copies:
        copy.wait()
    coarse = gsr[0].astype(F32)
    for n in range(1, 8):
        coarse = coarse + gsr[n].astype(F32)
    lane = lax.broadcasted_iota(jnp.int32, (1, 256), 1)
    factor = jnp.where(lane < TILE, SCALE, 1.0)
    for i in turns:
        halo_back(i).wait_recv()
        for b in range(4 * i, 4 * i + 4):
            rows = pl.ds(b * TILE, TILE)
            length = lens[0, group * 16 + b]
            live = lax.broadcasted_iota(jnp.int32, (TILE, 256), 0) < length
            share = coarse[b : b + 1, :] * (1.0 / jnp.full((1, 256), length, jnp.int32).astype(F32))
            extra = jnp.where(c == 0, rx[rows, :].astype(F32), 0.0)
            total = gkv[pl.ds(OWN + b * TILE, TILE), :] + rh[rows, :].astype(F32) + extra
            qg[rows, :] = ((total + jnp.where(live, share, 0.0)) * factor).astype(BF)
        give_back(qg, ret_kv, s_bkv, r_bkv, i)

    def mix(i, carry):
        rows = rows_of(i * 256, 256)
        mixed[rows, :] = jnp.dot(flat[3, rows, :], wo[...], preferred_element_type=F32).astype(BF)
        return carry

    lax.fori_loop(0, 2, mix, 0)
    mixed_written = pltpu.make_async_copy(mixed, mixed_out, s_in.at[0])
    mixed_written.start()
    for level in (0, 1):
        advance(0, level)
        advance(3, level)
    returned(qg, ret_kv, s_bkv, r_bkv)
    flatten(ret_kv, 0, 1)
    weight_grad(1, 1)
    flatten(ret_kv, TILE, 2)
    weight_grad(2, 2)
    advance(0, 2)
    advance(3, 2)
    begin(1)
    begin(2)

    def back(i, carry):
        rows = rows_of(i * 256, 256)
        total = lax.dot_general(flat[0, rows, :], wq[...], NT, preferred_element_type=F32)
        total = total + lax.dot_general(flat[1, rows, :], wk[...], NT, preferred_element_type=F32)
        total = total + lax.dot_general(flat[2, rows, :], wv[...], NT, preferred_element_type=F32)
        gin[rows, :] = total.astype(BF)
        return carry

    lax.fori_loop(0, 2, back, 0)
    gin_written = pltpu.make_async_copy(gin, gin_out, s_in.at[1])
    gin_written.start()
    for m in (0, 3):
        settled(m)
        give(m, 0)
    for level in range(3):
        advance(1, level)
        advance(2, level)
    finish(0)
    finish(3)
    for m in (1, 2):
        settled(m)
        give(m, 0)
    for n in range(2):
        last[n].wait()
    written = [pltpu.make_async_copy(out.at[m], total_out.at[m], s_in.at[2 + m]) for m in range(4)]
    written[0].start()
    written[3].start()
    finish(1)
    finish(2)
    for n in (2, 3):
        last[n].wait()
        written[n - 1].start()
    mixed_written.wait()
    gin_written.wait()
    for copy in written:
        copy.wait()
    for m in range(4):
        core_half(m).wait_send()
        crossing(m).wait_send()
        halo_back(m).wait_send()
    for copy in started:
        copy.wait_send()
    settle(cg, ret_cg, s_cg, r_cg)
    settle(qg, ret_kv, s_bkv, r_bkv)


def hand_over(mixed, gin, total, *refs):
    mixed_out, gin_out, outs = refs[0], refs[1], refs[2:6]
    narrow, wide, s_in, s_out, kept, s_kept, s_pass = refs[6:]
    halves = [pl.ds(0, 512), pl.ds(512, 512)]
    held = [
        pltpu.make_async_copy(src, kept.at[n], s_kept.at[n]) for n, src in enumerate((mixed, gin))
    ]
    passed = [
        pltpu.make_async_copy(kept.at[n], dst, s_pass.at[n])
        for n, dst in enumerate((mixed_out, gin_out))
    ]
    loads = [
        pltpu.make_async_copy(total.at[n // 2, halves[n % 2]], narrow.at[n], s_in.at[n]) for n in range(8)
    ]
    for copy in loads + held:
        copy.start()
    stores = []
    for n in range(8):
        loads[n].wait()
        wide[n] = narrow[n].astype(F32)
        to = outs[3].at[:, halves[n % 2]] if n >= 6 else outs[n // 2].at[halves[n % 2]]
        stores.append(pltpu.make_async_copy(wide.at[n], to, s_out.at[n]))
        stores[n].start()
    for n in range(2):
        held[n].wait()
        passed[n].start()
    for copy in stores + passed:
        copy.wait()


ORDERS = ("yxz", "xzy", "zxy", "yzx")
UNROLL = 4

HB = pl.BlockSpec(memory_space=pl.ANY)
VM = pl.BlockSpec(memory_space=pltpu.VMEM)
SM = pl.BlockSpec(memory_space=pltpu.SMEM)
DMA = pltpu.SemaphoreType.DMA


def shape(*dims, kind=BF):
    return jax.ShapeDtypeStruct(dims, kind)


def local(tokens, lengths, w_query, w_key, w_value, w_out, cotangent):
    vm = pltpu.VMEM
    slabs = lambda n: [vm((2048, 256), BF)] * n
    heads = lambda n: [vm((4, 512, 256), BF)] * n
    mixed, gin, total = pl.pallas_call(
        whole_kernel,
        out_shape=(shape(512, 1024), shape(512, 1024), shape(4, 1024, 512)),
        in_specs=[SM] + [HB] * 6,
        out_specs=(HB, HB, HB),
        scratch_shapes=[vm((512, 1024), BF), vm((512, 1024), BF), vm((4, 1024, 512), BF)]
        + [vm((512, 1024), BF), vm((1024, 512), BF), vm((512, 1024), BF)]
        + [vm((1024, 512), BF)] * 3
        + [vm((512, 1024), BF), vm((6144, 256), BF)]
        + slabs(1)
        + [vm((8, 16, 256), BF)]
        + heads(2)
        + [vm((16, 256), F32)]
        + [
            vm((256, 49 * TILE), BF),
            vm((UNROLL, 256, 10 * TILE), BF),
            vm((UNROLL, 256, 256), BF),
            vm((UNROLL, 256, 256), BF),
            vm((UNROLL, 10 * TILE, 256), F32),
            vm((UNROLL, 10 * TILE, 256), BF),
            vm((6144, 256), F32),
            vm((128, 256), F32),
        ]
        + slabs(3)
        + [vm((8, 16, 256), BF)] * 2
        + heads(2)
        + [
            vm((4, 512, 512), BF),
            vm((4, 2, 1024, 256), BF),
            vm((4, 1024, 256), BF),
            vm((4, 1024, 256), BF),
            vm((4, 3, 256, 256), BF),
            vm((4, 256, 256), BF),
            vm((4, 3, 64, 256), BF),
            vm((4, 4, 64, 256), BF),
        ]
        + [DMA((6,))]
        + [DMA((4,))] * 8
        + [DMA((8,))] * 2
        + [DMA((4,))] * 8
        + [DMA((8,))] * 2
        + [DMA((2, 4))] * 2
        + [DMA((3, 4, 3))] * 2
        + [DMA((2, 4, 3))] * 2,
        compiler_params=pltpu.CompilerParams(
            collective_id=0, has_side_effects=True, vmem_limit_bytes=62 * MIB
        ),
        name="whole",
    )(lengths, tokens[0], w_key, w_value, w_query, cotangent[0], w_out)
    mixed, gin, *weights = pl.pallas_call(
        hand_over,
        out_shape=(shape(512, 1024), shape(512, 1024))
        + (shape(1024, 512, kind=F32),) * 3
        + (shape(512, 1024, kind=F32),),
        in_specs=[HB] * 3,
        out_specs=(HB,) * 6,
        scratch_shapes=[vm((8, 512, 512), BF), vm((8, 512, 512), F32), DMA((8,)), DMA((8,))]
        + [vm((2, 512, 1024), BF), DMA((2,)), DMA((2,))],
        compiler_params=pltpu.CompilerParams(vmem_limit_bytes=62 * MIB),
        name="hand_over",
    )(mixed, gin, total)
    return (mixed[None], gin[None], *weights)


def solution(mesh):
    placed = (P("dp", "seq", None), P("dp", None), P(), P(), P(), P(), P("dp", "seq", None))
    return jax.shard_map(
        local,
        mesh=mesh,
        in_specs=placed,
        out_specs=(P("dp", "seq", None), P("dp", "seq", None), P(), P(), P(), P()),
        check_vma=False,
    )
```

```python
import functools
import math

import jax
import jax.numpy as jnp
from jax import lax
from jax.experimental import pallas as pl
from jax.experimental.pallas import tpu as pltpu
from jax.sharding import PartitionSpec as P

MESH = pl.DeviceIdType.MESH
BF = jnp.bfloat16
F32 = jnp.float32
HEADS = 4
TILE = 128
OFFSETS = (0, 1, 2, 4, 8, 12, 16, 24, 32)
SCALE = 1.0 / math.sqrt(128.0)
LOG2E = 1.4426950408889634
NEG = -1e30
NT = (((1,), (1,)), ((), ()))
TN = (((0,), (0,)), ((), ()))
OWN = 32 * TILE
MIB = 1024 * 1024


def place():
    s = lax.axis_index("seq")
    return lax.axis_index("dp"), lax.div(s, 8), lax.rem(lax.div(s, 2), 4), lax.rem(s, 2)


def device(y, x, z, c):
    return (y, (x * 4 + z) * 2 + c)


def turn(a, d):
    return lax.rem(a + d, 4)


def remote(src, dst, send, recv, to):
    return pltpu.make_async_remote_copy(
        src_ref=src, dst_ref=dst, send_sem=send, recv_sem=recv, device_id=to, device_id_type=MESH
    )


def all_partners(y, x, z, c):
    found = [device(y, x, z, 1 - c)]
    for d in (1, 2, 3):
        found.append(device(turn(y, d), x, z, c))
        for core in (0, 1):
            found.append(device(y, turn(x, d), z, core))
            found.append(device(y, x, turn(z, d), core))
    return found


def rows_of(start, count):
    return pl.ds(pl.multiple_of(start, TILE), count)


def whole_kernel(
    lens, tok_in, wk_in, wv_in, wq_in, cot_in, wo_in, mixed_out, gin_out, total_out,
    mixed, gin, out,
    tok, tokt, cot, wq, wk, wv, wo,
    kv, qg, summ, kvs, qgs, sums,
    kvt, gt, pair, pairt, sc, dsp, gkv, gsum, cg,
    rx, rh, gss, gsr, ret_kv, ret_cg, flat,
    wg, got0, w0, got1, w1, got2, got3,
    s_in, s_kv, r_kv, s_qg, r_qg, s_h, r_h, s_x, r_x, s_s, r_s,
    s_bkv, r_bkv, s_cg, r_cg, s_bh, r_bh, s_bx, r_bx, s_gs, r_gs,
    s0, r0, s1, r1, s2, r2,
):
    y, x, z, c = place()
    loads = []
    for n, (a, b) in enumerate(
        ((tok_in, tok), (wk_in, wk), (wv_in, wv), (wq_in, wq), (cot_in, cot), (wo_in, wo))
    ):
        copy = pltpu.make_async_copy(a, b, s_in.at[n])
        copy.start()
        loads.append(copy)
    partners = all_partners(y, x, z, c)
    barrier = pltpu.get_barrier_semaphore()
    for to in partners:
        pl.semaphore_signal(barrier, inc=1, device_id=to, device_id_type=MESH)
    other = device(y, x, z, 1 - c)
    home = lax.div(z, 2)
    at_home = c == home
    slot = lax.rem(z, 2) * 2 + c
    group = 2 * x + c

    def project(src, w, dst, lane):
        def half(i, carry):
            rows = rows_of(i * 256, 256)
            got = jnp.dot(src[rows, :], w[...], preferred_element_type=F32)
            for h in range(HEADS):
                dst[h, rows, lane : lane + TILE] = got[:, h * TILE : (h + 1) * TILE].astype(BF)
            return carry

        lax.fori_loop(0, 2, half, 0)

    def exchange(staged, landing, base, send, recv):
        spot = rows_of(base + slot * 512, 512)
        copies = []
        near = remote(staged.at[z], landing.at[spot], send.at[0], recv.at[slot], other)

        @pl.when(at_home)
        def _():
            landing[spot, :] = staged[z]

        @pl.when(jnp.logical_not(at_home))
        def _():
            near.start()

        for d in (1, 3, 2):
            h = turn(z, d)
            copy = remote(staged.at[h], landing.at[spot], send.at[d], recv.at[slot], device(y, x, h, home))
            if d != 2:
                copy.start()
            copies.append(copy)
        return copies, near

    def settle_out(copies, near):
        for copy in copies:
            copy.wait_send()

        @pl.when(jnp.logical_not(at_home))
        def _():
            near.wait_send()

    def arrived(staged, landing, base, send, recv, i):
        mine = jnp.logical_and(z == 2 * c + lax.div(i, 2), c == lax.rem(i, 2))

        @pl.when(jnp.logical_not(mine))
        def _():
            remote(
                staged.at[0], landing.at[rows_of(base + i * 512, 512)], send.at[0], recv.at[i], other
            ).wait_recv()

    for n in range(3):
        loads[n].wait()
    project(tok, wk, kvs, 0)
    project(tok, wv, kvs, TILE)
    pl.semaphore_wait(barrier, len(partners))
    kv_sent = exchange(kvs, kv, OWN, s_kv, r_kv)
    for n in range(3, 6):
        loads[n].wait()
    project(tok, wq, qgs, 0)
    first_own = ((x * 4 + z) * 2 + c) * 4

    def grads(i, carry):
        rows = rows_of(i * TILE, TILE)
        got = lax.dot_general(cot[rows, :], wo[...], NT, preferred_element_type=F32)
        live = lax.broadcasted_iota(jnp.int32, (TILE, 512), 0) < lens[0, first_own + i]
        got = jnp.where(live, got, 0.0).astype(BF)
        for h in range(HEADS):
            qgs[h, rows, TILE : 2 * TILE] = got[:, h * TILE : (h + 1) * TILE]
        return carry

    lax.fori_loop(0, 4, grads, 0)
    kv_sent[0][2].start()

    ahead = device(y, turn(x, 1), z, c)
    behind = device(y, turn(x, 3), z, c)

    def halo_copy(i):
        return remote(
            kv.at[rows_of(OWN + i * 512, 512)], kv.at[rows_of(i * 512, 512)], s_h.at[i], r_h.at[i], ahead
        )

    def across_copy(start, i):
        return remote(
            kv.at[rows_of(start + i * 512, 512)],
            kv.at[rows_of(2048 + i * 512, 512)],
            s_x.at[i],
            r_x.at[i],
            other,
        )

    nearest = lax.rem(z + jnp.where(at_home, 0, 1), 2) * 2
    order = [lax.rem(nearest + k, 4) for k in range(4)]
    for i in order:
        arrived(kvs, kv, OWN, s_kv, r_kv, i)
        halo_copy(i).start()

        @pl.when(c == 0)
        def _():
            across_copy(OWN, i).start()

    qg_sent = exchange(qgs, qg, 0, s_qg, r_qg)
    qg_sent[0][2].start()

    def summary(i, carry):
        rows = rows_of(OWN + i * TILE, TILE)
        length = lens[0, group * 16 + i]
        live = lax.broadcasted_iota(jnp.int32, (TILE, 256), 0) < length
        total = jnp.sum(jnp.where(live, kv[rows, :].astype(F32), 0.0), axis=0, keepdims=True)
        sums[pl.ds(i, 1), :] = total / jnp.full((1, 256), length, jnp.int32).astype(F32)
        return carry

    lax.fori_loop(0, 16, summary, 0)
    summ[group] = sums[...].astype(BF)
    sum_copies = []
    pairs_of = [(d, cc) for d in range(4) for cc in (0, 1) if (d, cc) != (0, 0)]
    for d, cc in pairs_of:
        n = d * 2 + cc
        core = lax.rem(c + cc, 2)
        copy = remote(summ.at[group], summ.at[group], s_s.at[n], r_s.at[n], device(y, turn(x, d), z, core))
        copy.start()
        sum_copies.append(copy)

    def prepare(b, carry):
        rows = rows_of(b * TILE, TILE)
        kvt[:, rows] = jnp.transpose(kv[rows, :])
        return carry

    def clear(b, carry):
        gkv[rows_of(b * TILE, TILE), :] = jnp.zeros((TILE, 256), F32)
        return carry

    lax.fori_loop(0, 48, clear, 0)
    gsum[...] = jnp.zeros_like(gsum)
    for u in range(UNROLL):
        pair[u] = jnp.zeros((256, 256), BF)
        pairt[u] = jnp.zeros((256, 256), BF)
    lax.fori_loop(32, 48, prepare, 0)

    def turned(i, carry):
        cols = rows_of(i * TILE, TILE)
        tokt[cols, :] = jnp.transpose(tok[:, cols])
        return carry

    lax.fori_loop(0, 8, turned, 0)
    for i in order:
        halo_copy(i).wait_recv()

        @pl.when(c == 1)
        def _():
            across_copy(0, i).start()

    lax.fori_loop(0, 16, prepare, 0)
    for i in range(4):
        across_copy(0, i).wait()
        halo_copy(i).wait_send()
        arrived(qgs, qg, 0, s_qg, r_qg, i)
    lax.fori_loop(16, 32, prepare, 0)
    for copy in sum_copies:
        copy.wait()
    kvt[:, 48 * TILE : 49 * TILE] = jnp.transpose(summ[...].reshape(TILE, 256))
    settle_out(*kv_sent)
    settle_out(*qg_sent)

    key_slot = lax.broadcasted_iota(jnp.int32, (TILE, TILE), 0)
    query_slot = lax.broadcasted_iota(jnp.int32, (TILE, TILE), 1)
    count = len(OFFSETS)

    def bar(it, carry):
        ids = [it * UNROLL + u for u in range(UNROLL)]
        tops, scales, deltas = [], [], []
        for u, qb in enumerate(ids):
            rows = rows_of(qb * TILE, TILE)
            pair[u, 0:TILE, 0:TILE] = qg[rows, 0:TILE]
            pair[u, TILE:, TILE:] = qg[rows, TILE:]
            pairt[u, 0:TILE, 0:TILE] = jnp.transpose(qg[rows, 0:TILE])
            pairt[u, TILE:, TILE:] = jnp.transpose(qg[rows, TILE:])
            both = pairt[u]
            this = 16 * group + qb
            top = None
            for j in range(count + 1):
                here = slice(j * TILE, (j + 1) * TILE)
                if j < count:
                    spot = rows_of((32 + qb - OFFSETS[j]) * TILE, TILE)
                    bar_id = this - OFFSETS[j]
                    length = jnp.where(bar_id >= 0, lens[0, jnp.maximum(bar_id, 0)], 0)
                    source = kv[spot, :]
                    gt[u, :, here] = kvt[:, spot]
                    ok = key_slot < length
                    if j == 0:
                        ok = jnp.logical_and(ok, key_slot <= query_slot)
                else:
                    source = summ[...].reshape(TILE, 256)
                    gt[u, :, here] = kvt[:, 48 * TILE : 49 * TILE]
                    distance = this - key_slot
                    ok = distance >= 1
                    for o in OFFSETS[1:]:
                        ok = jnp.logical_and(ok, distance != o)
                got = jnp.dot(source, both, preferred_element_type=F32)
                score = jnp.where(ok, got[:, :TILE] * (SCALE * LOG2E), NEG)
                sc[u, here, :TILE] = score
                sc[u, here, TILE:] = got[:, TILE:]
                high = jnp.max(score, axis=0, keepdims=True)
                top = high if top is None else jnp.maximum(top, high)
            tops.append(top)
        for u in range(UNROLL):
            total = jnp.zeros((1, TILE), F32)
            weighted = jnp.zeros((1, TILE), F32)
            for j in range(count + 1):
                here = slice(j * TILE, (j + 1) * TILE)
                e = jnp.exp2(sc[u, here, :TILE] - tops[u])
                sc[u, here, :TILE] = e
                total = total + jnp.sum(e, axis=0, keepdims=True)
                weighted = weighted + jnp.sum(e * sc[u, here, TILE:], axis=0, keepdims=True)
            scales.append(1.0 / total)
            deltas.append(weighted * scales[u])
        for u, qb in enumerate(ids):
            rows = rows_of(qb * TILE, TILE)
            both = pair[u]
            for j in range(count + 1):
                here = slice(j * TILE, (j + 1) * TILE)
                p = sc[u, here, :TILE] * scales[u]
                ds = (p * (sc[u, here, TILE:] - deltas[u])).astype(BF)
                block = jnp.concatenate([ds, p.astype(BF)], axis=1)
                dsp[u, here, :] = block
                got = jnp.dot(block, both, preferred_element_type=F32)
                if j < count:
                    spot = rows_of((32 + qb - OFFSETS[j]) * TILE, TILE)
                    gkv[spot, :] += got
                else:
                    gsum[...] += got
            both_out = jnp.dot(gt[u], dsp[u], preferred_element_type=F32)
            cg[rows, 0:TILE] = jnp.transpose(both_out[:TILE, :TILE] * SCALE).astype(BF)
            context = jnp.transpose(both_out[TILE:, TILE:])
            cg[rows, TILE:] = jnp.where(key_slot < lens[0, 16 * group + qb], context, 0.0).astype(BF)
        return carry

    def owner(i):
        to_z = 2 * c + lax.div(i, 2)
        core = lax.rem(i, 2)
        mine = jnp.logical_and(z == to_z, c == core)
        return device(y, x, to_z, core), mine

    def give_back(src, landing, send, recv, i):
        to, mine = owner(i)
        rows = rows_of(i * 512, 512)

        @pl.when(mine)
        def _():
            landing[z] = src[rows, :]

        @pl.when(jnp.logical_not(mine))
        def _():
            remote(src.at[rows], landing.at[z], send.at[i], recv.at[z], to).start()

    def settle(src, landing, send, recv):
        for i in range(4):
            to, mine = owner(i)

            @pl.when(jnp.logical_not(mine))
            def _():
                remote(src.at[pl.ds(i * 512, 512)], landing.at[z], send.at[i], recv.at[z], to).wait_send()

    def returned(src, landing, send, recv):
        for h in range(HEADS):
            mine = jnp.logical_and(z == h, at_home)

            @pl.when(jnp.logical_not(mine))
            def _():
                remote(src.at[pl.ds(0, 512)], landing.at[h], send.at[0], recv.at[h], other).wait_recv()

    def crossing(i):
        rows = rows_of(i * 512, 512)
        return remote(kvs.at[i], rx.at[rows], s_bx.at[i], r_bx.at[i], other)

    def cross(i):
        kvs[i] = gkv[rows_of(2048 + i * 512, 512), :].astype(BF)
        crossing(i).start()

    def halo_back(i):
        rows = rows_of(i * 512, 512)
        return remote(qgs.at[i], rh.at[rows], s_bh.at[i], r_bh.at[i], behind)

    def core_one(i):
        @pl.when(c == 1)
        def _():
            rows = pl.ds(i * 512, 512)
            qgs[i] = (gkv[rows, :] + rx[rows, :].astype(F32)).astype(BF)
            halo_back(i).start()

    def chunk(step, carry):
        i = jnp.where(step == 1, 2, jnp.where(step == 2, 1, step))
        lax.fori_loop(0, 4 // UNROLL, lambda u, kept: bar(i * (4 // UNROLL) + u, kept), 0)

        @pl.when(c == 0)
        def _():
            rows = rows_of(i * 512, 512)
            qgs[i] = gkv[rows, :].astype(BF)
            halo_back(i).start()

        @pl.when(step == 1)
        def _():
            cross(0)

        @pl.when(step == 2)
        def _():
            cross(2)
            crossing(0).wait_recv()
            core_one(0)

        give_back(cg, ret_cg, s_cg, r_cg, i)
        return carry

    lax.fori_loop(0, 4, chunk, 0)
    cross(1)
    cross(3)
    gss[...] = gsum[...].astype(BF).reshape(8, 16, 256)
    gsr[group] = gss[group]
    back_copies = []
    for d, cc in pairs_of:
        n = d * 2 + cc
        to_x, core = turn(x, d), lax.rem(c + cc, 2)
        copy = remote(
            gss.at[to_x * 2 + core], gsr.at[group], s_gs.at[n], r_gs.at[n], device(y, to_x, z, core)
        )
        copy.start()
        back_copies.append(copy)
    turns = (0, 2, 1, 3)
    for i in turns[1:]:
        crossing(i).wait_recv()
        core_one(i)

    def flatten(src, lane, n):
        for h in range(HEADS):
            flat[n, :, h * TILE : (h + 1) * TILE] = src[h, :, lane : lane + TILE]

    where = {"y": y, "x": x, "z": z}
    levels = ((w0, got1, 256), (w1, got2, 64))
    pending = [None] * 4
    started = []
    last = []

    def along(axis, d):
        at = dict(where)
        at[axis] = turn(where[axis], d)
        return device(at["y"], at["x"], at["z"], c)

    def core_half(m):
        return remote(wg.at[m, 1 - c], got0.at[m], s0.at[0, m], r0.at[0, m], other)

    def send_level(m, level):
        src, got, size = levels[level]
        copies = []
        axis = ORDERS[m][level]
        for d in (1, 2, 3):
            piece = pl.ds(pl.multiple_of(turn(where[axis], d) * size, 16), size)
            copy = remote(
                src.at[m, piece], got.at[m, d - 1], s1.at[level, m, d - 1], r1.at[level, m, d - 1], along(axis, d)
            )
            copy.start()
            copies.append(copy)
        pending[m] = copies
        started.extend(copies)

    def place_rows(m, level):
        start = where[ORDERS[m][0]] * 256
        if level == 1:
            start = start + where[ORDERS[m][1]] * 64
        return pl.ds(pl.multiple_of(start, 16), levels[level][2])

    half = pl.ds(pl.multiple_of(c * 256, 256), 256)

    def give(m, level):
        block = out.at[m, place_rows(m, level), half]
        copies = []
        for d in (1, 2, 3):
            copy = remote(
                block, block, s2.at[level, m, d - 1], r2.at[level, m, d - 1], along(ORDERS[m][level], d)
            )
            copy.start()
            copies.append(copy)
        pending[m] = copies
        started.extend(copies)

    def settled(m):
        for copy in pending[m]:
            copy.wait_recv()

    def begin(m):
        core_half(m).wait_recv()

        def add(i, carry):
            rows = rows_of(i * 256, 256)
            w0[m, rows, :] = (wg[m, c, rows, :].astype(F32) + got0[m, rows, :].astype(F32)).astype(BF)
            return carry

        lax.fori_loop(0, 4, add, 0)
        send_level(m, 0)

    def advance(m, level):
        settled(m)
        if level == 2:
            total = got3[m, 0].astype(F32)
            for n in range(1, 4):
                total = total + got3[m, n].astype(F32)
            out[m, place_rows(m, 1), half] = total.astype(BF)
            give(m, 1)
            return
        src, got, size = levels[level]
        mine = pl.ds(pl.multiple_of(where[ORDERS[m][level]] * size, 16), size)
        total = src[m, mine, :].astype(F32)
        for n in range(3):
            total = total + got[m, n].astype(F32)
        if level == 0:
            w1[m] = total.astype(BF)
            send_level(m, 1)
        else:
            axis = ORDERS[m][2]
            got3[m, where[axis]] = total.astype(BF)
            block = got3.at[m, where[axis]]
            copies = []
            for d in (1, 2, 3):
                copy = remote(block, block, s1.at[2, m, d - 1], r1.at[2, m, d - 1], along(axis, d))
                copy.start()
                copies.append(copy)
            pending[m] = copies
            started.extend(copies)

    def finish(m):
        settled(m)
        copy = remote(out.at[m, :, half], out.at[m, :, half], s0.at[1, m], r0.at[1, m], other)
        copy.start()
        last.append(copy)

    def weight_grad(n, m):
        def part(i, carry):
            cols = rows_of(i * 256, 256)
            got = jnp.dot(tokt[cols, :], flat[n], preferred_element_type=F32).astype(BF)
            wg[m, 0, cols, :] = got[:, :256]
            wg[m, 1, cols, :] = got[:, 256:]
            return carry

        lax.fori_loop(0, 4, part, 0)
        core_half(m).start()

    returned(cg, ret_cg, s_cg, r_cg)
    flatten(ret_cg, 0, 0)
    weight_grad(0, 0)
    flatten(ret_cg, TILE, 3)

    def out_grad(i, carry):
        cols = rows_of(i * 256, 256)
        got = lax.dot_general(flat[3], cot[:, cols], TN, preferred_element_type=F32).astype(BF)
        wg[3, lax.rem(i, 2), rows_of(lax.div(i, 2) * 512, 512), :] = got
        return carry

    lax.fori_loop(0, 4, out_grad, 0)
    core_half(3).start()
    begin(0)

    for copy in back_copies:
        copy.wait()
    coarse = gsr[0].astype(F32)
    for n in range(1, 8):
        coarse = coarse + gsr[n].astype(F32)
    lane = lax.broadcasted_iota(jnp.int32, (1, 256), 1)
    factor = jnp.where(lane < TILE, SCALE, 1.0)
    for i in turns:
        halo_back(i).wait_recv()
        for b in range(4 * i, 4 * i + 4):
            rows = pl.ds(b * TILE, TILE)
            length = lens[0, group * 16 + b]
            live = lax.broadcasted_iota(jnp.int32, (TILE, 256), 0) < length
            share = coarse[b : b + 1, :] * (1.0 / jnp.full((1, 256), length, jnp.int32).astype(F32))
            extra = jnp.where(c == 0, rx[rows, :].astype(F32), 0.0)
            total = gkv[pl.ds(OWN + b * TILE, TILE), :] + rh[rows, :].astype(F32) + extra
            qg[rows, :] = ((total + jnp.where(live, share, 0.0)) * factor).astype(BF)
        give_back(qg, ret_kv, s_bkv, r_bkv, i)

    begin(3)

    def mix(i, carry):
        rows = rows_of(i * 256, 256)
        mixed[rows, :] = jnp.dot(flat[3, rows, :], wo[...], preferred_element_type=F32).astype(BF)
        return carry

    lax.fori_loop(0, 2, mix, 0)
    mixed_written = pltpu.make_async_copy(mixed, mixed_out, s_in.at[0])
    mixed_written.start()
    advance(0, 0)
    advance(0, 1)
    advance(3, 0)
    returned(qg, ret_kv, s_bkv, r_bkv)
    flatten(ret_kv, 0, 1)
    weight_grad(1, 1)
    flatten(ret_kv, TILE, 2)
    weight_grad(2, 2)
    advance(0, 2)
    advance(3, 1)
    begin(1)
    begin(2)

    def back(i, carry):
        rows = rows_of(i * 256, 256)
        total = lax.dot_general(flat[0, rows, :], wq[...], NT, preferred_element_type=F32)
        total = total + lax.dot_general(flat[1, rows, :], wk[...], NT, preferred_element_type=F32)
        total = total + lax.dot_general(flat[2, rows, :], wv[...], NT, preferred_element_type=F32)
        gin[rows, :] = total.astype(BF)
        return carry

    lax.fori_loop(0, 2, back, 0)
    gin_written = pltpu.make_async_copy(gin, gin_out, s_in.at[1])
    gin_written.start()
    advance(3, 2)
    for m in (0, 3):
        settled(m)
        give(m, 0)
    for level in range(3):
        advance(1, level)
        advance(2, level)
    finish(0)
    finish(3)
    for m in (1, 2):
        settled(m)
        give(m, 0)
    for n in range(2):
        last[n].wait()
    written = [pltpu.make_async_copy(out.at[m], total_out.at[m], s_in.at[2 + m]) for m in range(4)]
    written[0].start()
    written[3].start()
    finish(1)
    finish(2)
    for n in (2, 3):
        last[n].wait()
        written[n - 1].start()
    mixed_written.wait()
    gin_written.wait()
    for copy in written:
        copy.wait()
    for m in range(4):
        core_half(m).wait_send()
        crossing(m).wait_send()
        halo_back(m).wait_send()
    for copy in started:
        copy.wait_send()
    settle(cg, ret_cg, s_cg, r_cg)
    settle(qg, ret_kv, s_bkv, r_bkv)


def hand_over(mixed, gin, total, *refs):
    mixed_out, gin_out, outs = refs[0], refs[1], refs[2:6]
    narrow, wide, s_in, s_out, kept, s_kept, s_pass = refs[6:]
    halves = [pl.ds(0, 512), pl.ds(512, 512)]
    held = [
        pltpu.make_async_copy(src, kept.at[n], s_kept.at[n]) for n, src in enumerate((mixed, gin))
    ]
    passed = [
        pltpu.make_async_copy(kept.at[n], dst, s_pass.at[n])
        for n, dst in enumerate((mixed_out, gin_out))
    ]
    loads = [
        pltpu.make_async_copy(total.at[n // 2, halves[n % 2]], narrow.at[n], s_in.at[n]) for n in range(8)
    ]
    for copy in loads + held:
        copy.start()
    stores = []
    for n in range(8):
        loads[n].wait()
        wide[n] = narrow[n].astype(F32)
        to = outs[3].at[:, halves[n % 2]] if n >= 6 else outs[n // 2].at[halves[n % 2]]
        stores.append(pltpu.make_async_copy(wide.at[n], to, s_out.at[n]))
        stores[n].start()
    for n in range(2):
        held[n].wait()
        passed[n].start()
    for copy in stores + passed:
        copy.wait()


ORDERS = ("yxz", "zyx", "xzy", "xyz")
UNROLL = 4

HB = pl.BlockSpec(memory_space=pl.ANY)
VM = pl.BlockSpec(memory_space=pltpu.VMEM)
SM = pl.BlockSpec(memory_space=pltpu.SMEM)
DMA = pltpu.SemaphoreType.DMA


def shape(*dims, kind=BF):
    return jax.ShapeDtypeStruct(dims, kind)


def local(tokens, lengths, w_query, w_key, w_value, w_out, cotangent):
    vm = pltpu.VMEM
    slabs = lambda n: [vm((2048, 256), BF)] * n
    heads = lambda n: [vm((4, 512, 256), BF)] * n
    mixed, gin, total = pl.pallas_call(
        whole_kernel,
        out_shape=(shape(512, 1024), shape(512, 1024), shape(4, 1024, 512)),
        in_specs=[SM] + [HB] * 6,
        out_specs=(HB, HB, HB),
        scratch_shapes=[vm((512, 1024), BF), vm((512, 1024), BF), vm((4, 1024, 512), BF)]
        + [vm((512, 1024), BF), vm((1024, 512), BF), vm((512, 1024), BF)]
        + [vm((1024, 512), BF)] * 3
        + [vm((512, 1024), BF), vm((6144, 256), BF)]
        + slabs(1)
        + [vm((8, 16, 256), BF)]
        + heads(2)
        + [vm((16, 256), F32)]
        + [
            vm((256, 49 * TILE), BF),
            vm((UNROLL, 256, 10 * TILE), BF),
            vm((UNROLL, 256, 256), BF),
            vm((UNROLL, 256, 256), BF),
            vm((UNROLL, 10 * TILE, 256), F32),
            vm((UNROLL, 10 * TILE, 256), BF),
            vm((6144, 256), F32),
            vm((128, 256), F32),
        ]
        + slabs(3)
        + [vm((8, 16, 256), BF)] * 2
        + heads(2)
        + [
            vm((4, 512, 512), BF),
            vm((4, 2, 1024, 256), BF),
            vm((4, 1024, 256), BF),
            vm((4, 1024, 256), BF),
            vm((4, 3, 256, 256), BF),
            vm((4, 256, 256), BF),
            vm((4, 3, 64, 256), BF),
            vm((4, 4, 64, 256), BF),
        ]
        + [DMA((6,))]
        + [DMA((4,))] * 8
        + [DMA((8,))] * 2
        + [DMA((4,))] * 8
        + [DMA((8,))] * 2
        + [DMA((2, 4))] * 2
        + [DMA((3, 4, 3))] * 2
        + [DMA((2, 4, 3))] * 2,
        compiler_params=pltpu.CompilerParams(
            collective_id=0, has_side_effects=True, vmem_limit_bytes=62 * MIB
        ),
        name="whole",
    )(lengths, tokens[0], w_key, w_value, w_query, cotangent[0], w_out)
    mixed, gin, *weights = pl.pallas_call(
        hand_over,
        out_shape=(shape(512, 1024), shape(512, 1024))
        + (shape(1024, 512, kind=F32),) * 3
        + (shape(512, 1024, kind=F32),),
        in_specs=[HB] * 3,
        out_specs=(HB,) * 6,
        scratch_shapes=[vm((8, 512, 512), BF), vm((8, 512, 512), F32), DMA((8,)), DMA((8,))]
        + [vm((2, 512, 1024), BF), DMA((2,)), DMA((2,))],
        compiler_params=pltpu.CompilerParams(vmem_limit_bytes=62 * MIB),
        name="hand_over",
    )(mixed, gin, total)
    return (mixed[None], gin[None], *weights)


def solution(mesh):
    placed = (P("dp", "seq", None), P("dp", None), P(), P(), P(), P(), P("dp", "seq", None))
    return jax.shard_map(
        local,
        mesh=mesh,
        in_specs=placed,
        out_specs=(P("dp", "seq", None), P("dp", "seq", None), P(), P(), P(), P()),
        check_vma=False,
    )
```

```python
import functools
import math

import jax
import jax.numpy as jnp
from jax import lax
from jax.experimental import pallas as pl
from jax.experimental.pallas import tpu as pltpu
from jax.sharding import PartitionSpec as P

MESH = pl.DeviceIdType.MESH
BF = jnp.bfloat16
F32 = jnp.float32
HEADS = 4
TILE = 128
OFFSETS = (0, 1, 2, 4, 8, 12, 16, 24, 32)
SCALE = 1.0 / math.sqrt(128.0)
LOG2E = 1.4426950408889634
NEG = -1e30
NT = (((1,), (1,)), ((), ()))
TN = (((0,), (0,)), ((), ()))
OWN = 32 * TILE
MIB = 1024 * 1024


def place():
    s = lax.axis_index("seq")
    return lax.axis_index("dp"), lax.div(s, 8), lax.rem(lax.div(s, 2), 4), lax.rem(s, 2)


def device(y, x, z, c):
    return (y, (x * 4 + z) * 2 + c)


def turn(a, d):
    return lax.rem(a + d, 4)


def remote(src, dst, send, recv, to):
    return pltpu.make_async_remote_copy(
        src_ref=src, dst_ref=dst, send_sem=send, recv_sem=recv, device_id=to, device_id_type=MESH
    )


def all_partners(y, x, z, c):
    found = [device(y, x, z, 1 - c)]
    for d in (1, 2, 3):
        found.append(device(turn(y, d), x, z, c))
        for core in (0, 1):
            found.append(device(y, turn(x, d), z, core))
            found.append(device(y, x, turn(z, d), core))
    return found


def rows_of(start, count):
    return pl.ds(pl.multiple_of(start, TILE), count)


def whole_kernel(
    lens, tok_in, wk_in, wv_in, wq_in, cot_in, wo_in, mixed_out, gin_out, total_out,
    mixed, gin, out,
    tok, tokt, cot, wq, wk, wv, wo,
    kv, qg, summ, kvs, qgs, sums,
    kvt, gt, pair, pairt, sc, dsp, gkv, gsum, cg,
    rx, rh, gss, gsr, ret_kv, ret_cg, flat,
    wg, got0, w0, got1, w1, got2, got3,
    s_in, s_kv, r_kv, s_qg, r_qg, s_h, r_h, s_x, r_x, s_s, r_s,
    s_bkv, r_bkv, s_cg, r_cg, s_bh, r_bh, s_bx, r_bx, s_gs, r_gs,
    s0, r0, s1, r1, s2, r2,
):
    y, x, z, c = place()
    loads = []
    for n, (a, b) in enumerate(
        ((tok_in, tok), (wk_in, wk), (wv_in, wv), (wq_in, wq), (cot_in, cot), (wo_in, wo))
    ):
        copy = pltpu.make_async_copy(a, b, s_in.at[n])
        copy.start()
        loads.append(copy)
    partners = all_partners(y, x, z, c)
    barrier = pltpu.get_barrier_semaphore()
    for to in partners:
        pl.semaphore_signal(barrier, inc=1, device_id=to, device_id_type=MESH)
    other = device(y, x, z, 1 - c)
    home = lax.div(z, 2)
    at_home = c == home
    slot = lax.rem(z, 2) * 2 + c
    group = 2 * x + c

    def project(src, w, dst, lane):
        def half(i, carry):
            rows = rows_of(i * 256, 256)
            got = jnp.dot(src[rows, :], w[...], preferred_element_type=F32)
            for h in range(HEADS):
                dst[h, rows, lane : lane + TILE] = got[:, h * TILE : (h + 1) * TILE].astype(BF)
            return carry

        lax.fori_loop(0, 2, half, 0)

    def exchange(staged, landing, base, send, recv):
        spot = rows_of(base + slot * 512, 512)
        copies = []
        near = remote(staged.at[z], landing.at[spot], send.at[0], recv.at[slot], other)

        @pl.when(at_home)
        def _():
            landing[spot, :] = staged[z]

        @pl.when(jnp.logical_not(at_home))
        def _():
            near.start()

        for d in (1, 3, 2):
            h = turn(z, d)
            copy = remote(staged.at[h], landing.at[spot], send.at[d], recv.at[slot], device(y, x, h, home))
            if d != 2:
                copy.start()
            copies.append(copy)
        return copies, near

    def settle_out(copies, near):
        for copy in copies:
            copy.wait_send()

        @pl.when(jnp.logical_not(at_home))
        def _():
            near.wait_send()

    def arrived(staged, landing, base, send, recv, i):
        mine = jnp.logical_and(z == 2 * c + lax.div(i, 2), c == lax.rem(i, 2))

        @pl.when(jnp.logical_not(mine))
        def _():
            remote(
                staged.at[0], landing.at[rows_of(base + i * 512, 512)], send.at[0], recv.at[i], other
            ).wait_recv()

    for n in range(3):
        loads[n].wait()
    project(tok, wk, kvs, 0)
    project(tok, wv, kvs, TILE)
    pl.semaphore_wait(barrier, len(partners))
    kv_sent = exchange(kvs, kv, OWN, s_kv, r_kv)
    for n in range(3, 6):
        loads[n].wait()
    project(tok, wq, qgs, 0)
    first_own = ((x * 4 + z) * 2 + c) * 4

    def grads(i, carry):
        rows = rows_of(i * TILE, TILE)
        got = lax.dot_general(cot[rows, :], wo[...], NT, preferred_element_type=F32)
        live = lax.broadcasted_iota(jnp.int32, (TILE, 512), 0) < lens[0, first_own + i]
        got = jnp.where(live, got, 0.0).astype(BF)
        for h in range(HEADS):
            qgs[h, rows, TILE : 2 * TILE] = got[:, h * TILE : (h + 1) * TILE]
        return carry

    lax.fori_loop(0, 4, grads, 0)
    kv_sent[0][2].start()

    ahead = device(y, turn(x, 1), z, c)
    behind = device(y, turn(x, 3), z, c)

    def halo_copy(i):
        return remote(
            kv.at[rows_of(OWN + i * 512, 512)], kv.at[rows_of(i * 512, 512)], s_h.at[i], r_h.at[i], ahead
        )

    def across_copy(start, i):
        return remote(
            kv.at[rows_of(start + i * 512, 512)],
            kv.at[rows_of(2048 + i * 512, 512)],
            s_x.at[i],
            r_x.at[i],
            other,
        )

    nearest = lax.rem(z + jnp.where(at_home, 0, 1), 2) * 2
    order = [lax.rem(nearest + k, 4) for k in range(4)]
    for i in order:
        arrived(kvs, kv, OWN, s_kv, r_kv, i)
        halo_copy(i).start()

        @pl.when(c == 0)
        def _():
            across_copy(OWN, i).start()

    qg_sent = exchange(qgs, qg, 0, s_qg, r_qg)
    qg_sent[0][2].start()

    def summary(i, carry):
        rows = rows_of(OWN + i * TILE, TILE)
        length = lens[0, group * 16 + i]
        live = lax.broadcasted_iota(jnp.int32, (TILE, 256), 0) < length
        total = jnp.sum(jnp.where(live, kv[rows, :].astype(F32), 0.0), axis=0, keepdims=True)
        sums[pl.ds(i, 1), :] = total / jnp.full((1, 256), length, jnp.int32).astype(F32)
        return carry

    lax.fori_loop(0, 16, summary, 0)
    summ[group] = sums[...].astype(BF)
    sum_copies = []
    pairs_of = [(d, cc) for d in range(4) for cc in (0, 1) if (d, cc) != (0, 0)]
    for d, cc in pairs_of:
        n = d * 2 + cc
        core = lax.rem(c + cc, 2)
        copy = remote(summ.at[group], summ.at[group], s_s.at[n], r_s.at[n], device(y, turn(x, d), z, core))
        copy.start()
        sum_copies.append(copy)

    def prepare(b, carry):
        rows = rows_of(b * TILE, TILE)
        kvt[:, rows] = jnp.transpose(kv[rows, :])
        return carry

    def clear(b, carry):
        gkv[rows_of(b * TILE, TILE), :] = jnp.zeros((TILE, 256), F32)
        return carry

    lax.fori_loop(0, 48, clear, 0)
    gsum[...] = jnp.zeros_like(gsum)
    for u in range(UNROLL):
        pair[u] = jnp.zeros((256, 256), BF)
        pairt[u] = jnp.zeros((256, 256), BF)
    lax.fori_loop(32, 48, prepare, 0)

    def turned(i, carry):
        cols = rows_of(i * TILE, TILE)
        tokt[cols, :] = jnp.transpose(tok[:, cols])
        return carry

    lax.fori_loop(0, 8, turned, 0)
    for i in order:
        halo_copy(i).wait_recv()

        @pl.when(c == 1)
        def _():
            across_copy(0, i).start()

        lax.fori_loop(i * 4, i * 4 + 4, prepare, 0)

    for i in range(4):
        arrived(qgs, qg, 0, s_qg, r_qg, i)
    for i in order:
        across_copy(0, i).wait_recv()
        lax.fori_loop(16 + i * 4, 20 + i * 4, prepare, 0)
    for i in range(4):
        across_copy(0, i).wait_send()
        halo_copy(i).wait_send()
    for copy in sum_copies:
        copy.wait()
    kvt[:, 48 * TILE : 49 * TILE] = jnp.transpose(summ[...].reshape(TILE, 256))
    settle_out(*kv_sent)
    settle_out(*qg_sent)

    key_slot = lax.broadcasted_iota(jnp.int32, (TILE, TILE), 0)
    query_slot = lax.broadcasted_iota(jnp.int32, (TILE, TILE), 1)
    count = len(OFFSETS)

    def bar(it, carry):
        ids = [it * UNROLL + u for u in range(UNROLL)]
        tops, scales, deltas = [], [], []
        for u, qb in enumerate(ids):
            rows = rows_of(qb * TILE, TILE)
            pair[u, 0:TILE, 0:TILE] = qg[rows, 0:TILE]
            pair[u, TILE:, TILE:] = qg[rows, TILE:]
            pairt[u, 0:TILE, 0:TILE] = jnp.transpose(qg[rows, 0:TILE])
            pairt[u, TILE:, TILE:] = jnp.transpose(qg[rows, TILE:])
            both = pairt[u]
            this = 16 * group + qb
            top = None
            for j in range(count + 1):
                here = slice(j * TILE, (j + 1) * TILE)
                if j < count:
                    spot = rows_of((32 + qb - OFFSETS[j]) * TILE, TILE)
                    bar_id = this - OFFSETS[j]
                    length = jnp.where(bar_id >= 0, lens[0, jnp.maximum(bar_id, 0)], 0)
                    source = kv[spot, :]
                    gt[u, :, here] = kvt[:, spot]
                    ok = key_slot < length
                    if j == 0:
                        ok = jnp.logical_and(ok, key_slot <= query_slot)
                else:
                    source = summ[...].reshape(TILE, 256)
                    gt[u, :, here] = kvt[:, 48 * TILE : 49 * TILE]
                    distance = this - key_slot
                    ok = distance >= 1
                    for o in OFFSETS[1:]:
                        ok = jnp.logical_and(ok, distance != o)
                got = jnp.dot(source, both, preferred_element_type=F32)
                score = jnp.where(ok, got[:, :TILE] * (SCALE * LOG2E), NEG)
                sc[u, here, :TILE] = score
                sc[u, here, TILE:] = got[:, TILE:]
                high = jnp.max(score, axis=0, keepdims=True)
                top = high if top is None else jnp.maximum(top, high)
            tops.append(top)
        for u in range(UNROLL):
            total = jnp.zeros((1, TILE), F32)
            weighted = jnp.zeros((1, TILE), F32)
            for j in range(count + 1):
                here = slice(j * TILE, (j + 1) * TILE)
                e = jnp.exp2(sc[u, here, :TILE] - tops[u])
                total = total + jnp.sum(e, axis=0, keepdims=True)
                weighted = weighted + jnp.sum(e * sc[u, here, TILE:], axis=0, keepdims=True)
            scales.append(tops[u] + jnp.log(total) * LOG2E)
            deltas.append(weighted / total)
        for u, qb in enumerate(ids):
            rows = rows_of(qb * TILE, TILE)
            both = pair[u]
            for j in range(count + 1):
                here = slice(j * TILE, (j + 1) * TILE)
                p = jnp.exp2(sc[u, here, :TILE] - scales[u])
                ds = (p * (sc[u, here, TILE:] - deltas[u])).astype(BF)
                block = jnp.concatenate([ds, p.astype(BF)], axis=1)
                dsp[u, here, :] = block
                got = jnp.dot(block, both, preferred_element_type=F32)
                if j < count:
                    spot = rows_of((32 + qb - OFFSETS[j]) * TILE, TILE)
                    gkv[spot, :] += got
                else:
                    gsum[...] += got
            both_out = jnp.dot(gt[u], dsp[u], preferred_element_type=F32)
            cg[rows, 0:TILE] = jnp.transpose(both_out[:TILE, :TILE] * SCALE).astype(BF)
            context = jnp.transpose(both_out[TILE:, TILE:])
            cg[rows, TILE:] = jnp.where(key_slot < lens[0, 16 * group + qb], context, 0.0).astype(BF)
        return carry

    def owner(i):
        to_z = 2 * c + lax.div(i, 2)
        core = lax.rem(i, 2)
        mine = jnp.logical_and(z == to_z, c == core)
        return device(y, x, to_z, core), mine

    def give_back(src, landing, send, recv, i):
        to, mine = owner(i)
        rows = rows_of(i * 512, 512)

        @pl.when(mine)
        def _():
            landing[z] = src[rows, :]

        @pl.when(jnp.logical_not(mine))
        def _():
            remote(src.at[rows], landing.at[z], send.at[i], recv.at[z], to).start()

    def settle(src, landing, send, recv):
        for i in range(4):
            to, mine = owner(i)

            @pl.when(jnp.logical_not(mine))
            def _():
                remote(src.at[pl.ds(i * 512, 512)], landing.at[z], send.at[i], recv.at[z], to).wait_send()

    def returned(src, landing, send, recv):
        for h in range(HEADS):
            mine = jnp.logical_and(z == h, at_home)

            @pl.when(jnp.logical_not(mine))
            def _():
                remote(src.at[pl.ds(0, 512)], landing.at[h], send.at[0], recv.at[h], other).wait_recv()

    def half_copy(i, h, to):
        part = pl.ds(h * 256, 256)
        return remote(
            qg.at[pl.ds(i * 512 + h * 256, 256)], ret_kv.at[z, part], s_bkv.at[i, h], r_bkv.at[z, h], to
        )

    def give_half(i, h):
        to, mine = owner(i)

        @pl.when(mine)
        def _():
            ret_kv[z, h * 256 : h * 256 + 256] = qg[i * 512 + h * 256 : i * 512 + h * 256 + 256, :]

        @pl.when(jnp.logical_not(mine))
        def _():
            half_copy(i, h, to).start()

    def settle_halves():
        for i in range(4):
            to, mine = owner(i)

            @pl.when(jnp.logical_not(mine))
            def _():
                for h in (0, 1):
                    half_copy(i, h, to).wait_send()

    def returned_halves():
        part = [pl.ds(0, 256), pl.ds(256, 256)]
        for n in range(HEADS):
            mine = jnp.logical_and(z == n, at_home)

            @pl.when(jnp.logical_not(mine))
            def _():
                for h in (0, 1):
                    remote(
                        qg.at[part[0]], ret_kv.at[n, part[h]], s_bkv.at[0, h], r_bkv.at[n, h], other
                    ).wait_recv()

    def crossing(i):
        rows = rows_of(i * 512, 512)
        return remote(kvs.at[i], rx.at[rows], s_bx.at[i], r_bx.at[i], other)

    def cross(i):
        kvs[i] = gkv[rows_of(2048 + i * 512, 512), :].astype(BF)
        crossing(i).start()

    def halo_back(i, h):
        part = pl.ds(h * 256, 256)
        rows = rows_of(i * 512 + h * 256, 256)
        return remote(qgs.at[i, part], rh.at[rows], s_bh.at[i, h], r_bh.at[i, h], behind)

    def core_one(i):
        @pl.when(c == 1)
        def _():
            rows = pl.ds(i * 512, 512)
            qgs[i] = (gkv[rows, :] + rx[rows, :].astype(F32)).astype(BF)
            for h in (0, 1):
                halo_back(i, h).start()

    def chunk(step, carry):
        i = jnp.where(step == 1, 2, jnp.where(step == 2, 1, step))
        lax.fori_loop(0, 4 // UNROLL, lambda u, kept: bar(i * (4 // UNROLL) + u, kept), 0)

        @pl.when(c == 0)
        def _():
            rows = rows_of(i * 512, 512)
            qgs[i] = gkv[rows, :].astype(BF)
            for h in (0, 1):
                halo_back(i, h).start()

        @pl.when(step == 1)
        def _():
            cross(0)

        @pl.when(step == 2)
        def _():
            cross(2)
            crossing(0).wait_recv()
            core_one(0)

        give_back(cg, ret_cg, s_cg, r_cg, i)
        return carry

    lax.fori_loop(0, 4, chunk, 0)
    cross(1)
    cross(3)
    gss[...] = gsum[...].astype(BF).reshape(8, 16, 256)
    gsr[group] = gss[group]
    back_copies = []
    for d, cc in pairs_of:
        n = d * 2 + cc
        to_x, core = turn(x, d), lax.rem(c + cc, 2)
        copy = remote(
            gss.at[to_x * 2 + core], gsr.at[group], s_gs.at[n], r_gs.at[n], device(y, to_x, z, core)
        )
        copy.start()
        back_copies.append(copy)
    turns = (0, 2, 1, 3)
    for i in turns[1:]:
        crossing(i).wait_recv()
        core_one(i)

    def flatten(src, lane, n):
        for h in range(HEADS):
            flat[n, :, h * TILE : (h + 1) * TILE] = src[h, :, lane : lane + TILE]

    where = {"y": y, "x": x, "z": z}
    levels = ((w0, got1, 256), (w1, got2, 64))
    pending = [None] * 4
    started = []
    last = []

    def along(axis, d):
        at = dict(where)
        at[axis] = turn(where[axis], d)
        return device(at["y"], at["x"], at["z"], c)

    def core_half(m):
        return remote(wg.at[m, 1 - c], got0.at[m], s0.at[0, m], r0.at[0, m], other)

    def send_level(m, level):
        src, got, size = levels[level]
        copies = []
        axis = ORDERS[m][level]
        for d in (1, 2, 3):
            piece = pl.ds(pl.multiple_of(turn(where[axis], d) * size, 16), size)
            copy = remote(
                src.at[m, piece], got.at[m, d - 1], s1.at[level, m, d - 1], r1.at[level, m, d - 1], along(axis, d)
            )
            copy.start()
            copies.append(copy)
        pending[m] = copies
        started.extend(copies)

    def place_rows(m, level):
        start = where[ORDERS[m][0]] * 256
        if level == 1:
            start = start + where[ORDERS[m][1]] * 64
        return pl.ds(pl.multiple_of(start, 16), levels[level][2])

    half = pl.ds(pl.multiple_of(c * 256, 256), 256)

    def give(m, level):
        block = out.at[m, place_rows(m, level), half]
        copies = []
        for d in (1, 2, 3):
            copy = remote(
                block, block, s2.at[level, m, d - 1], r2.at[level, m, d - 1], along(ORDERS[m][level], d)
            )
            copy.start()
            copies.append(copy)
        pending[m] = copies
        started.extend(copies)

    def settled(m):
        for copy in pending[m]:
            copy.wait_recv()

    def begin(m):
        core_half(m).wait_recv()

        def add(i, carry):
            rows = rows_of(i * 256, 256)
            w0[m, rows, :] = (wg[m, c, rows, :].astype(F32) + got0[m, rows, :].astype(F32)).astype(BF)
            return carry

        lax.fori_loop(0, 4, add, 0)
        send_level(m, 0)

    def advance(m, level):
        settled(m)
        if level == 2:
            total = got3[m, 0].astype(F32)
            for n in range(1, 4):
                total = total + got3[m, n].astype(F32)
            out[m, place_rows(m, 1), half] = total.astype(BF)
            give(m, 1)
            return
        src, got, size = levels[level]
        mine = pl.ds(pl.multiple_of(where[ORDERS[m][level]] * size, 16), size)
        total = src[m, mine, :].astype(F32)
        for n in range(3):
            total = total + got[m, n].astype(F32)
        if level == 0:
            w1[m] = total.astype(BF)
            send_level(m, 1)
        else:
            axis = ORDERS[m][2]
            got3[m, where[axis]] = total.astype(BF)
            block = got3.at[m, where[axis]]
            copies = []
            for d in (1, 2, 3):
                copy = remote(block, block, s1.at[2, m, d - 1], r1.at[2, m, d - 1], along(axis, d))
                copy.start()
                copies.append(copy)
            pending[m] = copies
            started.extend(copies)

    def finish(m):
        settled(m)
        copy = remote(out.at[m, :, half], out.at[m, :, half], s0.at[1, m], r0.at[1, m], other)
        copy.start()
        last.append(copy)

    def weight_grad(n, m):
        def part(i, carry):
            cols = rows_of(i * 256, 256)
            got = jnp.dot(tokt[cols, :], flat[n], preferred_element_type=F32).astype(BF)
            wg[m, 0, cols, :] = got[:, :256]
            wg[m, 1, cols, :] = got[:, 256:]
            return carry

        lax.fori_loop(0, 4, part, 0)
        core_half(m).start()

    returned(cg, ret_cg, s_cg, r_cg)
    flatten(ret_cg, 0, 0)
    weight_grad(0, 0)
    flatten(ret_cg, TILE, 3)

    def out_grad(i, carry):
        cols = rows_of(i * 256, 256)
        got = lax.dot_general(flat[3], cot[:, cols], TN, preferred_element_type=F32).astype(BF)
        wg[3, lax.rem(i, 2), rows_of(lax.div(i, 2) * 512, 512), :] = got
        return carry

    lax.fori_loop(0, 4, out_grad, 0)
    core_half(3).start()
    begin(0)

    for copy in back_copies:
        copy.wait()
    coarse = gsr[0].astype(F32)
    for n in range(1, 8):
        coarse = coarse + gsr[n].astype(F32)
    lane = lax.broadcasted_iota(jnp.int32, (1, 256), 1)
    factor = jnp.where(lane < TILE, SCALE, 1.0)
    for i, h in [(i, h) for i in turns for h in (0, 1)]:
        halo_back(i, h).wait_recv()
        for b in (4 * i + 2 * h, 4 * i + 2 * h + 1):
            rows = pl.ds(b * TILE, TILE)
            length = lens[0, group * 16 + b]
            live = lax.broadcasted_iota(jnp.int32, (TILE, 256), 0) < length
            share = coarse[b : b + 1, :] * (1.0 / jnp.full((1, 256), length, jnp.int32).astype(F32))
            extra = jnp.where(c == 0, rx[rows, :].astype(F32), 0.0)
            total = gkv[pl.ds(OWN + b * TILE, TILE), :] + rh[rows, :].astype(F32) + extra
            qg[rows, :] = ((total + jnp.where(live, share, 0.0)) * factor).astype(BF)
        give_half(i, h)

    begin(3)

    def mix(i, carry):
        rows = rows_of(i * 256, 256)
        mixed[rows, :] = jnp.dot(flat[3, rows, :], wo[...], preferred_element_type=F32).astype(BF)
        return carry

    lax.fori_loop(0, 2, mix, 0)
    mixed_written = pltpu.make_async_copy(mixed, mixed_out, s_in.at[0])
    mixed_written.start()
    advance(0, 0)
    advance(0, 1)
    advance(3, 0)
    returned_halves()
    flatten(ret_kv, 0, 1)
    weight_grad(1, 1)
    flatten(ret_kv, TILE, 2)
    weight_grad(2, 2)
    advance(0, 2)
    advance(3, 1)
    begin(1)
    begin(2)

    def back(i, carry):
        rows = rows_of(i * 256, 256)
        total = lax.dot_general(flat[0, rows, :], wq[...], NT, preferred_element_type=F32)
        total = total + lax.dot_general(flat[1, rows, :], wk[...], NT, preferred_element_type=F32)
        total = total + lax.dot_general(flat[2, rows, :], wv[...], NT, preferred_element_type=F32)
        gin[rows, :] = total.astype(BF)
        return carry

    lax.fori_loop(0, 2, back, 0)
    gin_written = pltpu.make_async_copy(gin, gin_out, s_in.at[1])
    gin_written.start()
    advance(3, 2)
    for m in (0, 3):
        settled(m)
        give(m, 0)
    for level in range(3):
        advance(1, level)
        advance(2, level)
    finish(0)
    finish(3)
    for m in (1, 2):
        settled(m)
        give(m, 0)
    for n in range(2):
        last[n].wait()
    written = [pltpu.make_async_copy(out.at[m], total_out.at[m], s_in.at[2 + m]) for m in range(4)]
    written[0].start()
    written[3].start()
    finish(1)
    finish(2)
    for n in (2, 3):
        last[n].wait()
        written[n - 1].start()
    mixed_written.wait()
    gin_written.wait()
    for copy in written:
        copy.wait()
    for m in range(4):
        core_half(m).wait_send()
        crossing(m).wait_send()
        for h in (0, 1):
            halo_back(m, h).wait_send()
    for copy in started:
        copy.wait_send()
    settle(cg, ret_cg, s_cg, r_cg)
    settle_halves()


def hand_over(mixed, gin, total, *refs):
    mixed_out, gin_out, outs = refs[0], refs[1], refs[2:6]
    narrow, wide, s_in, s_out, kept, s_kept, s_pass = refs[6:]
    halves = [pl.ds(0, 512), pl.ds(512, 512)]
    held = [
        pltpu.make_async_copy(src, kept.at[n], s_kept.at[n]) for n, src in enumerate((mixed, gin))
    ]
    passed = [
        pltpu.make_async_copy(kept.at[n], dst, s_pass.at[n])
        for n, dst in enumerate((mixed_out, gin_out))
    ]
    loads = [
        pltpu.make_async_copy(total.at[n // 2, halves[n % 2]], narrow.at[n], s_in.at[n]) for n in range(8)
    ]
    for copy in loads + held:
        copy.start()
    stores = []
    for n in range(8):
        loads[n].wait()
        wide[n] = narrow[n].astype(F32)
        to = outs[3].at[:, halves[n % 2]] if n >= 6 else outs[n // 2].at[halves[n % 2]]
        stores.append(pltpu.make_async_copy(wide.at[n], to, s_out.at[n]))
        stores[n].start()
    for n in range(2):
        held[n].wait()
        passed[n].start()
    for copy in stores + passed:
        copy.wait()


ORDERS = ("yxz", "zyx", "xzy", "xyz")
UNROLL = 4

HB = pl.BlockSpec(memory_space=pl.ANY)
VM = pl.BlockSpec(memory_space=pltpu.VMEM)
SM = pl.BlockSpec(memory_space=pltpu.SMEM)
DMA = pltpu.SemaphoreType.DMA


def shape(*dims, kind=BF):
    return jax.ShapeDtypeStruct(dims, kind)


def local(tokens, lengths, w_query, w_key, w_value, w_out, cotangent):
    vm = pltpu.VMEM
    slabs = lambda n: [vm((2048, 256), BF)] * n
    heads = lambda n: [vm((4, 512, 256), BF)] * n
    mixed, gin, total = pl.pallas_call(
        whole_kernel,
        out_shape=(shape(512, 1024), shape(512, 1024), shape(4, 1024, 512)),
        in_specs=[SM] + [HB] * 6,
        out_specs=(HB, HB, HB),
        scratch_shapes=[vm((512, 1024), BF), vm((512, 1024), BF), vm((4, 1024, 512), BF)]
        + [vm((512, 1024), BF), vm((1024, 512), BF), vm((512, 1024), BF)]
        + [vm((1024, 512), BF)] * 3
        + [vm((512, 1024), BF), vm((6144, 256), BF)]
        + slabs(1)
        + [vm((8, 16, 256), BF)]
        + heads(2)
        + [vm((16, 256), F32)]
        + [
            vm((256, 49 * TILE), BF),
            vm((UNROLL, 256, 10 * TILE), BF),
            vm((UNROLL, 256, 256), BF),
            vm((UNROLL, 256, 256), BF),
            vm((UNROLL, 10 * TILE, 256), F32),
            vm((UNROLL, 10 * TILE, 256), BF),
            vm((6144, 256), F32),
            vm((128, 256), F32),
        ]
        + slabs(3)
        + [vm((8, 16, 256), BF)] * 2
        + heads(2)
        + [
            vm((4, 512, 512), BF),
            vm((4, 2, 1024, 256), BF),
            vm((4, 1024, 256), BF),
            vm((4, 1024, 256), BF),
            vm((4, 3, 256, 256), BF),
            vm((4, 256, 256), BF),
            vm((4, 3, 64, 256), BF),
            vm((4, 4, 64, 256), BF),
        ]
        + [DMA((6,))]
        + [DMA((4,))] * 8
        + [DMA((8,))] * 2
        + [DMA((4, 2))] * 2
        + [DMA((4,))] * 2
        + [DMA((4, 2))] * 2
        + [DMA((4,))] * 2
        + [DMA((8,))] * 2
        + [DMA((2, 4))] * 2
        + [DMA((3, 4, 3))] * 2
        + [DMA((2, 4, 3))] * 2,
        compiler_params=pltpu.CompilerParams(
            collective_id=0, has_side_effects=True, vmem_limit_bytes=62 * MIB
        ),
        name="whole",
    )(lengths, tokens[0], w_key, w_value, w_query, cotangent[0], w_out)
    mixed, gin, *weights = pl.pallas_call(
        hand_over,
        out_shape=(shape(512, 1024), shape(512, 1024))
        + (shape(1024, 512, kind=F32),) * 3
        + (shape(512, 1024, kind=F32),),
        in_specs=[HB] * 3,
        out_specs=(HB,) * 6,
        scratch_shapes=[vm((8, 512, 512), BF), vm((8, 512, 512), F32), DMA((8,)), DMA((8,))]
        + [vm((2, 512, 1024), BF), DMA((2,)), DMA((2,))],
        compiler_params=pltpu.CompilerParams(vmem_limit_bytes=62 * MIB),
        name="hand_over",
    )(mixed, gin, total)
    return (mixed[None], gin[None], *weights)


def solution(mesh):
    placed = (P("dp", "seq", None), P("dp", None), P(), P(), P(), P(), P("dp", "seq", None))
    return jax.shard_map(
        local,
        mesh=mesh,
        in_specs=placed,
        out_specs=(P("dp", "seq", None), P("dp", "seq", None), P(), P(), P(), P()),
        check_vma=False,
    )
```

```python
import functools
import math

import jax
import jax.numpy as jnp
from jax import lax
from jax.experimental import pallas as pl
from jax.experimental.pallas import tpu as pltpu
from jax.sharding import PartitionSpec as P

MESH = pl.DeviceIdType.MESH
BF = jnp.bfloat16
F32 = jnp.float32
HEADS = 4
TILE = 128
OFFSETS = (0, 1, 2, 4, 8, 12, 16, 24, 32)
SCALE = 1.0 / math.sqrt(128.0)
LOG2E = 1.4426950408889634
NEG = -1e30
NT = (((1,), (1,)), ((), ()))
TN = (((0,), (0,)), ((), ()))
OWN = 32 * TILE
MIB = 1024 * 1024


def place():
    s = lax.axis_index("seq")
    return lax.axis_index("dp"), lax.div(s, 8), lax.rem(lax.div(s, 2), 4), lax.rem(s, 2)


def device(y, x, z, c):
    return (y, (x * 4 + z) * 2 + c)


def turn(a, d):
    return lax.rem(a + d, 4)


def remote(src, dst, send, recv, to):
    return pltpu.make_async_remote_copy(
        src_ref=src, dst_ref=dst, send_sem=send, recv_sem=recv, device_id=to, device_id_type=MESH
    )


def all_partners(y, x, z, c):
    found = [device(y, x, z, 1 - c)]
    for d in (1, 2, 3):
        found.append(device(turn(y, d), x, z, c))
        for core in (0, 1):
            found.append(device(y, turn(x, d), z, core))
            found.append(device(y, x, turn(z, d), core))
    return found


def rows_of(start, count):
    return pl.ds(pl.multiple_of(start, TILE), count)


def whole_kernel(
    lens, tok_in, wk_in, wv_in, wq_in, cot_in, wo_in, mixed_out, gin_out, total_out,
    mixed, gin, out,
    tok, tokt, cot, wq, wk, wv, wo,
    kv, qg, summ, kvs, qgs, sums,
    kvt, gt, pair, pairt, sc, dsp, gkv, gsum, cg,
    rx, rh, gss, gsr, ret_kv, ret_cg, flat,
    wg, got0, w0, got1, w1, got2, got3,
    s_in, s_kv, r_kv, s_qg, r_qg, s_h, r_h, s_x, r_x, s_s, r_s,
    s_bkv, r_bkv, s_cg, r_cg, s_bh, r_bh, s_bx, r_bx, s_gs, r_gs,
    s0, r0, s1, r1, s2, r2, s3, r3,
):
    y, x, z, c = place()
    loads = []
    for n, (a, b) in enumerate(
        ((tok_in, tok), (wk_in, wk), (wv_in, wv), (wq_in, wq), (cot_in, cot), (wo_in, wo))
    ):
        copy = pltpu.make_async_copy(a, b, s_in.at[n])
        copy.start()
        loads.append(copy)
    partners = all_partners(y, x, z, c)
    barrier = pltpu.get_barrier_semaphore()
    for to in partners:
        pl.semaphore_signal(barrier, inc=1, device_id=to, device_id_type=MESH)
    other = device(y, x, z, 1 - c)
    home = lax.div(z, 2)
    at_home = c == home
    slot = lax.rem(z, 2) * 2 + c
    group = 2 * x + c

    def project(src, w, dst, lane):
        def half(i, carry):
            rows = rows_of(i * 256, 256)
            got = jnp.dot(src[rows, :], w[...], preferred_element_type=F32)
            for h in range(HEADS):
                dst[h, rows, lane : lane + TILE] = got[:, h * TILE : (h + 1) * TILE].astype(BF)
            return carry

        lax.fori_loop(0, 2, half, 0)

    def exchange(staged, landing, base, send, recv):
        spot = rows_of(base + slot * 512, 512)
        copies = []
        near = remote(staged.at[z], landing.at[spot], send.at[0], recv.at[slot], other)

        @pl.when(at_home)
        def _():
            landing[spot, :] = staged[z]

        @pl.when(jnp.logical_not(at_home))
        def _():
            near.start()

        for d in (1, 3, 2):
            h = turn(z, d)
            copy = remote(staged.at[h], landing.at[spot], send.at[d], recv.at[slot], device(y, x, h, home))
            if d != 2:
                copy.start()
            copies.append(copy)
        return copies, near

    def settle_out(copies, near):
        for copy in copies:
            copy.wait_send()

        @pl.when(jnp.logical_not(at_home))
        def _():
            near.wait_send()

    def arrived(staged, landing, base, send, recv, i):
        mine = jnp.logical_and(z == 2 * c + lax.div(i, 2), c == lax.rem(i, 2))

        @pl.when(jnp.logical_not(mine))
        def _():
            remote(
                staged.at[0], landing.at[rows_of(base + i * 512, 512)], send.at[0], recv.at[i], other
            ).wait_recv()

    for n in range(3):
        loads[n].wait()
    project(tok, wk, kvs, 0)
    project(tok, wv, kvs, TILE)
    pl.semaphore_wait(barrier, len(partners))
    kv_sent = exchange(kvs, kv, OWN, s_kv, r_kv)
    for n in range(3, 6):
        loads[n].wait()
    project(tok, wq, qgs, 0)
    first_own = ((x * 4 + z) * 2 + c) * 4

    def grads(i, carry):
        rows = rows_of(i * TILE, TILE)
        got = lax.dot_general(cot[rows, :], wo[...], NT, preferred_element_type=F32)
        live = lax.broadcasted_iota(jnp.int32, (TILE, 512), 0) < lens[0, first_own + i]
        got = jnp.where(live, got, 0.0).astype(BF)
        for h in range(HEADS):
            qgs[h, rows, TILE : 2 * TILE] = got[:, h * TILE : (h + 1) * TILE]
        return carry

    lax.fori_loop(0, 4, grads, 0)
    kv_sent[0][2].start()

    ahead = device(y, turn(x, 1), z, c)
    behind = device(y, turn(x, 3), z, c)

    def halo_copy(i):
        return remote(
            kv.at[rows_of(OWN + i * 512, 512)], kv.at[rows_of(i * 512, 512)], s_h.at[i], r_h.at[i], ahead
        )

    def across_copy(start, i):
        return remote(
            kv.at[rows_of(start + i * 512, 512)],
            kv.at[rows_of(2048 + i * 512, 512)],
            s_x.at[i],
            r_x.at[i],
            other,
        )

    nearest = lax.rem(z + jnp.where(at_home, 0, 1), 2) * 2
    order = [lax.rem(nearest + k, 4) for k in range(4)]
    for i in order:
        arrived(kvs, kv, OWN, s_kv, r_kv, i)
        halo_copy(i).start()

        @pl.when(c == 0)
        def _():
            across_copy(OWN, i).start()

    qg_sent = exchange(qgs, qg, 0, s_qg, r_qg)
    qg_sent[0][2].start()

    def summary(i, carry):
        rows = rows_of(OWN + i * TILE, TILE)
        length = lens[0, group * 16 + i]
        live = lax.broadcasted_iota(jnp.int32, (TILE, 256), 0) < length
        total = jnp.sum(jnp.where(live, kv[rows, :].astype(F32), 0.0), axis=0, keepdims=True)
        sums[pl.ds(i, 1), :] = total / jnp.full((1, 256), length, jnp.int32).astype(F32)
        return carry

    lax.fori_loop(0, 16, summary, 0)
    summ[group] = sums[...].astype(BF)
    sum_copies = []
    pairs_of = [(d, cc) for d in range(4) for cc in (0, 1) if (d, cc) != (0, 0)]
    for d, cc in pairs_of:
        n = d * 2 + cc
        core = lax.rem(c + cc, 2)
        copy = remote(summ.at[group], summ.at[group], s_s.at[n], r_s.at[n], device(y, turn(x, d), z, core))
        copy.start()
        sum_copies.append(copy)

    def prepare(b, carry):
        rows = rows_of(b * TILE, TILE)
        kvt[:, rows] = jnp.transpose(kv[rows, :])
        return carry

    def clear(b, carry):
        gkv[rows_of(b * TILE, TILE), :] = jnp.zeros((TILE, 256), F32)
        return carry

    lax.fori_loop(0, 48, clear, 0)
    gsum[...] = jnp.zeros_like(gsum)
    for u in range(UNROLL):
        pair[u] = jnp.zeros((256, 256), BF)
        pairt[u] = jnp.zeros((256, 256), BF)
    lax.fori_loop(32, 48, prepare, 0)

    def turned(i, carry):
        cols = rows_of(i * TILE, TILE)
        tokt[cols, :] = jnp.transpose(tok[:, cols])
        return carry

    lax.fori_loop(0, 8, turned, 0)
    for i in order:
        halo_copy(i).wait_recv()

        @pl.when(c == 1)
        def _():
            across_copy(0, i).start()

        lax.fori_loop(i * 4, i * 4 + 4, prepare, 0)

    for i in range(4):
        arrived(qgs, qg, 0, s_qg, r_qg, i)
    for i in order:
        across_copy(0, i).wait_recv()
        lax.fori_loop(16 + i * 4, 20 + i * 4, prepare, 0)
    for i in range(4):
        across_copy(0, i).wait_send()
        halo_copy(i).wait_send()
    for copy in sum_copies:
        copy.wait()
    kvt[:, 48 * TILE : 49 * TILE] = jnp.transpose(summ[...].reshape(TILE, 256))
    settle_out(*kv_sent)
    settle_out(*qg_sent)

    key_slot = lax.broadcasted_iota(jnp.int32, (TILE, TILE), 0)
    query_slot = lax.broadcasted_iota(jnp.int32, (TILE, TILE), 1)
    count = len(OFFSETS)

    def bar(it, carry):
        ids = [it * UNROLL + u for u in range(UNROLL)]
        tops, scales, deltas = [], [], []
        for u, qb in enumerate(ids):
            rows = rows_of(qb * TILE, TILE)
            pair[u, 0:TILE, 0:TILE] = qg[rows, 0:TILE]
            pair[u, TILE:, TILE:] = qg[rows, TILE:]
            pairt[u, 0:TILE, 0:TILE] = jnp.transpose(qg[rows, 0:TILE])
            pairt[u, TILE:, TILE:] = jnp.transpose(qg[rows, TILE:])
            both = pairt[u]
            this = 16 * group + qb
            top = None
            for j in range(count + 1):
                here = slice(j * TILE, (j + 1) * TILE)
                if j < count:
                    spot = rows_of((32 + qb - OFFSETS[j]) * TILE, TILE)
                    bar_id = this - OFFSETS[j]
                    length = jnp.where(bar_id >= 0, lens[0, jnp.maximum(bar_id, 0)], 0)
                    source = kv[spot, :]
                    gt[u, :, here] = kvt[:, spot]
                    ok = key_slot < length
                    if j == 0:
                        ok = jnp.logical_and(ok, key_slot <= query_slot)
                else:
                    source = summ[...].reshape(TILE, 256)
                    gt[u, :, here] = kvt[:, 48 * TILE : 49 * TILE]
                    distance = this - key_slot
                    ok = distance >= 1
                    for o in OFFSETS[1:]:
                        ok = jnp.logical_and(ok, distance != o)
                got = jnp.dot(source, both, preferred_element_type=F32)
                score = jnp.where(ok, got[:, :TILE] * (SCALE * LOG2E), NEG)
                sc[u, here, :TILE] = score
                sc[u, here, TILE:] = got[:, TILE:]
                high = jnp.max(score, axis=0, keepdims=True)
                top = high if top is None else jnp.maximum(top, high)
            tops.append(top)
        for u in range(UNROLL):
            total = jnp.zeros((1, TILE), F32)
            weighted = jnp.zeros((1, TILE), F32)
            for j in range(count + 1):
                here = slice(j * TILE, (j + 1) * TILE)
                e = jnp.exp2(sc[u, here, :TILE] - tops[u])
                total = total + jnp.sum(e, axis=0, keepdims=True)
                weighted = weighted + jnp.sum(e * sc[u, here, TILE:], axis=0, keepdims=True)
            scales.append(tops[u] + jnp.log(total) * LOG2E)
            deltas.append(weighted / total)
        for u, qb in enumerate(ids):
            rows = rows_of(qb * TILE, TILE)
            both = pair[u]
            for j in range(count + 1):
                here = slice(j * TILE, (j + 1) * TILE)
                p = jnp.exp2(sc[u, here, :TILE] - scales[u])
                ds = (p * (sc[u, here, TILE:] - deltas[u])).astype(BF)
                block = jnp.concatenate([ds, p.astype(BF)], axis=1)
                dsp[u, here, :] = block
                got = jnp.dot(block, both, preferred_element_type=F32)
                if j < count:
                    spot = rows_of((32 + qb - OFFSETS[j]) * TILE, TILE)
                    gkv[spot, :] += got
                else:
                    gsum[...] += got
            both_out = jnp.dot(gt[u], dsp[u], preferred_element_type=F32)
            cg[rows, 0:TILE] = jnp.transpose(both_out[:TILE, :TILE] * SCALE).astype(BF)
            context = jnp.transpose(both_out[TILE:, TILE:])
            cg[rows, TILE:] = jnp.where(key_slot < lens[0, 16 * group + qb], context, 0.0).astype(BF)
        return carry

    def owner(i):
        to_z = 2 * c + lax.div(i, 2)
        core = lax.rem(i, 2)
        mine = jnp.logical_and(z == to_z, c == core)
        return device(y, x, to_z, core), mine

    def give_back(src, landing, send, recv, i):
        to, mine = owner(i)
        rows = rows_of(i * 512, 512)

        @pl.when(mine)
        def _():
            landing[z] = src[rows, :]

        @pl.when(jnp.logical_not(mine))
        def _():
            remote(src.at[rows], landing.at[z], send.at[i], recv.at[z], to).start()

    def settle(src, landing, send, recv):
        for i in range(4):
            to, mine = owner(i)

            @pl.when(jnp.logical_not(mine))
            def _():
                remote(src.at[pl.ds(i * 512, 512)], landing.at[z], send.at[i], recv.at[z], to).wait_send()

    def returned(src, landing, send, recv):
        for h in range(HEADS):
            mine = jnp.logical_and(z == h, at_home)

            @pl.when(jnp.logical_not(mine))
            def _():
                remote(src.at[pl.ds(0, 512)], landing.at[h], send.at[0], recv.at[h], other).wait_recv()

    def half_copy(i, h, to):
        part = pl.ds(h * 256, 256)
        return remote(
            qg.at[pl.ds(i * 512 + h * 256, 256)], ret_kv.at[z, part], s_bkv.at[i, h], r_bkv.at[z, h], to
        )

    def give_half(i, h):
        to, mine = owner(i)

        @pl.when(mine)
        def _():
            ret_kv[z, h * 256 : h * 256 + 256] = qg[i * 512 + h * 256 : i * 512 + h * 256 + 256, :]

        @pl.when(jnp.logical_not(mine))
        def _():
            half_copy(i, h, to).start()

    def settle_halves():
        for i in range(4):
            to, mine = owner(i)

            @pl.when(jnp.logical_not(mine))
            def _():
                for h in (0, 1):
                    half_copy(i, h, to).wait_send()

    def returned_halves():
        part = [pl.ds(0, 256), pl.ds(256, 256)]
        for n in range(HEADS):
            mine = jnp.logical_and(z == n, at_home)

            @pl.when(jnp.logical_not(mine))
            def _():
                for h in (0, 1):
                    remote(
                        qg.at[part[0]], ret_kv.at[n, part[h]], s_bkv.at[0, h], r_bkv.at[n, h], other
                    ).wait_recv()

    def crossing(i):
        rows = rows_of(i * 512, 512)
        return remote(kvs.at[i], rx.at[rows], s_bx.at[i], r_bx.at[i], other)

    def cross(i):
        kvs[i] = gkv[rows_of(2048 + i * 512, 512), :].astype(BF)
        crossing(i).start()

    def halo_back(i, h):
        part = pl.ds(h * 256, 256)
        rows = rows_of(i * 512 + h * 256, 256)
        return remote(qgs.at[i, part], rh.at[rows], s_bh.at[i, h], r_bh.at[i, h], behind)

    def core_one(i):
        @pl.when(c == 1)
        def _():
            rows = pl.ds(i * 512, 512)
            qgs[i] = (gkv[rows, :] + rx[rows, :].astype(F32)).astype(BF)
            for h in (0, 1):
                halo_back(i, h).start()

    def chunk(step, carry):
        i = jnp.where(step == 1, 2, jnp.where(step == 2, 1, step))
        lax.fori_loop(0, 4 // UNROLL, lambda u, kept: bar(i * (4 // UNROLL) + u, kept), 0)

        @pl.when(c == 0)
        def _():
            rows = rows_of(i * 512, 512)
            qgs[i] = gkv[rows, :].astype(BF)
            for h in (0, 1):
                halo_back(i, h).start()

        @pl.when(step == 1)
        def _():
            cross(0)

        @pl.when(step == 2)
        def _():
            cross(2)
            crossing(0).wait_recv()
            core_one(0)

        give_back(cg, ret_cg, s_cg, r_cg, i)
        return carry

    lax.fori_loop(0, 4, chunk, 0)
    cross(1)
    cross(3)
    gss[...] = gsum[...].astype(BF).reshape(8, 16, 256)
    gsr[group] = gss[group]
    back_copies = []
    for d, cc in pairs_of:
        n = d * 2 + cc
        to_x, core = turn(x, d), lax.rem(c + cc, 2)
        copy = remote(
            gss.at[to_x * 2 + core], gsr.at[group], s_gs.at[n], r_gs.at[n], device(y, to_x, z, core)
        )
        copy.start()
        back_copies.append(copy)
    turns = (0, 2, 1, 3)
    for i in turns[1:]:
        crossing(i).wait_recv()
        core_one(i)

    def flatten(src, lane, n):
        for h in range(HEADS):
            flat[n, :, h * TILE : (h + 1) * TILE] = src[h, :, lane : lane + TILE]

    where = {"y": y, "x": x, "z": z}
    levels = ((w0, got1, 256), (w1, got2, 64))
    pending = [None] * 4
    started = []
    last = [[], [], [], []]

    def along(axis, d):
        at = dict(where)
        at[axis] = turn(where[axis], d)
        return device(at["y"], at["x"], at["z"], c)

    def core_half(m):
        return remote(wg.at[m, 1 - c], got0.at[m], s0.at[0, m], r0.at[0, m], other)

    def send_level(m, level):
        src, got, size = levels[level]
        copies = []
        axis = ORDERS[m][level]
        for d in (1, 2, 3):
            piece = pl.ds(pl.multiple_of(turn(where[axis], d) * size, 16), size)
            copy = remote(
                src.at[m, piece], got.at[m, d - 1], s1.at[level, m, d - 1], r1.at[level, m, d - 1], along(axis, d)
            )
            copy.start()
            copies.append(copy)
        pending[m] = copies
        started.extend(copies)

    def place_rows(m, level):
        start = where[ORDERS[m][0]] * 256
        if level == 1:
            start = start + where[ORDERS[m][1]] * 64
        return pl.ds(pl.multiple_of(start, 16), levels[level][2])

    half = pl.ds(pl.multiple_of(c * 256, 256), 256)

    def give(m, level):
        block = out.at[m, place_rows(m, level), half]
        copies = []
        for d in (1, 2, 3):
            copy = remote(
                block, block, s2.at[level, m, d - 1], r2.at[level, m, d - 1], along(ORDERS[m][level], d)
            )
            copy.start()
            copies.append(copy)
        if level == 0:
            hand_on(m, 0)
        pending[m] = copies
        started.extend(copies)

    def settled(m):
        for copy in pending[m]:
            copy.wait_recv()

    def begin(m):
        core_half(m).wait_recv()

        def add(i, carry):
            rows = rows_of(i * 256, 256)
            w0[m, rows, :] = (wg[m, c, rows, :].astype(F32) + got0[m, rows, :].astype(F32)).astype(BF)
            return carry

        lax.fori_loop(0, 4, add, 0)
        send_level(m, 0)

    def advance(m, level):
        settled(m)
        if level == 2:
            total = got3[m, 0].astype(F32)
            for n in range(1, 4):
                total = total + got3[m, n].astype(F32)
            out[m, place_rows(m, 1), half] = total.astype(BF)
            give(m, 1)
            return
        src, got, size = levels[level]
        mine = pl.ds(pl.multiple_of(where[ORDERS[m][level]] * size, 16), size)
        total = src[m, mine, :].astype(F32)
        for n in range(3):
            total = total + got[m, n].astype(F32)
        if level == 0:
            w1[m] = total.astype(BF)
            send_level(m, 1)
        else:
            axis = ORDERS[m][2]
            got3[m, where[axis]] = total.astype(BF)
            block = got3.at[m, where[axis]]
            copies = []
            for d in (1, 2, 3):
                copy = remote(block, block, s1.at[2, m, d - 1], r1.at[2, m, d - 1], along(axis, d))
                copy.start()
                copies.append(copy)
            pending[m] = copies
            started.extend(copies)

    def hand_on(m, d):
        rows = pl.ds(pl.multiple_of(turn(where[ORDERS[m][0]], 4 - d) * 256, 16), 256)
        block = out.at[m, rows, half]
        copy = remote(block, block, s3.at[m, d], r3.at[m, d], other)
        copy.start()
        last[m].append(copy)

    def finish(m):
        for d in (1, 2, 3):
            pending[m][d - 1].wait_recv()
            hand_on(m, d)

    def weight_grad(n, m):
        def part(i, carry):
            cols = rows_of(i * 256, 256)
            got = jnp.dot(tokt[cols, :], flat[n], preferred_element_type=F32).astype(BF)
            wg[m, 0, cols, :] = got[:, :256]
            wg[m, 1, cols, :] = got[:, 256:]
            return carry

        lax.fori_loop(0, 4, part, 0)
        core_half(m).start()

    returned(cg, ret_cg, s_cg, r_cg)
    flatten(ret_cg, 0, 0)
    weight_grad(0, 0)
    flatten(ret_cg, TILE, 3)

    def out_grad(i, carry):
        cols = rows_of(i * 256, 256)
        got = lax.dot_general(flat[3], cot[:, cols], TN, preferred_element_type=F32).astype(BF)
        wg[3, lax.rem(i, 2), rows_of(lax.div(i, 2) * 512, 512), :] = got
        return carry

    lax.fori_loop(0, 4, out_grad, 0)
    core_half(3).start()
    begin(0)

    for copy in back_copies:
        copy.wait()
    coarse = gsr[0].astype(F32)
    for n in range(1, 8):
        coarse = coarse + gsr[n].astype(F32)
    lane = lax.broadcasted_iota(jnp.int32, (1, 256), 1)
    factor = jnp.where(lane < TILE, SCALE, 1.0)
    for i, h in [(i, h) for i in turns for h in (0, 1)]:
        halo_back(i, h).wait_recv()
        for b in (4 * i + 2 * h, 4 * i + 2 * h + 1):
            rows = pl.ds(b * TILE, TILE)
            length = lens[0, group * 16 + b]
            live = lax.broadcasted_iota(jnp.int32, (TILE, 256), 0) < length
            share = coarse[b : b + 1, :] * (1.0 / jnp.full((1, 256), length, jnp.int32).astype(F32))
            extra = jnp.where(c == 0, rx[rows, :].astype(F32), 0.0)
            total = gkv[pl.ds(OWN + b * TILE, TILE), :] + rh[rows, :].astype(F32) + extra
            qg[rows, :] = ((total + jnp.where(live, share, 0.0)) * factor).astype(BF)
        give_half(i, h)

    begin(3)

    def mix(i, carry):
        rows = rows_of(i * 256, 256)
        mixed[rows, :] = jnp.dot(flat[3, rows, :], wo[...], preferred_element_type=F32).astype(BF)
        return carry

    lax.fori_loop(0, 2, mix, 0)
    mixed_written = pltpu.make_async_copy(mixed, mixed_out, s_in.at[0])
    mixed_written.start()
    advance(0, 0)
    advance(0, 1)
    advance(3, 0)
    returned_halves()
    flatten(ret_kv, 0, 1)
    weight_grad(1, 1)
    flatten(ret_kv, TILE, 2)
    weight_grad(2, 2)
    advance(0, 2)
    advance(3, 1)
    begin(1)
    begin(2)

    def back(i, carry):
        rows = rows_of(i * 256, 256)
        total = lax.dot_general(flat[0, rows, :], wq[...], NT, preferred_element_type=F32)
        total = total + lax.dot_general(flat[1, rows, :], wk[...], NT, preferred_element_type=F32)
        total = total + lax.dot_general(flat[2, rows, :], wv[...], NT, preferred_element_type=F32)
        gin[rows, :] = total.astype(BF)
        return carry

    lax.fori_loop(0, 2, back, 0)
    gin_written = pltpu.make_async_copy(gin, gin_out, s_in.at[1])
    gin_written.start()
    advance(3, 2)
    for m in (0, 3):
        settled(m)
        give(m, 0)
    for level in range(3):
        advance(1, level)
        advance(2, level)
    finish(0)
    finish(3)
    for m in (1, 2):
        settled(m)
        give(m, 0)
    for copy in last[0] + last[3]:
        copy.wait()
    written = [pltpu.make_async_copy(out.at[m], total_out.at[m], s_in.at[2 + m]) for m in range(4)]
    written[0].start()
    written[3].start()
    finish(1)
    finish(2)
    for m in (1, 2):
        for copy in last[m]:
            copy.wait()
        written[m].start()
    mixed_written.wait()
    gin_written.wait()
    for copy in written:
        copy.wait()
    for m in range(4):
        core_half(m).wait_send()
        crossing(m).wait_send()
        for h in (0, 1):
            halo_back(m, h).wait_send()
    for copy in started:
        copy.wait_send()
    settle(cg, ret_cg, s_cg, r_cg)
    settle_halves()


def hand_over(mixed, gin, total, *refs):
    mixed_out, gin_out, outs = refs[0], refs[1], refs[2:6]
    narrow, wide, s_in, s_out, kept, s_kept, s_pass = refs[6:]
    halves = [pl.ds(0, 512), pl.ds(512, 512)]
    held = [
        pltpu.make_async_copy(src, kept.at[n], s_kept.at[n]) for n, src in enumerate((mixed, gin))
    ]
    passed = [
        pltpu.make_async_copy(kept.at[n], dst, s_pass.at[n])
        for n, dst in enumerate((mixed_out, gin_out))
    ]
    loads = [
        pltpu.make_async_copy(total.at[n // 2, halves[n % 2]], narrow.at[n], s_in.at[n]) for n in range(8)
    ]
    for copy in loads + held:
        copy.start()
    stores = []
    for n in range(8):
        loads[n].wait()
        wide[n] = narrow[n].astype(F32)
        to = outs[3].at[:, halves[n % 2]] if n >= 6 else outs[n // 2].at[halves[n % 2]]
        stores.append(pltpu.make_async_copy(wide.at[n], to, s_out.at[n]))
        stores[n].start()
    for n in range(2):
        held[n].wait()
        passed[n].start()
    for copy in stores + passed:
        copy.wait()


ORDERS = ("yxz", "zyx", "xzy", "xyz")
UNROLL = 4

HB = pl.BlockSpec(memory_space=pl.ANY)
VM = pl.BlockSpec(memory_space=pltpu.VMEM)
SM = pl.BlockSpec(memory_space=pltpu.SMEM)
DMA = pltpu.SemaphoreType.DMA


def shape(*dims, kind=BF):
    return jax.ShapeDtypeStruct(dims, kind)


def local(tokens, lengths, w_query, w_key, w_value, w_out, cotangent):
    vm = pltpu.VMEM
    slabs = lambda n: [vm((2048, 256), BF)] * n
    heads = lambda n: [vm((4, 512, 256), BF)] * n
    mixed, gin, total = pl.pallas_call(
        whole_kernel,
        out_shape=(shape(512, 1024), shape(512, 1024), shape(4, 1024, 512)),
        in_specs=[SM] + [HB] * 6,
        out_specs=(HB, HB, HB),
        scratch_shapes=[vm((512, 1024), BF), vm((512, 1024), BF), vm((4, 1024, 512), BF)]
        + [vm((512, 1024), BF), vm((1024, 512), BF), vm((512, 1024), BF)]
        + [vm((1024, 512), BF)] * 3
        + [vm((512, 1024), BF), vm((6144, 256), BF)]
        + slabs(1)
        + [vm((8, 16, 256), BF)]
        + heads(2)
        + [vm((16, 256), F32)]
        + [
            vm((256, 49 * TILE), BF),
            vm((UNROLL, 256, 10 * TILE), BF),
            vm((UNROLL, 256, 256), BF),
            vm((UNROLL, 256, 256), BF),
            vm((UNROLL, 10 * TILE, 256), F32),
            vm((UNROLL, 10 * TILE, 256), BF),
            vm((6144, 256), F32),
            vm((128, 256), F32),
        ]
        + slabs(3)
        + [vm((8, 16, 256), BF)] * 2
        + heads(2)
        + [
            vm((4, 512, 512), BF),
            vm((4, 2, 1024, 256), BF),
            vm((4, 1024, 256), BF),
            vm((4, 1024, 256), BF),
            vm((4, 3, 256, 256), BF),
            vm((4, 256, 256), BF),
            vm((4, 3, 64, 256), BF),
            vm((4, 4, 64, 256), BF),
        ]
        + [DMA((6,))]
        + [DMA((4,))] * 8
        + [DMA((8,))] * 2
        + [DMA((4, 2))] * 2
        + [DMA((4,))] * 2
        + [DMA((4, 2))] * 2
        + [DMA((4,))] * 2
        + [DMA((8,))] * 2
        + [DMA((2, 4))] * 2
        + [DMA((3, 4, 3))] * 2
        + [DMA((2, 4, 3))] * 2
        + [DMA((4, 4))] * 2,
        compiler_params=pltpu.CompilerParams(
            collective_id=0, has_side_effects=True, vmem_limit_bytes=62 * MIB
        ),
        name="whole",
    )(lengths, tokens[0], w_key, w_value, w_query, cotangent[0], w_out)
    mixed, gin, *weights = pl.pallas_call(
        hand_over,
        out_shape=(shape(512, 1024), shape(512, 1024))
        + (shape(1024, 512, kind=F32),) * 3
        + (shape(512, 1024, kind=F32),),
        in_specs=[HB] * 3,
        out_specs=(HB,) * 6,
        scratch_shapes=[vm((8, 512, 512), BF), vm((8, 512, 512), F32), DMA((8,)), DMA((8,))]
        + [vm((2, 512, 1024), BF), DMA((2,)), DMA((2,))],
        compiler_params=pltpu.CompilerParams(vmem_limit_bytes=62 * MIB),
        name="hand_over",
    )(mixed, gin, total)
    return (mixed[None], gin[None], *weights)


def solution(mesh):
    placed = (P("dp", "seq", None), P("dp", None), P(), P(), P(), P(), P("dp", "seq", None))
    return jax.shard_map(
        local,
        mesh=mesh,
        in_specs=placed,
        out_specs=(P("dp", "seq", None), P("dp", "seq", None), P(), P(), P(), P()),
        check_vma=False,
    )
```
